32 devices in a mesh: seq: 8 (over y, x, core), fsdp: 4 (over z).
Axes of the slice: x: 2, y: 2, z: 4, core: 2. Of those that a mesh axis runs over, the one named last changes fastest.
Arguments:
- tokens: bfloat16 [4, 2048, 1152], P('fsdp', 'seq'), may hold values from -6 to 6
- cotangent: bfloat16 [4, 2048, 1152], P('fsdp', 'seq'), may hold values from -6 to 6
- doc_lengths: int32 [4, 3], P('fsdp'), may hold values from 682 to 684, as said below
- true_counts: int32 [4, 3], P('fsdp'), may hold values from 512 to 684, as said below
- w_query: bfloat16 [1152, 1024], P(('seq', 'fsdp')), may hold values from -0.1875 to 0.1875
- w_key: bfloat16 [1152, 256], P(('seq', 'fsdp')), may hold values from -0.1875 to 0.1875
- w_value: bfloat16 [1152, 256], P(('seq', 'fsdp')), may hold values from -0.1875 to 0.1875
- w_out: bfloat16 [1152, 1024], P(('seq', 'fsdp')), may hold values from -0.1875 to 0.1875
- w_gate: bfloat16 [1152, 6912], P('seq', 'fsdp'), may hold values from -0.1875 to 0.1875
- w_up: bfloat16 [1152, 6912], P('seq', 'fsdp'), may hold values from -0.1875 to 0.1875
- w_down: bfloat16 [1152, 6912], P('seq', 'fsdp'), may hold values from -0.078125 to 0.078125
- attn_norm_gain: bfloat16 [1152], P(('seq', 'fsdp')), may hold values from 0.5 to 1.5
- query_gain: bfloat16 [256], P(('seq', 'fsdp')), may hold values from 0.5 to 1.5
- key_gain: bfloat16 [256], P(('seq', 'fsdp')), may hold values from 0.5 to 1.5
- attn_post_gain: bfloat16 [1152], P(('seq', 'fsdp')), may hold values from 0.5 to 1.5
- ffn_norm_gain: bfloat16 [1152], P(('seq', 'fsdp')), may hold values from 0.5 to 1.5
- ffn_post_gain: bfloat16 [1152], P(('seq', 'fsdp')), may hold values from 0.5 to 1.5
Outputs:
- output: bfloat16 [4, 2048, 1152], P('fsdp', 'seq')
- input_grad: float32 [4, 2048, 1152], P('fsdp', 'seq')
- grad_query: float32 [1152, 1024], P(('seq', 'fsdp'))
- grad_key: float32 [1152, 256], P(('seq', 'fsdp'))
- grad_value: float32 [1152, 256], P(('seq', 'fsdp'))
- grad_out: float32 [1152, 1024], P(('seq', 'fsdp'))
- grad_gate: float32 [1152, 6912], P('seq', 'fsdp')
- grad_up: float32 [1152, 6912], P('seq', 'fsdp')
- grad_down: float32 [1152, 6912], P('seq', 'fsdp')
- grad_attn_norm: float32 [1152], P(('seq', 'fsdp'))
- grad_query_gain: float32 [256], P(('seq', 'fsdp'))
- grad_key_gain: float32 [256], P(('seq', 'fsdp'))
- grad_attn_post: float32 [1152], P(('seq', 'fsdp'))
- grad_ffn_norm: float32 [1152], P(('seq', 'fsdp'))
- grad_ffn_post: float32 [1152], P(('seq', 'fsdp'))
The draws below stay inside these ranges and needn't reach their ends.
Inputs may be any that keep to these rules, and one draw needn't show every extreme that they name: `doc_lengths`: row g gives the slot lengths of the 3 documents of group g, laid end to end in order; each row sums to 2048. In each group one document has the least length and one has the greatest. true_counts[g, k] is the number of real tokens of document k of group g; its first doc_lengths[g, k] - true_counts[g, k] slots are padding, at most min(doc_lengths[g, k] // 4, 256) of them.
All inputs are finite; a program needn't handle non-finite values.
Results may differ from the reference program's by a relative error of at most 0.02.
Values may be sent and summed in bfloat16 or wider, within the bound.
No kernel may reach another device: no remote copies, remote signals or barrier semaphores. Data moves between devices by JAX's collectives and lax.ppermute only.
A program may use at most 128 MiB of HBM per device.

```python
import jax
import jax.numpy as jnp
from jax import lax

D = 1152
HEADS = 4
HD = 256
FF = 6912
WINDOW = 512
DOCS = 3
MIN_LEN = 1024
SLOTS = 2048
GROUPS = 4


def document_layout(key):
    floor_len = min(MIN_LEN, SLOTS // DOCS)
    spare_slots = SLOTS - DOCS * floor_len

    def one_group(group_key):
        sub_keys = jax.random.split(group_key, 4)
        short_doc = jax.random.randint(sub_keys[0], (), 0, DOCS)
        long_doc = (short_doc + 1 + jax.random.randint(sub_keys[1], (), 0, DOCS - 1)) % DOCS
        doc_order = jnp.arange(DOCS)
        lengths = floor_len + jnp.where(doc_order == long_doc, spare_slots, 0)
        pad_limit = jnp.minimum(lengths // 4, WINDOW // 2)
        padding = jax.random.randint(sub_keys[3], (DOCS,), 0, pad_limit + 1)
        padding = jnp.where(doc_order == short_doc, pad_limit, padding)
        padding = jnp.where(doc_order == long_doc, 0, padding)
        return (lengths.astype(jnp.int32), (lengths - padding).astype(jnp.int32))
    group_keys = jax.random.split(key, GROUPS)
    return jax.vmap(one_group)(group_keys)


def draw_doc_lengths(key, part):
    return document_layout(key)[0]


def draw_true_counts(key, part):
    return document_layout(key)[1]


def levels(own_key, shape, pieces, low, largest):
    gain, own = 1.0, jax.random.fold_in(own_key, 6)
    for dim, parts in pieces:
        steps = jnp.exp(jax.random.uniform(jax.random.fold_in(own, dim), (parts,), jnp.float32, low / len(pieces), largest / len(pieces)))
        gain = gain * jnp.repeat(steps, shape[dim] // parts).reshape([-1 if axis == dim else 1 for axis in range(len(shape))])
    return gain


def centred(stream_key, shape, spread, reach, shards=(), held_as=jnp.bfloat16):
    loudness = levels(stream_key, shape, shards, -0.22, 0.18) if shards else 1.0
    values = jax.random.normal(stream_key, shape, jnp.float32) * spread * loudness
    return jnp.minimum(jnp.maximum(values, -reach), reach).astype(held_as)


def setup_inputs(seed: int = 0) -> dict:
    key_of = jax.random.split(jax.random.key(seed), 18)
    tokens = centred(key_of[0], (GROUPS, SLOTS, D), 1.0, 6.0, ((0, 4), (1, 8)))
    cotangent = centred(key_of[1], (GROUPS, SLOTS, D), 1.0, 6.0, ((0, 4), (1, 8)))
    doc_lengths = draw_doc_lengths(jax.random.fold_in(key_of[17], 71), 0)
    true_counts = draw_true_counts(jax.random.fold_in(key_of[17], 71), 0)
    w_query = centred(key_of[4], (D, HEADS * HD), D ** -0.5, 0.1875, ((0, 32),))
    w_key = centred(key_of[5], (D, HD), D ** -0.5, 0.1875, ((0, 32),))
    w_value = centred(key_of[6], (D, HD), D ** -0.5, 0.1875, ((0, 32),))
    w_out = centred(key_of[7], (D, HEADS * HD), (HEADS * HD) ** -0.5, 0.1875, ((0, 32),))
    w_gate = centred(key_of[8], (D, FF), D ** -0.5, 0.1875, ((0, 8), (1, 4)))
    w_up = centred(key_of[9], (D, FF), D ** -0.5, 0.1875, ((0, 8), (1, 4)))
    w_down = centred(key_of[10], (D, FF), FF ** -0.5, 0.078125, ((0, 8), (1, 4)))
    attn_norm_gain = jnp.clip(1.0 + 0.1 * jax.random.normal(key_of[11], (D,), jnp.float32), 0.5, 1.5).astype(jnp.bfloat16)
    query_gain = jnp.clip(1.0 + 0.1 * jax.random.normal(key_of[12], (HD,), jnp.float32), 0.5, 1.5).astype(jnp.bfloat16)
    key_gain = jnp.clip(1.0 + 0.1 * jax.random.normal(key_of[13], (HD,), jnp.float32), 0.5, 1.5).astype(jnp.bfloat16)
    attn_post_gain = jnp.clip(1.0 + 0.1 * jax.random.normal(key_of[14], (D,), jnp.float32), 0.5, 1.5).astype(jnp.bfloat16)
    ffn_norm_gain = jnp.clip(1.0 + 0.1 * jax.random.normal(key_of[15], (D,), jnp.float32), 0.5, 1.5).astype(jnp.bfloat16)
    ffn_post_gain = jnp.clip(1.0 + 0.1 * jax.random.normal(key_of[16], (D,), jnp.float32), 0.5, 1.5).astype(jnp.bfloat16)
    return {"tokens": tokens, "cotangent": cotangent, "doc_lengths": doc_lengths, "true_counts": true_counts, "w_query": w_query, "w_key": w_key, "w_value": w_value, "w_out": w_out, "w_gate": w_gate, "w_up": w_up, "w_down": w_down, "attn_norm_gain": attn_norm_gain, "query_gain": query_gain, "key_gain": key_gain, "attn_post_gain": attn_post_gain, "ffn_norm_gain": ffn_norm_gain, "ffn_post_gain": ffn_post_gain}


NORM_EPS = 1e-06
ROPE_BASE = 10000.0
NEGATIVE = -1e+30

@jax.custom_vjp
def low(v):
    return lax.optimization_barrier(v.astype(jnp.bfloat16)).astype(jnp.float32)

@jax.custom_vjp
def low_back(v):
    return v

def low_keep(v):
    return (low(v), None)

def low_pass(kept, grad):
    return (grad,)

def back_keep(v):
    return (v, None)

def back_low(kept, grad):
    return (low(grad),)
low.defvjp(low_keep, low_pass)
low_back.defvjp(back_keep, back_low)

def matmul(left_side, right_side):
    return jnp.dot(left_side, right_side, precision=lax.Precision.HIGHEST, preferred_element_type=jnp.float32)

def matmul_t(left_side, right_side):
    return lax.dot_general(left_side, right_side, (((1,), (1,)), ((), ())), precision=lax.Precision.HIGHEST, preferred_element_type=jnp.float32)

def scaled_norm(values, gain_vec):
    return values * lax.rsqrt(lax.optimization_barrier(jnp.mean(values * values, axis=-1, keepdims=True)) + NORM_EPS) * gain_vec

def rotate(values, position):
    half_dim = values.shape[-1] // 2
    frequency = ROPE_BASE ** (-2.0 * jnp.arange(half_dim, dtype=jnp.float32) / values.shape[-1])
    angles = position.astype(jnp.float32)[..., None] * frequency
    first_half = values[..., :half_dim]
    second_half = values[..., half_dim:]
    cosine = jnp.cos(angles)
    sine_part = jnp.sin(angles)
    return jnp.concatenate([first_half * cosine - second_half * sine_part, second_half * cosine + first_half * sine_part], axis=-1)

def layout(lengths, counts, first_slot, row_count):
    starts = (jnp.cumsum(lengths) - lengths).astype(jnp.int32)
    slot_index = (first_slot + jnp.arange(row_count, dtype=jnp.int32)).astype(jnp.int32)
    member = (slot_index[:, None] >= starts[None, :]).astype(jnp.int32)
    document = (lax.optimization_barrier(jnp.sum(member, axis=1)) - 1).astype(jnp.int32)
    onehot = (document[:, None] == jnp.arange(lengths.shape[0], dtype=jnp.int32)[None, :]).astype(jnp.int32)
    position = (slot_index - lax.optimization_barrier(jnp.sum(onehot * starts[None, :], axis=1))).astype(jnp.int32)
    padded = lax.optimization_barrier(jnp.sum(onehot * (lengths - counts)[None, :], axis=1)).astype(jnp.int32)
    return (position, padded)

def visible(position, padded, distance):
    query_pos = position[:, None]
    return (distance >= 0) & (distance < WINDOW) & (distance <= query_pos) & ((query_pos - distance >= padded[:, None]) | (distance == 0))

def attend(queries, key_rows, values, position, padded):
    block_rows = min(512, SLOTS)
    key_pad = jnp.concatenate([jnp.zeros((WINDOW, HD), jnp.float32), key_rows], axis=0)
    value_pad = jnp.concatenate([jnp.zeros((WINDOW, HD), jnp.float32), values], axis=0)
    distance = WINDOW + jnp.arange(block_rows, dtype=jnp.int32)[:, None] - jnp.arange(block_rows + WINDOW, dtype=jnp.int32)[None, :]
    score_scale = HD ** (-0.5)

    @jax.checkpoint
    def one_block(block_id):
        first_row = (block_id * block_rows).astype(jnp.int32)
        query_block = lax.dynamic_slice_in_dim(queries, first_row, block_rows, 0)
        key_block = lax.dynamic_slice_in_dim(key_pad, first_row, block_rows + WINDOW, 0)
        value_block = lax.dynamic_slice_in_dim(value_pad, first_row, block_rows + WINDOW, 0)
        row_pos = lax.dynamic_slice_in_dim(position, first_row, block_rows, 0)
        row_pad = lax.dynamic_slice_in_dim(padded, first_row, block_rows, 0)
        raw_scores = jnp.einsum('qhd,kd->hqk', query_block, key_block, precision=lax.Precision.HIGHEST)
        raw_scores = low_back(raw_scores)
        scores = jnp.where(visible(row_pos, row_pad, distance)[None], raw_scores * score_scale, NEGATIVE)
        attn_probs = low(jax.nn.softmax(scores, axis=-1))
        attended = jnp.einsum('hqk,kd->qhd', attn_probs, value_block, precision=lax.Precision.HIGHEST)
        return attended.reshape(block_rows, HEADS * HD)
    blocks = lax.map(one_block, jnp.arange(SLOTS // block_rows, dtype=jnp.int32))
    return blocks.reshape(SLOTS, HEADS * HD)

def layer(inputs, w_query, w_key, w_value, w_out, w_gate, w_up, w_down, gain_an, gain_q, gain_k, gain_ap, gain_fn, gain_fp, position, padded):
    attn_in = low(scaled_norm(inputs, gain_an))
    query_lin = low_back(matmul(attn_in, w_query))
    key_lin = low_back(matmul(attn_in, w_key))
    values = low(low_back(matmul(attn_in, w_value)))
    queries = low(rotate(scaled_norm(query_lin.reshape(SLOTS, HEADS, HD), gain_q), position[:, None]))
    key_rows = low(rotate(scaled_norm(key_lin, gain_k), position))
    attended = low_back(low(attend(queries, key_rows, values, position, padded)))
    attn_out = low_back(matmul_t(attended, w_out))
    middle = inputs + scaled_norm(attn_out, gain_ap)
    ffn_in = low(scaled_norm(middle, gain_fn))
    gate_proj = low_back(matmul(ffn_in, w_gate))
    up_proj = low_back(matmul(ffn_in, w_up))
    act_low = low(jax.nn.gelu(gate_proj, approximate=True) * up_proj)
    ffn_out = low_back(matmul_t(act_low, w_down))
    return middle + scaled_norm(ffn_out, gain_fp)

def reference(tokens, cotangent, doc_lengths, true_counts, w_query, w_key, w_value, w_out, w_gate, w_up, w_down, attn_norm_gain, query_gain, key_gain, attn_post_gain, ffn_norm_gain, ffn_post_gain):
    params = tuple((weight.astype(jnp.float32) for weight in (w_query, w_key, w_value, w_out, w_gate, w_up, w_down, attn_norm_gain, query_gain, key_gain, attn_post_gain, ffn_norm_gain, ffn_post_gain)))

    def one_group(totals, group_item):
        group_tokens, group_cot, lengths, counts = group_item
        position, padded = layout(lengths, counts, 0, SLOTS)

        def forward(inputs, *weights):
            return layer(inputs, *weights, position, padded)
        result, pull_back = jax.vjp(forward, group_tokens.astype(jnp.float32), *params)
        gradients = pull_back(group_cot.astype(jnp.float32))
        totals = tuple((total + grad_part for total, grad_part in zip(totals, gradients[1:])))
        return (totals, (result.astype(jnp.bfloat16), gradients[0]))
    zero_grads = tuple((jnp.zeros_like(weight) for weight in params))
    totals, stacked = lax.scan(one_group, zero_grads, (tokens, cotangent, doc_lengths, true_counts))
    return (stacked[0], stacked[1], totals[0], totals[1], totals[2], totals[3], totals[4], totals[5], totals[6], totals[7], totals[8], totals[9], totals[10], totals[11], totals[12])
```

```python
import jax
import jax.numpy as jnp
from jax import lax
from jax.sharding import PartitionSpec as P

WINDOW = 512


NORM_EPS = 1e-06
ROPE_BASE = 10000.0
NEGATIVE = -1e30


def from_behind(value, axis, steps):
    count = lax.axis_size(axis)
    first, last = (max(0, -steps), min(count, count - steps))
    return lax.ppermute(value, axis, [(source, source + steps) for source in range(first, last)])


def seq_masks():
    return [1 << bit for bit in range(lax.axis_size("seq").bit_length() - 1)]


def swap(value, axis, mask):
    count = lax.axis_size(axis)
    return lax.ppermute(value, axis, [(source, source ^ mask) for source in range(count)])


def shift(value, axis, steps):
    count = lax.axis_size(axis)
    return lax.ppermute(value, axis, [(source, (source + steps) % count) for source in range(count)])


def gather_seq(block, order):
    stack, held = block[None], []
    for mask in order:
        place = sum(1 for other in held if other > mask)
        full = stack.reshape((2,) * len(held) + block.shape)
        stack = jnp.stack([full, swap(full, "seq", mask)], axis=place)
        held.append(mask)
    stack = stack.reshape((-1,) + block.shape)
    index = jnp.arange(stack.shape[0], dtype=jnp.int32) ^ lax.axis_index("seq")
    return jnp.take(stack, index, axis=0, mode="clip")


def gather_seq_rows(block, split):
    far = seq_masks()[1:]
    top = gather_seq(block[:split], far[::-1] + [1])
    bottom = gather_seq(block[split:], far + [1])
    whole = jnp.concatenate([top, bottom], axis=1)
    return whole.reshape((-1,) + block.shape[1:])


def scatter_seq(blocks, order):
    masks = seq_masks()[::-1]
    shape = blocks.shape[1:]
    part = blocks.reshape((2,) * len(masks) + shape)
    me = lax.axis_index("seq")
    for mask in order:
        axis = masks.index(mask)
        bit = (me // mask) % 2
        keep = lax.dynamic_index_in_dim(part, bit, axis, keepdims=False)
        send = lax.dynamic_index_in_dim(part, 1 - bit, axis, keepdims=False)
        got = swap(send.astype(jnp.bfloat16), "seq", mask)
        part = keep.astype(jnp.float32) + got.astype(jnp.float32)
        masks.remove(mask)
    return part


def scatter_seq_rows(rows, split):
    blocks = rows.reshape((lax.axis_size("seq"), -1) + rows.shape[1:])
    far = seq_masks()[1:]
    top = scatter_seq(blocks[:, :split], [1] + far[::-1])
    bottom = scatter_seq(blocks[:, split:], [1] + far)
    return jnp.concatenate([top, bottom], axis=0)


def gather_fsdp(block):
    count = lax.axis_size("fsdp")
    parts = [block] + [shift(block, "fsdp", steps) for steps in range(1, count)]
    index = (lax.axis_index("fsdp") - jnp.arange(count, dtype=jnp.int32)) % count
    stack = jnp.take(jnp.stack(parts), index, axis=0, mode="clip")
    return stack.reshape((-1,) + block.shape[1:])


def scatter_fsdp(rows):
    count = lax.axis_size("fsdp")
    blocks = rows.reshape((count, -1) + rows.shape[1:])
    mine = lax.axis_index("fsdp")
    total = lax.dynamic_index_in_dim(blocks, mine, 0, keepdims=False)
    for steps in range(1, count):
        send = lax.dynamic_index_in_dim(blocks, (mine + steps) % count, 0, keepdims=False)
        total = total + shift(send.astype(jnp.bfloat16), "fsdp", steps).astype(jnp.float32)
    return total


def half_rows(count):
    return (count // 2 + 15) // 16 * 16


def pack_gains(wide, narrow):
    rows = wide[0].shape[0]
    columns = wide + [jnp.pad(vec, (0, rows - vec.shape[0])) for vec in narrow]
    return jnp.stack(columns + [jnp.zeros((rows,), wide[0].dtype)] * (128 - len(columns)), axis=1)


def matmul(left_side, right_side):
    return jnp.dot(left_side, right_side, preferred_element_type=jnp.float32)


def matmul_t(left_side, right_side):
    return lax.dot_general(
        left_side, right_side, (((1,), (1,)), ((), ())), preferred_element_type=jnp.float32
    )


def matmul_tn(left_side, right_side):
    return lax.dot_general(
        left_side, right_side, (((0,), (0,)), ((), ())), preferred_element_type=jnp.float32
    )


def scaled_norm(values, gain_vec):
    return (
        values * lax.rsqrt(jnp.mean(values * values, axis=-1, keepdims=True) + NORM_EPS) * gain_vec
    )


def rotate(values, position):
    half_dim = values.shape[-1] // 2
    frequency = ROPE_BASE ** (-2.0 * jnp.arange(half_dim, dtype=jnp.float32) / values.shape[-1])
    angles = position.astype(jnp.float32)[..., None] * frequency
    first_half = values[..., :half_dim]
    second_half = values[..., half_dim:]
    cosine = jnp.cos(angles)
    sine_part = jnp.sin(angles)
    return jnp.concatenate(
        [
            first_half * cosine - second_half * sine_part,
            second_half * cosine + first_half * sine_part,
        ],
        axis=-1,
    )


def layout(lengths, counts, first_slot, row_count):
    starts = jnp.cumsum(lengths) - lengths
    slot_index = first_slot + jnp.arange(row_count, dtype=jnp.int32)
    member = (slot_index[:, None] >= starts[None, :]).astype(jnp.int32)
    document = jnp.sum(member, axis=1) - 1
    onehot = (document[:, None] == jnp.arange(lengths.shape[0], dtype=jnp.int32)[None, :]).astype(
        jnp.int32
    )
    position = slot_index - jnp.sum(onehot * starts[None, :], axis=1)
    padded = jnp.sum(onehot * (lengths - counts)[None, :], axis=1)
    return (position, padded)


def visible(position, padded, distance):
    query_pos = position[:, None]
    return (
        (distance >= 0)
        & (distance < WINDOW)
        & (distance <= query_pos)
        & ((query_pos - distance >= padded[:, None]) | (distance == 0))
    )


def block_scores(query_block, key_block, row_pos, row_pad, distance, score_scale):
    raw_scores = jnp.einsum(
        "qhd,kd->hqk", query_block, key_block, preferred_element_type=jnp.float32
    )
    return jnp.where(visible(row_pos, row_pad, distance)[None], raw_scores * score_scale, NEGATIVE)


def on_device(
    tokens,
    cotangent,
    doc_lengths,
    true_counts,
    w_query,
    w_key,
    w_value,
    w_out,
    w_gate,
    w_up,
    w_down,
    attn_norm_gain,
    query_gain,
    key_gain,
    attn_post_gain,
    ffn_norm_gain,
    ffn_post_gain,
):
    row_count = tokens.shape[1]
    head_dim = w_key.shape[1]
    heads_width = w_query.shape[1]
    head_count = heads_width // head_dim
    score_scale = head_dim ** (-0.5)
    hop_count = (WINDOW + row_count - 1) // row_count
    block_rows = min(512, row_count)
    inputs = tokens[0].astype(jnp.float32)
    upstream = cotangent[0].astype(jnp.float32)
    position, padded = layout(
        doc_lengths[0], true_counts[0], lax.axis_index("seq") * row_count, row_count
    )
    shards = lax.axis_size("seq") * lax.axis_size("fsdp")
    narrow_rows = query_gain.shape[0]
    first_pack = jnp.concatenate(
        [
            w_query,
            w_key,
            w_value,
            pack_gains(
                [attn_norm_gain, attn_post_gain, ffn_norm_gain, ffn_post_gain],
                [query_gain, key_gain],
            ),
        ],
        axis=1,
    )
    first_rows = gather_fsdp(first_pack)
    out_rows = gather_fsdp(w_out)
    split = half_rows(first_rows.shape[0])
    first_full = gather_seq_rows(first_rows, split)
    wo_full = gather_seq_rows(out_rows, split)
    wq_full = first_full[:, :heads_width]
    wk_full = first_full[:, heads_width : heads_width + head_dim]
    wv_full = first_full[:, heads_width + head_dim : heads_width + 2 * head_dim]
    gain_cols = first_full[:, heads_width + 2 * head_dim :].astype(jnp.float32)
    gain_an, gain_ap, gain_fn, gain_fp = [gain_cols[:, index] for index in range(4)]
    gain_q, gain_k = [
        gain_cols[:, index].reshape(shards, -1)[:, :narrow_rows].reshape(-1) for index in (4, 5)
    ]
    far = seq_masks()[1:]
    wg_full = gather_seq(w_gate, far[::-1] + [1]).reshape(-1, w_gate.shape[1])
    wu_full = gather_seq(w_up, far + [1]).reshape(-1, w_up.shape[1])
    wd_full = gather_seq_rows(w_down, half_rows(w_down.shape[0]))
    attn_in_f, an_pull = jax.vjp(scaled_norm, inputs, gain_an)
    attn_in = attn_in_f.astype(jnp.bfloat16)
    query_lin = matmul(attn_in, wq_full).reshape(row_count, head_count, head_dim)
    key_lin = matmul(attn_in, wk_full)
    values = matmul(attn_in, wv_full).astype(jnp.bfloat16)
    query_rot, q_pull = jax.vjp(
        lambda lin_part, gain_vec: rotate(scaled_norm(lin_part, gain_vec), position[:, None]),
        query_lin,
        gain_q,
    )
    key_rot, k_pull = jax.vjp(
        lambda lin_part, gain_vec: rotate(scaled_norm(lin_part, gain_vec), position),
        key_lin,
        gain_k,
    )
    queries = query_rot.astype(jnp.bfloat16)
    key_rows = key_rot.astype(jnp.bfloat16)
    kv_stack = jnp.stack([key_rows, values], axis=0)
    far_parts = []
    for step_back in range(hop_count, 0, -1):
        far_parts.append(from_behind(kv_stack, "seq", step_back))
    extended = jnp.concatenate(far_parts + [kv_stack], axis=1)
    key_ext = extended[0]
    value_ext = extended[1]
    distance = (
        WINDOW
        + jnp.arange(block_rows, dtype=jnp.int32)[:, None]
        - jnp.arange(block_rows + WINDOW, dtype=jnp.int32)[None, :]
    )
    scores = block_scores(queries, key_ext, position, padded, distance, score_scale)
    row_peak = jnp.max(scores, axis=-1, keepdims=True)
    exp_scores = jnp.exp(scores - row_peak)
    row_total = jnp.sum(exp_scores, axis=-1, keepdims=True)
    attn_probs = exp_scores / row_total
    log_parts = row_peak + jnp.log(row_total)
    attended_parts = jnp.einsum(
        "hqk,kd->qhd",
        attn_probs.astype(jnp.bfloat16),
        value_ext,
        preferred_element_type=jnp.float32,
    )
    attended = attended_parts.reshape(row_count, heads_width)
    attended_low = attended.astype(jnp.bfloat16)
    attn_out = matmul_t(attended_low, wo_full)
    post_attn, ap_pull = jax.vjp(scaled_norm, attn_out, gain_ap)
    middle = inputs + post_attn
    ffn_in_f, fn_pull = jax.vjp(scaled_norm, middle, gain_fn)
    ffn_in = ffn_in_f.astype(jnp.bfloat16)
    ffn_rows_in = lax.all_gather(ffn_in, "fsdp", axis=0, tiled=True)
    gate_proj = matmul(ffn_rows_in, wg_full)
    up_proj = matmul(ffn_rows_in, wu_full)
    act_f, act_pull = jax.vjp(
        lambda gate_in, up_in: jax.nn.gelu(gate_in, approximate=True) * up_in, gate_proj, up_proj
    )
    act_low = act_f.astype(jnp.bfloat16)
    ffn_out = lax.psum_scatter(
        matmul_t(act_low, wd_full).astype(jnp.bfloat16), "fsdp", scatter_dimension=0, tiled=True
    ).astype(jnp.float32)
    post_ffn, fp_pull = jax.vjp(scaled_norm, ffn_out, gain_fp)
    output = (middle + post_ffn).astype(jnp.bfloat16)[None]
    d_ffn_out, grad_fp = fp_pull(upstream)
    d_ffn_low = d_ffn_out.astype(jnp.bfloat16)
    d_rows = lax.all_gather(d_ffn_low, "fsdp", axis=0, tiled=True)
    d_act = matmul(d_rows, wd_full)
    grad_down = matmul_tn(d_rows, act_low)
    d_gate, d_up = act_pull(d_act)
    d_gate_low = d_gate.astype(jnp.bfloat16)
    d_up_low = d_up.astype(jnp.bfloat16)
    grad_gate = matmul_tn(ffn_rows_in, d_gate_low)
    grad_up = matmul_tn(ffn_rows_in, d_up_low)
    d_ffn_in = lax.psum_scatter(
        (matmul_t(d_gate_low, wg_full) + matmul_t(d_up_low, wu_full)).astype(jnp.bfloat16),
        "fsdp",
        scatter_dimension=0,
        tiled=True,
    ).astype(jnp.float32)
    d_mid_part, grad_fn = fn_pull(d_ffn_in)
    d_middle = upstream + d_mid_part
    d_attn_out, grad_ap = ap_pull(d_middle)
    d_attn_low = d_attn_out.astype(jnp.bfloat16)
    grad_out = matmul_tn(d_attn_low, attended_low)
    d_attended = (
        matmul(d_attn_low, wo_full).astype(jnp.bfloat16).reshape(row_count, head_count, head_dim)
    )
    d_key_ext = jnp.zeros((WINDOW + row_count, head_dim), jnp.float32)
    d_value_ext = jnp.zeros((WINDOW + row_count, head_dim), jnp.float32)
    scores = block_scores(queries, key_ext, position, padded, distance, score_scale)
    attn_probs = jnp.exp(scores - log_parts)
    probs_low = attn_probs.astype(jnp.bfloat16)
    d_probs = jnp.einsum("qhd,kd->hqk", d_attended, value_ext, preferred_element_type=jnp.float32)
    row_delta = jnp.sum(attn_probs * d_probs, axis=-1, keepdims=True)
    d_scores = (attn_probs * (d_probs - row_delta) * score_scale).astype(jnp.bfloat16)
    query_grad_parts = jnp.einsum(
        "hqk,kd->qhd", d_scores, key_ext, preferred_element_type=jnp.float32
    )
    d_key_ext = d_key_ext.at[0 : block_rows + WINDOW].add(
        jnp.einsum("hqk,qhd->kd", d_scores, queries, preferred_element_type=jnp.float32)
    )
    d_value_ext = d_value_ext.at[0 : block_rows + WINDOW].add(
        jnp.einsum("hqk,qhd->kd", probs_low, d_attended, preferred_element_type=jnp.float32)
    )
    grad_stack = jnp.stack([d_key_ext, d_value_ext], axis=0)
    halo_part = jnp.concatenate(
        [
            jnp.zeros((2, hop_count * row_count - WINDOW, head_dim), jnp.float32),
            grad_stack[:, :WINDOW],
        ],
        axis=1,
    )
    local_part = grad_stack[:, WINDOW:]
    for step_back in range(hop_count, 0, -1):
        piece_start = (hop_count - step_back) * row_count
        local_part = local_part + from_behind(
            halo_part[:, piece_start : piece_start + row_count].astype(jnp.bfloat16),
            "seq",
            -step_back,
        ).astype(jnp.float32)
    d_query_lin, grad_q = q_pull(query_grad_parts)
    d_key_lin, grad_k = k_pull(local_part[0])
    d_query_low = d_query_lin.reshape(row_count, heads_width).astype(jnp.bfloat16)
    d_key_low = d_key_lin.astype(jnp.bfloat16)
    d_value_low = local_part[1].astype(jnp.bfloat16)
    grad_query = matmul_tn(attn_in, d_query_low)
    grad_key = matmul_tn(attn_in, d_key_low)
    grad_value = matmul_tn(attn_in, d_value_low)
    d_attn_in = (
        matmul_t(d_query_low, wq_full)
        + matmul_t(d_key_low, wk_full)
        + matmul_t(d_value_low, wv_full)
    )
    d_in_part, grad_an = an_pull(d_attn_in)
    input_grad = (d_middle + d_in_part)[None]
    grad_split = half_rows(first_rows.shape[0])
    query_rows = scatter_fsdp(scatter_seq_rows(grad_query, grad_split))
    out_grad_rows = scatter_fsdp(scatter_seq_rows(grad_out, grad_split))
    spare = grad_an.shape[0] // shards - narrow_rows
    narrow_grads = [
        jnp.pad(vec.reshape(shards, -1), ((0, 0), (0, spare))).reshape(-1) for vec in (grad_q, grad_k)
    ]
    last_pack = jnp.concatenate(
        [
            grad_key,
            grad_value,
            pack_gains([grad_an, grad_ap, grad_fn, grad_fp] + narrow_grads, []),
        ],
        axis=1,
    )
    last_rows = scatter_fsdp(scatter_seq_rows(last_pack, grad_split))
    gain_rows = last_rows[:, 2 * head_dim :]
    ffn_grads = (
        scatter_seq(grad_gate.astype(jnp.bfloat16).reshape((-1,) + w_gate.shape), [1] + far[::-1]),
        scatter_seq(grad_up.astype(jnp.bfloat16).reshape((-1,) + w_up.shape), [1] + far),
        scatter_seq_rows(grad_down.astype(jnp.bfloat16), half_rows(w_down.shape[0])),
    )
    reduced = (
        query_rows,
        last_rows[:, :head_dim],
        last_rows[:, head_dim : 2 * head_dim],
        out_grad_rows,
        gain_rows[:, 0],
        gain_rows[:narrow_rows, 4],
        gain_rows[:narrow_rows, 5],
        gain_rows[:, 1],
        gain_rows[:, 2],
        gain_rows[:, 3],
    )
    return (
        output,
        input_grad,
        reduced[0],
        reduced[1],
        reduced[2],
        reduced[3],
        ffn_grads[0],
        ffn_grads[1],
        ffn_grads[2],
        reduced[4],
        reduced[5],
        reduced[6],
        reduced[7],
        reduced[8],
        reduced[9],
    )


def solution(mesh):
    return jax.shard_map(
        on_device,
        mesh=mesh,
        in_specs=(
            P("fsdp", "seq", None),
            P("fsdp", "seq", None),
            P("fsdp", None),
            P("fsdp", None),
            P(("seq", "fsdp"), None),
            P(("seq", "fsdp"), None),
            P(("seq", "fsdp"), None),
            P(("seq", "fsdp"), None),
            P("seq", "fsdp"),
            P("seq", "fsdp"),
            P("seq", "fsdp"),
            P(("seq", "fsdp")),
            P(("seq", "fsdp")),
            P(("seq", "fsdp")),
            P(("seq", "fsdp")),
            P(("seq", "fsdp")),
            P(("seq", "fsdp")),
        ),
        out_specs=(
            P("fsdp", "seq", None),
            P("fsdp", "seq", None),
            P(("seq", "fsdp"), None),
            P(("seq", "fsdp"), None),
            P(("seq", "fsdp"), None),
            P(("seq", "fsdp"), None),
            P("seq", "fsdp"),
            P("seq", "fsdp"),
            P("seq", "fsdp"),
            P(("seq", "fsdp")),
            P(("seq", "fsdp")),
            P(("seq", "fsdp")),
            P(("seq", "fsdp")),
            P(("seq", "fsdp")),
            P(("seq", "fsdp")),
        ),
        check_vma=False,
    )
```

```python
import functools

import jax
import jax.numpy as jnp
from jax import lax
from jax.experimental import pallas as pl
from jax.experimental.pallas import tpu as pltpu
from jax.sharding import PartitionSpec as P

WINDOW = 512
NORM_EPS = 1e-06
ROPE_BASE = 10000.0
NEGATIVE = -1e30
LANES = 128
VMEM_LIMIT = 56 * 2**20
BF16 = jnp.bfloat16
F32 = jnp.float32


def from_behind(value, steps):
    count = lax.axis_size("seq")
    first, last = (max(0, -steps), min(count, count - steps))
    return lax.ppermute(value, "seq", [(source, source + steps) for source in range(first, last)])


def seq_masks():
    return [1 << bit for bit in range(lax.axis_size("seq").bit_length() - 1)]


def swap(value, axis, mask):
    count = lax.axis_size(axis)
    return lax.ppermute(value, axis, [(source, source ^ mask) for source in range(count)])


def shift(value, axis, steps):
    count = lax.axis_size(axis)
    return lax.ppermute(value, axis, [(source, (source + steps) % count) for source in range(count)])


def diagonal(value):
    seqs, planes = lax.axis_size("seq"), lax.axis_size("fsdp")
    pairs = [
        (seq * planes + plane, (seq ^ 2) * planes + (plane ^ 1))
        for seq in range(seqs)
        for plane in range(planes)
    ]
    return lax.ppermute(value, ("seq", "fsdp"), pairs)


def group_blocks(rows):
    return [diagonal(rows), swap(rows, "seq", 2), swap(rows, "fsdp", 1), rows]


def on_own_slice():
    return (lax.axis_index("seq") // 2) % 2 == lax.axis_index("fsdp") // 2


def ordered(parts):
    parts = [parts[rel] for rel in range(len(parts))]
    if parts[0].shape[0] % 16 == 0:
        return parts
    index = jnp.arange(len(parts), dtype=jnp.int32) ^ lax.axis_index("seq")
    whole = jnp.take(jnp.stack(parts), index, axis=0, mode="clip")
    return [whole.reshape(-1, whole.shape[-1])]


def gather_attn(block):
    parts = {0: block}
    for rel in range(2, lax.axis_size("seq"), 2):
        parts[rel] = swap(block, "seq", rel)
    for rel in list(parts):
        parts[rel ^ 1] = swap(parts[rel], "seq", 1)
    return ordered(parts)


def gather_ffn(block):
    other_plane = swap(block, "fsdp", 2)
    own = on_own_slice()
    mine = jnp.where(own, block, other_plane)
    theirs = jnp.where(own, other_plane, block)
    parts = {0: mine, 2: swap(theirs, "seq", 2)}
    for mask in [mask for mask in seq_masks() if mask > 2] + [1]:
        parts.update({rel ^ mask: swap(part, "seq", mask) for rel, part in parts.items()})
    return ordered(parts)


def add_rounded(first, second):
    return (first.astype(F32) + second.astype(F32)).astype(BF16)


def cut(pair, count):
    if len(pair) == 2:
        return pair
    index = jnp.arange(count, dtype=jnp.int32) ^ lax.axis_index("seq")
    blocks = jnp.take(pair[0].reshape(count, -1, pair[0].shape[-1]), index, axis=0, mode="clip")
    return blocks[0::2], blocks[1::2]


def scatter_ffn(pair):
    keep, send = cut(pair, lax.axis_size("seq"))
    part = add_rounded(keep, swap(send, "seq", 1))
    for mask in [mask for mask in seq_masks() if mask > 2][::-1]:
        half = part.shape[0] // 2
        part = add_rounded(part[:half], swap(part[half:], "seq", mask))
    crossed = swap(part[1], "seq", 2)
    own = on_own_slice()
    stays = jnp.where(own, part[0], crossed)
    leaves = jnp.where(own, crossed, part[0])
    return stays.astype(F32) + swap(leaves, "fsdp", 2).astype(F32)


def scatter_attn(pair):
    keep, send = cut(pair, lax.axis_size("seq"))
    part = add_rounded(keep, swap(send, "seq", 1))
    rows = part[0].astype(F32)
    for index in range(1, part.shape[0]):
        rows = rows + swap(part[index], "seq", 2 * index).astype(F32)
    planes = lax.axis_size("fsdp")
    blocks = rows.reshape((planes, -1) + rows.shape[1:])
    mine = lax.axis_index("fsdp")
    total = lax.dynamic_index_in_dim(blocks, mine, 0, keepdims=False)
    for steps in range(1, planes):
        send = lax.dynamic_index_in_dim(blocks, (mine + steps) % planes, 0, keepdims=False)
        total = total + shift(send.astype(BF16), "fsdp", steps).astype(F32)
    return total


def dot(left, right):
    return jnp.dot(left, right, preferred_element_type=F32)


def dot_t(left, right):
    return lax.dot_general(left, right, (((1,), (1,)), ((), ())), preferred_element_type=F32)


def dot_tn(left, right):
    return lax.dot_general(left, right, (((0,), (0,)), ((), ())), preferred_element_type=F32)


def inverse_rms(values):
    return lax.rsqrt(jnp.mean(values * values, axis=-1, keepdims=True) + NORM_EPS)


def norm_back(normed, scale, gain, upstream):
    scaled = upstream * gain
    back = scale * (scaled - normed * jnp.mean(scaled * normed, axis=-1, keepdims=True))
    return back, jnp.sum(upstream * normed, axis=0, keepdims=True)


def rotate(values, cosine, sine):
    half = values.shape[-1] // 2
    first, second = values[:, :half], values[:, half:]
    return jnp.concatenate(
        [first * cosine - second * sine, second * cosine + first * sine], axis=-1
    )


def iota(shape, dim):
    return lax.broadcasted_iota(jnp.int32, shape, dim)


def unit(shape, hits):
    return jnp.where(hits, 1.0, 0.0).astype(BF16)


def spread_matrix(narrow, wide, narrow_rows, wide_rows):
    row, col = iota((narrow, wide), 0), iota((narrow, wide), 1)
    return unit((narrow, wide), col == (row // narrow_rows) * wide_rows + row % narrow_rows)


def tiles_of(width, step):
    return [(start, min(step, width - start)) for start in range(0, width, step)]


def start_placing(parts, dest, sems, base, seq):
    rows = parts[0].shape[0]
    copies = []
    for rel, part in enumerate(parts):
        start = pl.multiple_of((seq ^ rel) * rows, 16) if len(parts) > 1 else 0
        copies.append(
            pltpu.make_async_copy(part, dest.at[pl.ds(start, rows), :], sems.at[base + rel])
        )
    for copy in copies:
        copy.start()
    return copies


def start_cutting(whole, outs, sems, base, seq):
    if len(outs) == 1:
        copies = [pltpu.make_async_copy(whole, outs[0], sems.at[base])]
    else:
        half, rows = outs[0].shape[0], outs[0].shape[1]
        copies = []
        for rel in range(2 * half):
            start = pl.multiple_of((seq ^ rel) * rows, 16)
            copies.append(
                pltpu.make_async_copy(
                    whole.at[pl.ds(start, rows), :], outs[rel % 2].at[rel // 2], sems.at[base + rel]
                )
            )
    for copy in copies:
        copy.start()
    return copies


def cut_shapes(height, width, count):
    rows = height // count
    if rows % 16:
        return [jax.ShapeDtypeStruct((height, width), BF16)]
    return [jax.ShapeDtypeStruct((count // 2, rows, width), BF16)] * 2


def wait_all(copies):
    for copy in copies:
        copy.wait()


SMEM_SPEC = pl.BlockSpec(memory_space=pltpu.SMEM)
VMEM_SPEC = pl.BlockSpec(memory_space=pltpu.VMEM)
ANY_SPEC = pl.BlockSpec(memory_space=pl.ANY)


def call(kernel, outs, out_specs, ins, in_specs, scratch=(), flops=0, moved=0, exps=0):
    return pl.pallas_call(
        kernel,
        out_shape=tuple(outs),
        in_specs=list(in_specs),
        out_specs=tuple(out_specs),
        scratch_shapes=list(scratch),
        compiler_params=pltpu.CompilerParams(vmem_limit_bytes=VMEM_LIMIT),
        cost_estimate=pl.CostEstimate(flops=flops, bytes_accessed=moved, transcendentals=exps),
    )(*ins)


def shape_of(dims, dtype):
    return jax.ShapeDtypeStruct(dims, dtype)


def pack_kernel(wq_ref, wk_ref, wv_ref, *refs):
    wide, narrow, out_ref = refs[:4], refs[4:6], refs[6]
    rows, heads_width, head_dim = wq_ref.shape[0], wq_ref.shape[1], wk_ref.shape[1]
    out_ref[:, :heads_width] = wq_ref[...]
    out_ref[:, heads_width : heads_width + head_dim] = wk_ref[...]
    out_ref[:, heads_width + head_dim : heads_width + 2 * head_dim] = wv_ref[...]
    row = iota((16, rows), 0)
    held = jnp.zeros((16, rows), F32)
    for index, ref in enumerate(wide):
        held = held + jnp.where(row == index, ref[...].astype(F32), 0.0)
    small = narrow[0].shape[1]
    fit = unit((small, rows), iota((small, rows), 0) == iota((small, rows), 1))
    for index, ref in enumerate(narrow):
        spread = dot(jnp.broadcast_to(ref[...].astype(F32), (16, small)).astype(BF16), fit)
        held = held + jnp.where(row == 4 + index, spread, 0.0)
    place = unit((16, LANES), iota((16, LANES), 0) == iota((16, LANES), 1))
    out_ref[:, heads_width + 2 * head_dim :] = dot_tn(held.astype(BF16), place).astype(BF16)


def pack_first(w_query, w_key, w_value, wide, narrow):
    rows = w_query.shape[0]
    width = w_query.shape[1] + 2 * w_key.shape[1] + LANES
    ins = [w_query, w_key, w_value] + [vec.reshape(1, -1) for vec in wide + narrow]
    return call(
        pack_kernel,
        [shape_of((rows, width), BF16)],
        [VMEM_SPEC],
        ins,
        [VMEM_SPEC] * len(ins),
    )[0]


def planes_kernel(place_ref, *refs):
    parts, out_ref = refs[:-1], refs[-1]
    count, rows = len(parts), parts[0].shape[0]
    total = None
    for steps, part in enumerate(parts):
        plane = lax.rem(place_ref[1] - steps + count, count)
        row, col = iota((count * rows, rows), 0), iota((count * rows, rows), 1)
        term = dot(unit((count * rows, rows), row == col + plane * rows), part[...])
        total = term if total is None else total + term
    out_ref[...] = total.astype(BF16)


def gather_planes(block, place):
    count = lax.axis_size("fsdp")
    parts = [block] + [shift(block, "fsdp", steps) for steps in range(1, count)]
    rows, width = block.shape
    return call(
        planes_kernel,
        [shape_of((count * rows, width), BF16)],
        [VMEM_SPEC],
        [place] + parts,
        [SMEM_SPEC] + [VMEM_SPEC] * count,
        flops=2 * count * count * rows * rows * width,
        moved=4 * count * rows * width,
    )[0]


def attend_kernel(
    part_count,
    narrow_rows,
    wide_rows,
    head_count,
    place_ref,
    near_ref,
    back_ref,
    far_ref,
    cos_ref,
    sin_ref,
    low_ref,
    *refs,
):
    parts = refs[:part_count]
    (
        attn_in_ref,
        query_lin_ref,
        key_lin_ref,
        query_ref,
        keys_ref,
        probs_ref,
        attended_ref,
        gains_ref,
        small_gains_ref,
    ) = refs[part_count : part_count + 9]
    weights, inside, sems = refs[part_count + 9 :]
    copies = start_placing(parts, weights, sems, 0, place_ref[0])
    rows, width = near_ref.shape
    head_dim = key_lin_ref.shape[1]
    heads_width = head_count * head_dim
    score_scale = head_dim**-0.5
    blocks = [far_ref, back_ref, near_ref]
    scales = []
    for ref in blocks:
        scales.append(inverse_rms(ref[...].astype(F32)))
    wait_all(copies)
    gain_cols = weights[:, heads_width + 2 * head_dim :]
    pick = unit((8, LANES), iota((8, LANES), 0) == iota((8, LANES), 1))
    gains = dot_t(pick, gain_cols)
    spread = spread_matrix(head_dim, width, narrow_rows, wide_rows)
    small_gains = dot_t(gains.astype(BF16), spread)
    gains_ref[...] = gains
    small_gains_ref[...] = small_gains
    gain_an, gain_q, gain_k = gains[0:1], small_gains[4:5], small_gains[5:6]
    for index, ref in enumerate(blocks):
        normed = ref[...].astype(F32) * scales[index] * gain_an
        inside[index * rows : (index + 1) * rows, :] = normed.astype(BF16)
    attn_in_ref[...] = inside[2 * rows :, :]
    for index in range(3):
        span = slice(index * rows, (index + 1) * rows)
        part_in = inside[span, :]
        key_lin = dot(part_in, weights[:, heads_width : heads_width + head_dim])
        value = dot(part_in, weights[:, heads_width + head_dim : heads_width + 2 * head_dim])
        key = rotate(key_lin * inverse_rms(key_lin) * gain_k, cos_ref[span, :], sin_ref[span, :])
        keys_ref[span, :head_dim] = key.astype(BF16)
        keys_ref[span, head_dim:] = value.astype(BF16)
        if index == 2:
            key_lin_ref[...] = key_lin
    cosine, sine = cos_ref[2 * rows :, :], sin_ref[2 * rows :, :]
    column = iota((rows, 3 * rows), 1)
    seen = (column >= low_ref[...]) & (column <= iota((rows, 3 * rows), 0) + 2 * rows)
    for head in range(head_count):
        lanes = slice(head * head_dim, (head + 1) * head_dim)
        query_lin = dot(inside[2 * rows :, :], weights[:, lanes])
        query_lin_ref[:, lanes] = query_lin
        query = rotate(query_lin * inverse_rms(query_lin) * gain_q, cosine, sine).astype(BF16)
        query_ref[:, lanes] = query
        scores = jnp.where(seen, dot_t(query, keys_ref[:, :head_dim]) * score_scale, NEGATIVE)
        raised = jnp.exp(scores - jnp.max(scores, axis=-1, keepdims=True))
        probs = (raised / jnp.sum(raised, axis=-1, keepdims=True)).astype(BF16)
        probs_ref[head * rows : (head + 1) * rows, :] = probs
        attended_ref[:, lanes] = dot(probs, keys_ref[:, head_dim:]).astype(BF16)


def attend(place, tokens3, cosine, sine, lowest, parts, head_count, head_dim, narrow_rows, wide_rows):
    rows, width = tokens3[0].shape
    heads_width = head_count * head_dim
    pack = parts[0].shape[1]
    outs = [
        shape_of((rows, width), BF16),
        shape_of((rows, heads_width), F32),
        shape_of((rows, head_dim), F32),
        shape_of((rows, heads_width), BF16),
        shape_of((3 * rows, 2 * head_dim), BF16),
        shape_of((head_count * rows, 3 * rows), BF16),
        shape_of((rows, heads_width), BF16),
        shape_of((8, width), F32),
        shape_of((8, head_dim), F32),
    ]
    return call(
        functools.partial(attend_kernel, len(parts), narrow_rows, wide_rows, head_count),
        outs,
        [VMEM_SPEC] * len(outs),
        [place] + list(tokens3) + [cosine, sine, lowest] + parts,
        [SMEM_SPEC] + [VMEM_SPEC] * 6 + [ANY_SPEC] * len(parts),
        [
            pltpu.VMEM((width, pack), BF16),
            pltpu.VMEM((3 * rows, width), BF16),
            pltpu.SemaphoreType.DMA((len(parts),)),
        ],
        flops=2 * rows * width * (heads_width + 6 * head_dim) + 12 * rows * rows * heads_width,
        moved=2 * width * pack + 16 * rows * width,
        exps=3 * head_count * rows * rows,
    )


def post_kernel(part_count, place_ref, tokens_ref, attended_ref, gains_ref, *refs):
    parts = refs[:part_count]
    attn_out_ref, middle_ref, ffn_in_ref, weights, sems = refs[part_count:]
    copies = start_placing(parts, weights, sems, 0, place_ref[0])
    wait_all(copies)
    attn_out = dot_t(attended_ref[...], weights[...])
    attn_out_ref[...] = attn_out
    middle = tokens_ref[...].astype(F32) + attn_out * inverse_rms(attn_out) * gains_ref[1:2, :]
    middle_ref[...] = middle
    ffn_in_ref[...] = (middle * inverse_rms(middle) * gains_ref[2:3, :]).astype(BF16)


def post_attention(place, tokens, attended, gains, parts):
    rows, width = tokens.shape
    inner = attended.shape[1]
    return call(
        functools.partial(post_kernel, len(parts)),
        [shape_of((rows, width), F32), shape_of((rows, width), F32), shape_of((rows, width), BF16)],
        [VMEM_SPEC] * 3,
        [place, tokens, attended, gains] + parts,
        [SMEM_SPEC] + [VMEM_SPEC] * 3 + [ANY_SPEC] * len(parts),
        [pltpu.VMEM((width, inner), BF16), pltpu.SemaphoreType.DMA((len(parts),))],
        flops=2 * rows * width * inner,
        moved=2 * width * inner + 14 * rows * width,
    )


def gelu_pair(gate):
    square = gate * gate
    tanh = jnp.tanh(gate * (0.7978845608028654 + 0.035677408136300125 * square))
    half = 0.5 + 0.5 * tanh
    value = gate * half
    slope = half + value * (1.0 - tanh) * (0.7978845608028654 + 0.10703222440890037 * square)
    return value, slope


def gate_up_kernel(part_count, place_ref, *refs):
    blocks, refs = refs[:4], refs[4:]
    gate_parts, up_parts = refs[:part_count], refs[part_count : 2 * part_count]
    act_ref, gate_slope_ref, up_slope_ref, held, gate_w, up_w, sems = refs[2 * part_count :]
    step = pl.program_id(0)

    @pl.when(step == 0)
    def _():
        copies = start_placing(gate_parts, gate_w, sems, 0, place_ref[0])
        copies += start_placing(up_parts, up_w, sems, part_count, place_ref[0])
        wait_all(copies)

    for index, block in enumerate(blocks):

        @pl.when(step == index)
        def _(block=block):
            held[...] = block[...]

    rows_in = held[...]
    for start, size in tiles_of(gate_w.shape[1], 256):
        lanes = slice(start, start + size)
        gate = dot(rows_in, gate_w[:, lanes])
        up = dot(rows_in, up_w[:, lanes])
        value, slope = gelu_pair(gate)
        act_ref[:, lanes] = (value * up).astype(BF16)
        gate_slope_ref[:, lanes] = (slope * up).astype(BF16)
        up_slope_ref[:, lanes] = value.astype(BF16)


def gate_up(place, blocks, gate_parts, up_parts):
    rows, width = blocks[0].shape
    hidden = gate_parts[0].shape[1]
    count = len(gate_parts)
    out = shape_of((4 * rows, hidden), BF16)
    return pl.pallas_call(
        functools.partial(gate_up_kernel, count),
        out_shape=(out,) * 3,
        grid=(4,),
        in_specs=[SMEM_SPEC]
        + [pl.BlockSpec((rows, width), lambda step: (0, 0))] * 4
        + [ANY_SPEC] * (2 * count),
        out_specs=(pl.BlockSpec((rows, hidden), lambda step: (step, 0)),) * 3,
        scratch_shapes=[
            pltpu.VMEM((rows, width), BF16),
            pltpu.VMEM((width, hidden), BF16),
            pltpu.VMEM((width, hidden), BF16),
            pltpu.SemaphoreType.DMA((2 * count,)),
        ],
        compiler_params=pltpu.CompilerParams(vmem_limit_bytes=VMEM_LIMIT),
        cost_estimate=pl.CostEstimate(
            flops=16 * rows * width * hidden,
            bytes_accessed=4 * width * hidden + 24 * rows * hidden,
            transcendentals=4 * rows * hidden,
        ),
    )(place, *blocks, *gate_parts, *up_parts)


def down_kernel(part_count, first, span, place_ref, act_ref, *refs):
    parts = refs[:part_count]
    outs = refs[part_count : part_count + span]
    held, weights, sems, act_sem = refs[part_count + span :]
    rows = outs[0].shape[0]
    fetch = pltpu.make_async_copy(
        act_ref.at[pl.ds(first * rows, span * rows), :], held, act_sem.at[0]
    )
    fetch.start()
    wait_all(start_placing(parts, weights, sems, 0, place_ref[0]))
    fetch.wait()
    for index, out in enumerate(outs):
        for start, size in tiles_of(weights.shape[0], 384):
            out[:, start : start + size] = dot_t(
                held[index * rows : (index + 1) * rows, :], weights[start : start + size, :]
            ).astype(BF16)


def down(place, act, first, span, parts):
    rows, hidden = act.shape[0] // 4, act.shape[1]
    width = parts[0].shape[0] * len(parts)
    return call(
        functools.partial(down_kernel, len(parts), first, span),
        [shape_of((rows, width), BF16)] * span,
        [VMEM_SPEC] * span,
        [place, act] + parts,
        [SMEM_SPEC, ANY_SPEC] + [ANY_SPEC] * len(parts),
        [
            pltpu.VMEM((span * rows, hidden), BF16),
            pltpu.VMEM((width, hidden), BF16),
            pltpu.SemaphoreType.DMA((len(parts),)),
            pltpu.SemaphoreType.DMA((1,)),
        ],
        flops=2 * span * rows * hidden * width,
        moved=2 * width * hidden + 2 * span * rows * (width + hidden),
    )


def turn_kernel(
    own_ref, far_ref, across_ref, along_ref, middle_ref, upstream_ref, gains_ref, *outs
):
    output_ref, back_ref, gain_grad_ref = outs
    total = own_ref[...].astype(F32) + far_ref[...].astype(F32)
    total = total + across_ref[...].astype(F32) + along_ref[...].astype(F32)
    scale = inverse_rms(total)
    normed = total * scale
    gain = gains_ref[3:4, :]
    output_ref[...] = (middle_ref[...] + normed * gain).astype(BF16)
    back, gain_grad = norm_back(normed, scale, gain, upstream_ref[...].astype(F32))
    back_ref[...] = back.astype(BF16)
    gain_grad_ref[...] = gain_grad


def turn(sums, middle, upstream, gains):
    rows, width = middle.shape
    return call(
        turn_kernel,
        [shape_of((rows, width), BF16), shape_of((rows, width), BF16), shape_of((1, width), F32)],
        [VMEM_SPEC] * 3,
        list(sums) + [middle, upstream, gains],
        [VMEM_SPEC] * 7,
        moved=20 * rows * width,
    )


def ffn_back_kernel(part_count, first, span, place_ref, *refs):
    backs, refs = refs[:span], refs[span:]
    gate_slope_ref, up_slope_ref = refs[:2]
    refs = refs[2:]
    down_parts, gate_parts, up_parts = [
        refs[index * part_count : (index + 1) * part_count] for index in range(3)
    ]
    refs = refs[3 * part_count :]
    outs, refs = refs[:span], refs[span:]
    d_gate_ref, d_up_ref, gate_slope, up_slope, down_w, gate_w, up_w, sems, slope_sems = refs
    rows = outs[0].shape[0]
    seq = place_ref[0]
    copies = start_placing(down_parts, down_w, sems, 0, seq)
    fetches = [
        pltpu.make_async_copy(
            source.at[pl.ds(first * rows, span * rows), :], dest, slope_sems.at[index]
        )
        for index, (source, dest) in enumerate(
            [(gate_slope_ref, gate_slope), (up_slope_ref, up_slope)]
        )
    ]
    for fetch in fetches:
        fetch.start()
    later = start_placing(gate_parts, gate_w, sems, part_count, seq)
    later += start_placing(up_parts, up_w, sems, 2 * part_count, seq)
    wait_all(copies)
    wait_all(fetches)
    for index in range(span):
        part = slice(index * rows, (index + 1) * rows)
        for start, size in tiles_of(down_w.shape[1], 256):
            lanes = slice(start, start + size)
            d_act = dot(backs[index][...], down_w[:, lanes])
            d_gate_ref[part, lanes] = (d_act * gate_slope[part, lanes].astype(F32)).astype(BF16)
            d_up_ref[part, lanes] = (d_act * up_slope[part, lanes].astype(F32)).astype(BF16)
    wait_all(later)
    for index in range(span):
        part = slice(index * rows, (index + 1) * rows)
        for start, size in tiles_of(gate_w.shape[0], 384):
            lanes = slice(start, start + size)
            total = dot_t(d_gate_ref[part, :], gate_w[lanes, :])
            total = total + dot_t(d_up_ref[part, :], up_w[lanes, :])
            outs[index][:, lanes] = total.astype(BF16)


def ffn_back(place, backs, first, gate_slope, up_slope, down_parts, gate_parts, up_parts):
    span = len(backs)
    rows, width = backs[0].shape
    hidden = gate_slope.shape[1]
    count = len(down_parts)
    hidden_out = shape_of((span * rows, hidden), BF16)
    return call(
        functools.partial(ffn_back_kernel, count, first, span),
        [shape_of((rows, width), BF16)] * span + [hidden_out] * 2,
        [VMEM_SPEC] * (span + 2),
        [place] + list(backs) + [gate_slope, up_slope] + down_parts + gate_parts + up_parts,
        [SMEM_SPEC] + [VMEM_SPEC] * span + [ANY_SPEC] * (2 + 3 * count),
        [
            pltpu.VMEM((span * rows, hidden), BF16),
            pltpu.VMEM((span * rows, hidden), BF16),
            pltpu.VMEM((width, hidden), BF16),
            pltpu.VMEM((width, hidden), BF16),
            pltpu.VMEM((width, hidden), BF16),
            pltpu.SemaphoreType.DMA((3 * count,)),
            pltpu.SemaphoreType.DMA((2,)),
        ],
        flops=6 * span * rows * hidden * width,
        moved=6 * width * hidden + 12 * span * rows * hidden,
    )


def weight_grad_kernel(left_count, right_count, place_ref, *refs):
    lefts, rights = refs[:left_count], refs[left_count : left_count + right_count]
    refs = refs[left_count + right_count :]
    outs, (left, right, whole, sems) = refs[:-4], refs[-4:]
    copies = []
    for pieces, dest in ((lefts, left), (rights, right)):
        start = 0
        for piece in pieces:
            size = piece.shape[0]
            copies.append(
                pltpu.make_async_copy(piece, dest.at[pl.ds(start, size), :], sems.at[len(copies)])
            )
            start += size
    for copy in copies:
        copy.start()
    wait_all(copies)
    for start, size in tiles_of(right.shape[1], 256):
        lanes = slice(start, start + size)
        whole[:, lanes] = dot_tn(left[...], right[:, lanes]).astype(BF16)
    wait_all(start_cutting(whole, outs, sems, 0, place_ref[0]))


def weight_grad(place, lefts, rights):
    height, width = lefts[0].shape[1], rights[0].shape[1]
    rows = sum(piece.shape[0] for piece in lefts)
    count = lax.axis_size("seq")
    outs = cut_shapes(height, width, count)
    return call(
        functools.partial(weight_grad_kernel, len(lefts), len(rights)),
        outs,
        [ANY_SPEC] * len(outs),
        [place] + list(lefts) + list(rights),
        [SMEM_SPEC] + [ANY_SPEC] * (len(lefts) + len(rights)),
        [
            pltpu.VMEM((rows, height), BF16),
            pltpu.VMEM((rows, width), BF16),
            pltpu.VMEM((height, width), BF16),
            pltpu.SemaphoreType.DMA((max(count, len(lefts) + len(rights)),)),
        ],
        flops=2 * rows * height * width,
        moved=2 * (rows * (height + width) + height * width),
    )


def attend_back_kernel(
    part_count,
    first_count,
    out_count,
    head_count,
    place_ref,
    own_ref,
    far_ref,
    across_ref,
    along_ref,
    middle_ref,
    upstream_ref,
    attn_out_ref,
    gains_ref,
    small_gains_ref,
    attended_ref,
    attn_in_ref,
    query_lin_ref,
    query_ref,
    keys_ref,
    probs_ref,
    cos_ref,
    sin_ref,
    *refs,
):
    out_parts, refs = refs[:part_count], refs[part_count:]
    first_parts, refs = refs[:first_count], refs[first_count:]
    grads, refs = refs[:out_count], refs[out_count:]
    d_middle_ref, d_in_ref, far_halo_ref, back_halo_ref, near_ref, rows_ref, query_gain_ref = refs[:7]
    out_w, first_w, whole, d_query, d_keys, sems = refs[7:]
    rows, width = middle_ref.shape
    head_dim = keys_ref.shape[1] // 2
    heads_width = head_count * head_dim
    score_scale = head_dim**-0.5
    seq = place_ref[0]
    copies = start_placing(out_parts, out_w, sems, 0, seq)
    later = start_placing(first_parts, first_w, sems, part_count, seq)
    total = own_ref[...].astype(F32) + far_ref[...].astype(F32)
    total = total + across_ref[...].astype(F32) + along_ref[...].astype(F32)
    middle = middle_ref[...]
    scale = inverse_rms(middle)
    back, grad_fn = norm_back(middle * scale, scale, gains_ref[2:3, :], total)
    d_middle = upstream_ref[...].astype(F32) + back
    d_middle_ref[...] = d_middle
    attn_out = attn_out_ref[...]
    scale = inverse_rms(attn_out)
    d_attn_out, grad_ap = norm_back(attn_out * scale, scale, gains_ref[1:2, :], d_middle)
    row = iota((8, width), 0)
    rows_ref[...] = jnp.where(row == 1, grad_ap, 0.0) + jnp.where(row == 2, grad_fn, 0.0)
    d_attn_low = d_attn_out.astype(BF16)
    for start, size in tiles_of(heads_width, 256):
        lanes = slice(start, start + size)
        whole[:, start : start + size] = dot_tn(d_attn_low, attended_ref[:, lanes]).astype(BF16)
    wait_all(copies)
    cosine, sine = cos_ref[2 * rows :, :], sin_ref[2 * rows :, :]
    gain_q = small_gains_ref[4:5, :]
    query_gain = jnp.zeros((1, head_dim), F32)
    for head in range(head_count):
        lanes = slice(head * head_dim, (head + 1) * head_dim)
        d_attended = dot(d_attn_low, out_w[:, lanes]).astype(BF16)
        probs_low = probs_ref[head * rows : (head + 1) * rows, :]
        probs = probs_low.astype(F32)
        d_probs = dot_t(d_attended, keys_ref[:, head_dim:])
        delta = jnp.sum(probs * d_probs, axis=-1, keepdims=True)
        d_scores = (probs * (d_probs - delta) * score_scale).astype(BF16)
        d_rotated = dot(d_scores, keys_ref[:, :head_dim])
        d_key = dot_tn(d_scores, query_ref[:, lanes])
        d_value = dot_tn(probs_low, d_attended)
        if head == 0:
            d_keys[:, :head_dim] = d_key
            d_keys[:, head_dim:] = d_value
        else:
            d_keys[:, :head_dim] += d_key
            d_keys[:, head_dim:] += d_value
        query_lin = query_lin_ref[:, lanes]
        scale = inverse_rms(query_lin)
        d_normed = rotate(d_rotated, cosine, -sine)
        back, gain_grad = norm_back(query_lin * scale, scale, gain_q, d_normed)
        query_gain = query_gain + gain_grad
        d_query[:, lanes] = back.astype(BF16)
    query_gain_ref[...] = query_gain
    far_halo_ref[...] = d_keys[:rows, :].astype(BF16)
    back_halo_ref[...] = d_keys[rows : 2 * rows, :].astype(BF16)
    near_ref[...] = d_keys[2 * rows :, :]
    for start, size in tiles_of(heads_width, 256):
        lanes = slice(start, start + size)
        whole[:, heads_width + start : heads_width + start + size] = dot_tn(
            attn_in_ref[...], d_query[:, lanes]
        ).astype(BF16)
    cuts = start_cutting(whole, grads, sems, part_count + first_count, seq)
    wait_all(later)
    for start, size in tiles_of(width, 384):
        lanes = slice(start, start + size)
        d_in_ref[:, lanes] = dot_t(d_query[...], first_w[lanes, :heads_width])
    wait_all(cuts)


def attend_back(place, sums, saved, cosine, sine, out_parts, first_parts, head_count):
    middle, upstream, attn_out, gains, small_gains, attended, attn_in, query_lin, query, keys, probs = saved
    rows, width = middle.shape
    head_dim = keys.shape[1] // 2
    heads_width = head_count * head_dim
    count = lax.axis_size("seq")
    cuts = cut_shapes(width, 2 * heads_width, count)
    outs = cuts + [
        shape_of((rows, width), F32),
        shape_of((rows, width), F32),
        shape_of((rows, 2 * head_dim), BF16),
        shape_of((rows, 2 * head_dim), BF16),
        shape_of((rows, 2 * head_dim), F32),
        shape_of((8, width), F32),
        shape_of((1, head_dim), F32),
    ]
    ins = [place] + list(sums) + list(saved) + [cosine, sine] + out_parts + first_parts
    return call(
        functools.partial(
            attend_back_kernel, len(out_parts), len(first_parts), len(cuts), head_count
        ),
        outs,
        [ANY_SPEC] * len(cuts) + [VMEM_SPEC] * 7,
        ins,
        [SMEM_SPEC] + [VMEM_SPEC] * 17 + [ANY_SPEC] * (len(out_parts) + len(first_parts)),
        [
            pltpu.VMEM((width, heads_width), BF16),
            pltpu.VMEM((width, first_parts[0].shape[1]), BF16),
            pltpu.VMEM((width, 2 * heads_width), BF16),
            pltpu.VMEM((rows, heads_width), BF16),
            pltpu.VMEM((3 * rows, 2 * head_dim), F32),
            pltpu.SemaphoreType.DMA((len(out_parts) + len(first_parts) + count,)),
        ],
        flops=8 * rows * width * heads_width + 30 * rows * rows * heads_width,
        moved=12 * width * heads_width + 30 * rows * width,
    )


def finish_kernel(
    first_count,
    out_count,
    narrow_rows,
    wide_rows,
    place_ref,
    near_ref,
    back_ref,
    far_ref,
    key_lin_ref,
    small_gains_ref,
    gains_ref,
    cos_ref,
    sin_ref,
    attn_in_ref,
    tokens_ref,
    d_middle_ref,
    d_in_ref,
    rows_ref,
    ffn_post_ref,
    query_gain_ref,
    *refs,
):
    first_parts, refs = refs[:first_count], refs[first_count:]
    grads, (input_grad_ref, first_w, whole, d_low, sems) = refs[:out_count], refs[out_count:]
    rows, width = tokens_ref.shape
    head_dim = key_lin_ref.shape[1]
    seq = place_ref[0]
    copies = start_placing(first_parts, first_w, sems, 0, seq)
    d_keys = near_ref[...] + back_ref[...].astype(F32) + far_ref[...].astype(F32)
    key_lin = key_lin_ref[...]
    scale = inverse_rms(key_lin)
    d_normed = rotate(d_keys[:, :head_dim], cos_ref[2 * rows :, :], -sin_ref[2 * rows :, :])
    back, key_gain = norm_back(key_lin * scale, scale, small_gains_ref[5:6, :], d_normed)
    d_low[:, :head_dim] = back.astype(BF16)
    d_low[:, head_dim:] = d_keys[:, head_dim:].astype(BF16)
    whole[:, : 2 * head_dim] = dot_tn(attn_in_ref[...], d_low[...]).astype(BF16)
    wait_all(copies)
    heads_width = first_w.shape[1] - 2 * head_dim - LANES
    d_attn_in = d_in_ref[...] + dot_t(
        d_low[...], first_w[:, heads_width : heads_width + 2 * head_dim]
    )
    inputs = tokens_ref[...].astype(F32)
    scale = inverse_rms(inputs)
    back, grad_an = norm_back(inputs * scale, scale, gains_ref[0:1, :], d_attn_in)
    input_grad_ref[...] = d_middle_ref[...] + back
    row = iota((8, width), 0)
    gain_rows = rows_ref[...] + jnp.where(row == 0, grad_an, 0.0)
    gain_rows = gain_rows + jnp.where(row == 3, ffn_post_ref[...], 0.0)
    small_row = iota((8, head_dim), 0)
    small = jnp.where(small_row == 4, query_gain_ref[...], 0.0)
    small = small + jnp.where(small_row == 5, key_gain, 0.0)
    spread = spread_matrix(head_dim, width, narrow_rows, wide_rows)
    gain_rows = gain_rows + dot(small.astype(BF16), spread)
    pick = unit((8, LANES), iota((8, LANES), 0) == iota((8, LANES), 1))
    whole[:, 2 * head_dim :] = dot_tn(gain_rows.astype(BF16), pick).astype(BF16)
    wait_all(start_cutting(whole, grads, sems, first_count, seq))


def finish(place, ins, parts, narrow_rows, wide_rows):
    tokens, key_lin, first_parts = ins[9], ins[3], parts
    rows, width = tokens.shape
    head_dim = key_lin.shape[1]
    count = lax.axis_size("seq")
    pack = 2 * head_dim + LANES
    cuts = cut_shapes(width, pack, count)
    return call(
        functools.partial(finish_kernel, len(parts), len(cuts), narrow_rows, wide_rows),
        cuts + [shape_of((rows, width), F32)],
        [ANY_SPEC] * len(cuts) + [VMEM_SPEC],
        [place] + list(ins) + first_parts,
        [SMEM_SPEC] + [VMEM_SPEC] * len(ins) + [ANY_SPEC] * len(parts),
        [
            pltpu.VMEM((width, first_parts[0].shape[1]), BF16),
            pltpu.VMEM((width, pack), BF16),
            pltpu.VMEM((rows, 2 * head_dim), BF16),
            pltpu.SemaphoreType.DMA((len(parts) + count,)),
        ],
        flops=8 * rows * width * head_dim,
        moved=4 * width * pack + 20 * rows * width,
    )


def layout(lengths, counts, first_slot, row_count):
    starts = jnp.cumsum(lengths) - lengths
    slot_index = first_slot + jnp.arange(row_count, dtype=jnp.int32)
    member = (slot_index[:, None] >= starts[None, :]).astype(jnp.int32)
    document = jnp.sum(member, axis=1) - 1
    onehot = (document[:, None] == jnp.arange(lengths.shape[0], dtype=jnp.int32)[None, :]).astype(
        jnp.int32
    )
    position = slot_index - jnp.sum(onehot * starts[None, :], axis=1)
    padded = jnp.sum(onehot * (lengths - counts)[None, :], axis=1)
    return (position, padded)


def on_device(
    tokens,
    cotangent,
    doc_lengths,
    true_counts,
    w_query,
    w_key,
    w_value,
    w_out,
    w_gate,
    w_up,
    w_down,
    attn_norm_gain,
    query_gain,
    key_gain,
    attn_post_gain,
    ffn_norm_gain,
    ffn_post_gain,
):
    row_count = tokens.shape[1]
    head_dim = w_key.shape[1]
    heads_width = w_query.shape[1]
    head_count = heads_width // head_dim
    seq_index, plane_index = lax.axis_index("seq"), lax.axis_index("fsdp")
    place = jnp.stack([seq_index, plane_index]).astype(jnp.int32)
    inputs, upstream = tokens[0], cotangent[0]
    wide_rows, narrow_rows = attn_norm_gain.shape[0], query_gain.shape[0]

    first_pack = pack_first(
        w_query,
        w_key,
        w_value,
        [attn_norm_gain, attn_post_gain, ffn_norm_gain, ffn_post_gain],
        [query_gain, key_gain],
    )
    first_parts = gather_attn(gather_planes(first_pack, place))
    out_parts = gather_attn(gather_planes(w_out, place))
    gate_parts = gather_ffn(w_gate)
    up_parts = gather_ffn(w_up)
    down_parts = gather_ffn(w_down)

    tokens3 = [from_behind(inputs, 2), from_behind(inputs, 1), inputs]
    first_slot = seq_index * row_count
    position, padded = layout(
        doc_lengths[0], true_counts[0], first_slot - WINDOW, row_count + WINDOW
    )
    frequency = ROPE_BASE ** (-2.0 * jnp.arange(head_dim // 2, dtype=F32) / head_dim)
    angles = position.astype(F32)[:, None] * frequency
    cosine, sine = jnp.cos(angles), jnp.sin(angles)
    reach = jnp.clip(position[WINDOW:] - padded[WINDOW:], 0, WINDOW - 1)
    lowest = (WINDOW + jnp.arange(row_count, dtype=jnp.int32) - reach)[:, None]

    attn_in, query_lin, key_lin, query, keys, probs, attended, gains, small_gains = attend(
        place,
        [tokens3[2], tokens3[1], tokens3[0]],
        cosine,
        sine,
        lowest,
        first_parts,
        head_count,
        head_dim,
        narrow_rows,
        wide_rows,
    )
    attn_out, middle, ffn_in = post_attention(place, inputs, attended, gains, out_parts)
    blocks = group_blocks(ffn_in)
    act, gate_slope, up_slope = gate_up(place, blocks, gate_parts, up_parts)
    (far,) = down(place, act, 0, 1, down_parts)
    far = diagonal(far)
    across, along = down(place, act, 1, 2, down_parts)
    across, along = swap(across, "seq", 2), swap(along, "fsdp", 1)
    (own,) = down(place, act, 3, 1, down_parts)
    output, d_ffn_low, grad_fp = turn([own, far, across, along], middle, upstream, gains)
    backs = group_blocks(d_ffn_low)
    slopes = (gate_slope, up_slope, down_parts, gate_parts, up_parts)
    far, far_gate, far_up = ffn_back(place, backs[:1], 0, *slopes)
    far = diagonal(far)
    across, along, side_gate, side_up = ffn_back(place, backs[1:3], 1, *slopes)
    across, along = swap(across, "seq", 2), swap(along, "fsdp", 1)
    own, own_gate, own_up = ffn_back(place, backs[3:], 3, *slopes)
    grad_down = scatter_ffn(weight_grad(place, backs, [act]))
    grad_gate = scatter_ffn(weight_grad(place, blocks, [far_gate, side_gate, own_gate]))
    grad_up = scatter_ffn(weight_grad(place, blocks, [far_up, side_up, own_up]))
    saved = (
        middle,
        upstream,
        attn_out,
        gains,
        small_gains,
        attended,
        attn_in,
        query_lin,
        query,
        keys,
        probs,
    )
    *head_grads, d_middle, d_in, far_halo, back_halo, near, gain_rows, query_gain_grad = attend_back(
        place, [own, far, across, along], saved, cosine, sine, out_parts, first_parts, head_count
    )
    head_rows = scatter_attn(head_grads)
    ins = [
        near,
        from_behind(back_halo, -1),
        from_behind(far_halo, -2),
        key_lin,
        small_gains,
        gains,
        cosine,
        sine,
        attn_in,
        inputs,
        d_middle,
        d_in,
        gain_rows,
        grad_fp,
        query_gain_grad,
    ]
    *last_grads, input_grad = finish(place, ins, first_parts, narrow_rows, wide_rows)
    last_rows = scatter_attn(last_grads)
    gain_cols = last_rows[:, 2 * head_dim :]
    return (
        output[None],
        input_grad[None],
        head_rows[:, heads_width:],
        last_rows[:, :head_dim],
        last_rows[:, head_dim : 2 * head_dim],
        head_rows[:, :heads_width],
        grad_gate,
        grad_up,
        grad_down,
        gain_cols[:, 0],
        gain_cols[:narrow_rows, 4],
        gain_cols[:narrow_rows, 5],
        gain_cols[:, 1],
        gain_cols[:, 2],
        gain_cols[:, 3],
    )


def solution(mesh):
    rows = P("fsdp", "seq", None)
    shard, tile, vector = P(("seq", "fsdp"), None), P("seq", "fsdp"), P(("seq", "fsdp"))
    groups = P("fsdp", None)
    return jax.shard_map(
        on_device,
        mesh=mesh,
        in_specs=(rows, rows, groups, groups) + (shard,) * 4 + (tile,) * 3 + (vector,) * 6,
        out_specs=(rows, rows) + (shard,) * 4 + (tile,) * 3 + (vector,) * 6,
        check_vma=False,
    )
```

```python
import functools

import jax
import jax.numpy as jnp
from jax import lax
from jax.experimental import pallas as pl
from jax.experimental.pallas import tpu as pltpu
from jax.sharding import PartitionSpec as P

WINDOW = 512
NORM_EPS = 1e-06
ROPE_BASE = 10000.0
NEGATIVE = -1e30
LANES = 128
VMEM_LIMIT = 56 * 2**20
BF16 = jnp.bfloat16
F32 = jnp.float32


def from_behind(value, steps):
    count = lax.axis_size("seq")
    first, last = (max(0, -steps), min(count, count - steps))
    return lax.ppermute(value, "seq", [(source, source + steps) for source in range(first, last)])


def seq_masks():
    return [1 << bit for bit in range(lax.axis_size("seq").bit_length() - 1)]


def swap(value, axis, mask):
    count = lax.axis_size(axis)
    return lax.ppermute(value, axis, [(source, source ^ mask) for source in range(count)])


def shift(value, axis, steps):
    count = lax.axis_size(axis)
    return lax.ppermute(value, axis, [(source, (source + steps) % count) for source in range(count)])


def diagonal(value):
    seqs, planes = lax.axis_size("seq"), lax.axis_size("fsdp")
    pairs = [
        (seq * planes + plane, (seq ^ 2) * planes + (plane ^ 1))
        for seq in range(seqs)
        for plane in range(planes)
    ]
    return lax.ppermute(value, ("seq", "fsdp"), pairs)


def group_blocks(rows):
    return [diagonal(rows), swap(rows, "seq", 2), swap(rows, "fsdp", 1), rows]


def on_own_slice():
    return (lax.axis_index("seq") // 2) % 2 == lax.axis_index("fsdp") // 2


def ordered(parts):
    parts = [parts[rel] for rel in range(len(parts))]
    if parts[0].shape[0] % 16 == 0:
        return parts
    index = jnp.arange(len(parts), dtype=jnp.int32) ^ lax.axis_index("seq")
    whole = jnp.take(jnp.stack(parts), index, axis=0, mode="clip")
    return [whole.reshape(-1, whole.shape[-1])]


def after(value, *earlier):
    return lax.optimization_barrier((value,) + earlier)[0]


def gather_far(block):
    parts = {0: block}
    for mask in [mask for mask in seq_masks() if mask > 2] + [2]:
        parts.update({rel ^ mask: swap(part, "seq", mask) for rel, part in parts.items()})
    return parts


def gather_core(parts):
    parts = dict(parts)
    parts.update({rel ^ 1: swap(part, "seq", 1) for rel, part in parts.items()})
    return ordered(parts)


def pick_slices(block, other_plane):
    own = on_own_slice()
    return jnp.where(own, block, other_plane), jnp.where(own, other_plane, block)


def spread_far(parts):
    parts = dict(parts)
    for mask in [mask for mask in seq_masks() if mask > 2]:
        parts.update({rel ^ mask: swap(part, "seq", mask) for rel, part in parts.items()})
    return parts


def add_rounded(first, second):
    return (first.astype(F32) + second.astype(F32)).astype(BF16)


def cut(pair, count):
    if len(pair) == 2:
        return pair
    index = jnp.arange(count, dtype=jnp.int32) ^ lax.axis_index("seq")
    blocks = jnp.take(pair[0].reshape(count, -1, pair[0].shape[-1]), index, axis=0, mode="clip")
    return blocks[0::2], blocks[1::2]


def merge_cores(pair):
    keep, send = cut(pair, lax.axis_size("seq"))
    return add_rounded(keep, swap(send, "seq", 1))


def merge_column(part, which, *earlier):
    part = part.reshape((-1, 2) + part.shape[1:])[:, which]
    got = None
    for mask in [mask for mask in seq_masks() if mask > 2][::-1]:
        half = part.shape[0] // 2
        leaving = part[half:]
        if got is None and earlier:
            leaving = after(leaving, *earlier)
        got = swap(leaving, "seq", mask)
        part = add_rounded(part[:half], got)
    return part[0], got


def merge_planes(near, crossed, *earlier):
    own = on_own_slice()
    stays = jnp.where(own, near, crossed)
    leaves = jnp.where(own, crossed, near)
    if earlier:
        leaves = after(leaves, *earlier)
    got = swap(leaves, "fsdp", 2)
    return stays.astype(F32) + got.astype(F32), got


def scatter_attn(pair):
    part = merge_cores(pair)
    half = part.shape[0] // 2
    part = part.reshape((half, 2) + part.shape[1:])
    part = add_rounded(part[:, 0], swap(part[:, 1], "seq", 2))
    for mask in [mask for mask in seq_masks() if mask > 2][::-1]:
        half = part.shape[0] // 2
        part = add_rounded(part[:half], swap(part[half:], "seq", mask))
    rows = part[0]
    planes = lax.axis_size("fsdp")
    blocks = rows.reshape((planes, -1) + rows.shape[1:])
    mine = lax.axis_index("fsdp")
    total = lax.dynamic_index_in_dim(blocks, mine, 0, keepdims=False).astype(F32)
    for steps in range(1, planes):
        send = lax.dynamic_index_in_dim(blocks, (mine + steps) % planes, 0, keepdims=False)
        total = total + shift(send, "fsdp", steps).astype(F32)
    return total


def dot(left, right):
    return jnp.dot(left, right, preferred_element_type=F32)


def dot_t(left, right):
    return lax.dot_general(left, right, (((1,), (1,)), ((), ())), preferred_element_type=F32)


def dot_tn(left, right):
    return lax.dot_general(left, right, (((0,), (0,)), ((), ())), preferred_element_type=F32)


def inverse_rms(values):
    return lax.rsqrt(jnp.mean(values * values, axis=-1, keepdims=True) + NORM_EPS)


def norm_back(normed, scale, gain, upstream):
    scaled = upstream * gain
    back = scale * (scaled - normed * jnp.mean(scaled * normed, axis=-1, keepdims=True))
    return back, jnp.sum(upstream * normed, axis=0, keepdims=True)


def rotate(values, cosine, sine):
    half = values.shape[-1] // 2
    first, second = values[:, :half], values[:, half:]
    return jnp.concatenate(
        [first * cosine - second * sine, second * cosine + first * sine], axis=-1
    )


def iota(shape, dim):
    return lax.broadcasted_iota(jnp.int32, shape, dim)


def unit(shape, hits):
    return jnp.where(hits, 1.0, 0.0).astype(BF16)


def spread_matrix(narrow, wide, narrow_rows, wide_rows):
    row, col = iota((narrow, wide), 0), iota((narrow, wide), 1)
    return unit((narrow, wide), col == (row // narrow_rows) * wide_rows + row % narrow_rows)


def tiles_of(width, step):
    return [(start, min(step, width - start)) for start in range(0, width, step)]


def parts_width(part, head_dim):
    return (part.shape[1] - 2 * head_dim - LANES) // 2


def start_placing(parts, dest, sems, base, seq, lane=0, lanes=None):
    rows = parts[0].shape[0]
    copies = []
    for rel, part in enumerate(parts):
        start = pl.multiple_of((seq ^ rel) * rows, 16) if len(parts) > 1 else 0
        if lanes is not None:
            part = part.at[:, pl.ds(lane, lanes)]
        copies.append(
            pltpu.make_async_copy(part, dest.at[pl.ds(start, rows), :], sems.at[base + rel])
        )
    for copy in copies:
        copy.start()
    return copies


def start_cutting(whole, outs, sems, base, seq):
    if len(outs) == 1:
        copies = [pltpu.make_async_copy(whole, outs[0], sems.at[base])]
    else:
        half, rows = outs[0].shape[0], outs[0].shape[1]
        copies = []
        for rel in range(2 * half):
            start = pl.multiple_of((seq ^ rel) * rows, 16)
            copies.append(
                pltpu.make_async_copy(
                    whole.at[pl.ds(start, rows), :], outs[rel % 2].at[rel // 2], sems.at[base + rel]
                )
            )
    for copy in copies:
        copy.start()
    return copies


def cut_shapes(height, width, count):
    rows = height // count
    if rows % 16:
        return [jax.ShapeDtypeStruct((height, width), BF16)]
    return [jax.ShapeDtypeStruct((count // 2, rows, width), BF16)] * 2


def wait_all(copies):
    for copy in copies:
        copy.wait()


SMEM_SPEC = pl.BlockSpec(memory_space=pltpu.SMEM)
VMEM_SPEC = pl.BlockSpec(memory_space=pltpu.VMEM)
ANY_SPEC = pl.BlockSpec(memory_space=pl.ANY)


def call(kernel, outs, out_specs, ins, in_specs, scratch=(), flops=0, moved=0, exps=0):
    return pl.pallas_call(
        kernel,
        out_shape=tuple(outs),
        in_specs=list(in_specs),
        out_specs=tuple(out_specs),
        scratch_shapes=list(scratch),
        compiler_params=pltpu.CompilerParams(vmem_limit_bytes=VMEM_LIMIT),
        cost_estimate=pl.CostEstimate(flops=flops, bytes_accessed=moved, transcendentals=exps),
    )(*ins)


def shape_of(dims, dtype):
    return jax.ShapeDtypeStruct(dims, dtype)


def pack_kernel(wq_ref, wk_ref, wv_ref, wo_ref, *refs):
    wide, narrow, out_ref = refs[:4], refs[4:6], refs[6]
    rows, heads_width, head_dim = wq_ref.shape[0], wq_ref.shape[1], wk_ref.shape[1]
    out_ref[:, :heads_width] = wq_ref[...]
    out_ref[:, heads_width : heads_width + head_dim] = wk_ref[...]
    out_ref[:, heads_width + head_dim : heads_width + 2 * head_dim] = wv_ref[...]
    row = iota((16, rows), 0)
    held = jnp.zeros((16, rows), F32)
    for index, ref in enumerate(wide):
        held = held + jnp.where(row == index, ref[...].astype(F32), 0.0)
    small = narrow[0].shape[1]
    fit = unit((small, rows), iota((small, rows), 0) == iota((small, rows), 1))
    for index, ref in enumerate(narrow):
        spread = dot(jnp.broadcast_to(ref[...].astype(F32), (16, small)).astype(BF16), fit)
        held = held + jnp.where(row == 4 + index, spread, 0.0)
    place = unit((16, LANES), iota((16, LANES), 0) == iota((16, LANES), 1))
    gain_start = heads_width + 2 * head_dim
    out_ref[:, gain_start : gain_start + LANES] = dot_tn(held.astype(BF16), place).astype(BF16)
    out_ref[:, gain_start + LANES :] = wo_ref[...]


def pack_attn(w_query, w_key, w_value, w_out, wide, narrow):
    rows = w_query.shape[0]
    width = 2 * w_query.shape[1] + 2 * w_key.shape[1] + LANES
    ins = [w_query, w_key, w_value, w_out] + [vec.reshape(1, -1) for vec in wide + narrow]
    return call(
        pack_kernel,
        [shape_of((rows, width), BF16)],
        [VMEM_SPEC],
        ins,
        [VMEM_SPEC] * len(ins),
    )[0]


def planes_kernel(place_ref, *refs):
    parts, out_ref = refs[:-1], refs[-1]
    count, rows = len(parts), parts[0].shape[0]
    total = None
    for steps, part in enumerate(parts):
        plane = lax.rem(place_ref[1] - steps + count, count)
        row, col = iota((count * rows, rows), 0), iota((count * rows, rows), 1)
        term = dot(unit((count * rows, rows), row == col + plane * rows), part[...])
        total = term if total is None else total + term
    out_ref[...] = total.astype(BF16)


def gather_planes(block, place):
    count = lax.axis_size("fsdp")
    parts = [block] + [shift(block, "fsdp", steps) for steps in range(1, count)]
    rows, width = block.shape
    return call(
        planes_kernel,
        [shape_of((count * rows, width), BF16)],
        [VMEM_SPEC],
        [place] + parts,
        [SMEM_SPEC] + [VMEM_SPEC] * count,
        flops=2 * count * count * rows * rows * width,
        moved=4 * count * rows * width,
    )[0]


def attend_kernel(
    part_count,
    narrow_rows,
    wide_rows,
    head_count,
    place_ref,
    near_ref,
    back_ref,
    far_ref,
    cos_ref,
    sin_ref,
    low_ref,
    *refs,
):
    parts = refs[:part_count]
    (
        attn_in_ref,
        query_lin_ref,
        key_lin_ref,
        query_ref,
        keys_ref,
        probs_ref,
        attended_ref,
        gains_ref,
        small_gains_ref,
        attn_out_ref,
        middle_ref,
        ffn_in_ref,
    ) = refs[part_count : part_count + 12]
    weights, inside, sems = refs[part_count + 12 :]
    copies = start_placing(parts, weights, sems, 0, place_ref[0])
    rows, width = near_ref.shape
    head_dim = key_lin_ref.shape[1]
    heads_width = head_count * head_dim
    score_scale = head_dim**-0.5
    blocks = [far_ref, back_ref, near_ref]
    scales = []
    for ref in blocks:
        scales.append(inverse_rms(ref[...].astype(F32)))
    wait_all(copies)
    gain_start = heads_width + 2 * head_dim
    gain_cols = weights[:, gain_start : gain_start + LANES]
    pick = unit((8, LANES), iota((8, LANES), 0) == iota((8, LANES), 1))
    gains = dot_t(pick, gain_cols)
    spread = spread_matrix(head_dim, width, narrow_rows, wide_rows)
    small_gains = dot_t(gains.astype(BF16), spread)
    gains_ref[...] = gains
    small_gains_ref[...] = small_gains
    gain_an, gain_q, gain_k = gains[0:1], small_gains[4:5], small_gains[5:6]
    for index, ref in enumerate(blocks):
        normed = ref[...].astype(F32) * scales[index] * gain_an
        inside[index * rows : (index + 1) * rows, :] = normed.astype(BF16)
    attn_in_ref[...] = inside[2 * rows :, :]
    for index in range(3):
        span = slice(index * rows, (index + 1) * rows)
        part_in = inside[span, :]
        key_lin = dot(part_in, weights[:, heads_width : heads_width + head_dim])
        value = dot(part_in, weights[:, heads_width + head_dim : heads_width + 2 * head_dim])
        key = rotate(key_lin * inverse_rms(key_lin) * gain_k, cos_ref[span, :], sin_ref[span, :])
        keys_ref[span, :head_dim] = key.astype(BF16)
        keys_ref[span, head_dim:] = value.astype(BF16)
        if index == 2:
            key_lin_ref[...] = key_lin
    cosine, sine = cos_ref[2 * rows :, :], sin_ref[2 * rows :, :]
    column = iota((rows, 3 * rows), 1)
    seen = (column >= low_ref[...]) & (column <= iota((rows, 3 * rows), 0) + 2 * rows)
    for head in range(head_count):
        lanes = slice(head * head_dim, (head + 1) * head_dim)
        query_lin = dot(inside[2 * rows :, :], weights[:, lanes])
        query_lin_ref[:, lanes] = query_lin
        query = rotate(query_lin * inverse_rms(query_lin) * gain_q, cosine, sine).astype(BF16)
        query_ref[:, lanes] = query
        scores = jnp.where(seen, dot_t(query, keys_ref[:, :head_dim]) * score_scale, NEGATIVE)
        raised = jnp.exp(scores - jnp.max(scores, axis=-1, keepdims=True))
        probs = (raised / jnp.sum(raised, axis=-1, keepdims=True)).astype(BF16)
        probs_ref[head * rows : (head + 1) * rows, :] = probs
        attended_ref[:, lanes] = dot(probs, keys_ref[:, head_dim:]).astype(BF16)
    for start, size in tiles_of(width, 384):
        attn_out_ref[:, start : start + size] = dot_t(
            attended_ref[...], weights[start : start + size, gain_start + LANES :]
        )
    attn_out = attn_out_ref[...]
    middle = near_ref[...].astype(F32) + attn_out * inverse_rms(attn_out) * gains[1:2]
    middle_ref[...] = middle
    ffn_in_ref[...] = (middle * inverse_rms(middle) * gains[2:3]).astype(BF16)


def attend(place, tokens3, cosine, sine, lowest, parts, head_count, head_dim, narrow_rows, wide_rows):
    rows, width = tokens3[0].shape
    heads_width = head_count * head_dim
    pack = parts[0].shape[1]
    outs = [
        shape_of((rows, width), BF16),
        shape_of((rows, heads_width), F32),
        shape_of((rows, head_dim), F32),
        shape_of((rows, heads_width), BF16),
        shape_of((3 * rows, 2 * head_dim), BF16),
        shape_of((head_count * rows, 3 * rows), BF16),
        shape_of((rows, heads_width), BF16),
        shape_of((8, width), F32),
        shape_of((8, head_dim), F32),
        shape_of((rows, width), F32),
        shape_of((rows, width), F32),
        shape_of((rows, width), BF16),
    ]
    return call(
        functools.partial(attend_kernel, len(parts), narrow_rows, wide_rows, head_count),
        outs,
        [VMEM_SPEC] * len(outs),
        [place] + list(tokens3) + [cosine, sine, lowest] + parts,
        [SMEM_SPEC] + [VMEM_SPEC] * 6 + [ANY_SPEC] * len(parts),
        [
            pltpu.VMEM((width, pack), BF16),
            pltpu.VMEM((3 * rows, width), BF16),
            pltpu.SemaphoreType.DMA((len(parts),)),
        ],
        flops=2 * rows * width * (heads_width + 6 * head_dim) + 12 * rows * rows * heads_width,
        moved=2 * width * pack + 16 * rows * width,
        exps=3 * head_count * rows * rows,
    )


def gelu_pair(gate):
    square = gate * gate
    tanh = jnp.tanh(gate * (0.7978845608028654 + 0.035677408136300125 * square))
    half = 0.5 + 0.5 * tanh
    value = gate * half
    slope = half + value * (1.0 - tanh) * (0.7978845608028654 + 0.10703222440890037 * square)
    return value, slope


def gate_up_kernel(part_count, place_ref, *refs):
    blocks, refs = refs[:4], refs[4:]
    parts = refs[:part_count]
    act_ref, gate_slope_ref, up_slope_ref, held, weights, sems = refs[part_count:]
    hidden, up_start = act_ref.shape[1], weights.shape[1] - act_ref.shape[1]
    step = pl.program_id(0)

    @pl.when(step == 0)
    def _():
        wait_all(start_placing(parts, weights, sems, 0, place_ref[0]))

    for index, block in enumerate(blocks):

        @pl.when(step == index)
        def _(block=block):
            held[...] = block[...]

    rows_in = held[...]
    for start, size in tiles_of(hidden, 256):
        lanes = slice(start, start + size)
        gate = dot(rows_in, weights[:, lanes])
        up = dot(rows_in, weights[:, up_start + start : up_start + start + size])
        value, slope = gelu_pair(gate)
        act_ref[:, lanes] = (value * up).astype(BF16)
        gate_slope_ref[:, lanes] = (slope * up).astype(BF16)
        up_slope_ref[:, lanes] = value.astype(BF16)


def gate_up(place, blocks, parts, hidden):
    rows, width = blocks[0].shape
    count = len(parts)
    out = shape_of((4 * rows, hidden), BF16)
    return pl.pallas_call(
        functools.partial(gate_up_kernel, count),
        out_shape=(out,) * 3,
        grid=(4,),
        in_specs=[SMEM_SPEC]
        + [pl.BlockSpec((rows, width), lambda step: (0, 0))] * 4
        + [ANY_SPEC] * count,
        out_specs=(pl.BlockSpec((rows, hidden), lambda step: (step, 0)),) * 3,
        scratch_shapes=[
            pltpu.VMEM((rows, width), BF16),
            pltpu.VMEM((width, parts[0].shape[1]), BF16),
            pltpu.SemaphoreType.DMA((count,)),
        ],
        compiler_params=pltpu.CompilerParams(vmem_limit_bytes=VMEM_LIMIT),
        cost_estimate=pl.CostEstimate(
            flops=16 * rows * width * hidden,
            bytes_accessed=4 * width * hidden + 24 * rows * hidden,
            transcendentals=4 * rows * hidden,
        ),
    )(place, *blocks, *parts)


def down_kernel(part_count, place_ref, act_ref, *refs):
    parts = refs[:part_count]
    outs = refs[part_count : part_count + 4]
    weights, sems = refs[part_count + 4 :]
    rows = outs[0].shape[0]
    wait_all(start_placing(parts, weights, sems, 0, place_ref[0]))
    for start, size in tiles_of(weights.shape[0], 256):
        lanes = slice(start, start + size)
        total = dot_t(act_ref[...], weights[lanes, :]).astype(BF16)
        for index, out in enumerate(outs):
            out[:, lanes] = total[index * rows : (index + 1) * rows]


def down(place, act, parts):
    rows, hidden = act.shape[0] // 4, act.shape[1]
    width = parts[0].shape[0] * len(parts)
    return call(
        functools.partial(down_kernel, len(parts)),
        [shape_of((rows, width), BF16)] * 4,
        [VMEM_SPEC] * 4,
        [place, act] + parts,
        [SMEM_SPEC, VMEM_SPEC] + [ANY_SPEC] * len(parts),
        [pltpu.VMEM((width, hidden), BF16), pltpu.SemaphoreType.DMA((len(parts),))],
        flops=8 * rows * hidden * width,
        moved=2 * width * hidden + 8 * rows * (width + hidden),
    )


def turn_kernel(
    own_ref, far_ref, across_ref, along_ref, middle_ref, upstream_ref, gains_ref, *outs
):
    output_ref, back_ref, gain_grad_ref = outs
    total = own_ref[...].astype(F32) + far_ref[...].astype(F32)
    total = total + across_ref[...].astype(F32) + along_ref[...].astype(F32)
    scale = inverse_rms(total)
    normed = total * scale
    gain = gains_ref[3:4, :]
    output_ref[...] = (middle_ref[...] + normed * gain).astype(BF16)
    back, gain_grad = norm_back(normed, scale, gain, upstream_ref[...].astype(F32))
    back_ref[...] = back.astype(BF16)
    gain_grad_ref[...] = gain_grad


def turn(sums, middle, upstream, gains):
    rows, width = middle.shape
    return call(
        turn_kernel,
        [shape_of((rows, width), BF16), shape_of((rows, width), BF16), shape_of((1, width), F32)],
        [VMEM_SPEC] * 3,
        list(sums) + [middle, upstream, gains],
        [VMEM_SPEC] * 7,
        moved=20 * rows * width,
    )


def ffn_back_kernel(part_count, first, span, place_ref, *refs):
    backs, refs = refs[:span], refs[span:]
    gate_slope_ref, up_slope_ref = refs[:2]
    refs = refs[2:]
    down_parts, gate_up_parts = refs[:part_count], refs[part_count : 2 * part_count]
    refs = refs[2 * part_count :]
    outs, refs = refs[:span], refs[span:]
    d_gate_ref, d_up_ref, held, gate_slope, up_slope, down_w, gate_up_w, sems, slope_sems = refs
    rows, hidden = outs[0].shape[0], d_gate_ref.shape[1]
    up_start = gate_up_w.shape[1] - hidden
    seq = place_ref[0]
    copies = start_placing(down_parts, down_w, sems, 0, seq)
    fetches = [
        pltpu.make_async_copy(
            source.at[pl.ds(first * rows, span * rows), :], dest, slope_sems.at[index]
        )
        for index, (source, dest) in enumerate(
            [(gate_slope_ref, gate_slope), (up_slope_ref, up_slope)]
        )
    ]
    for fetch in fetches:
        fetch.start()
    later = start_placing(gate_up_parts, gate_up_w, sems, part_count, seq)
    for index, back in enumerate(backs):
        held[index * rows : (index + 1) * rows, :] = back[...]
    wait_all(copies)
    wait_all(fetches)
    for start, size in tiles_of(hidden, 256):
        lanes = slice(start, start + size)
        d_act = dot(held[...], down_w[:, lanes])
        d_gate_ref[:, lanes] = (d_act * gate_slope[:, lanes].astype(F32)).astype(BF16)
        d_up_ref[:, lanes] = (d_act * up_slope[:, lanes].astype(F32)).astype(BF16)
    wait_all(later)
    for start, size in tiles_of(gate_up_w.shape[0], 256):
        lanes = slice(start, start + size)
        total = dot_t(d_gate_ref[...], gate_up_w[lanes, :hidden])
        total = (total + dot_t(d_up_ref[...], gate_up_w[lanes, up_start:])).astype(BF16)
        for index, out in enumerate(outs):
            out[:, lanes] = total[index * rows : (index + 1) * rows]


def ffn_back(place, backs, first, gate_slope, up_slope, down_parts, gate_up_parts):
    span = len(backs)
    rows, width = backs[0].shape
    hidden = gate_slope.shape[1]
    count = len(down_parts)
    hidden_out = shape_of((span * rows, hidden), BF16)
    return call(
        functools.partial(ffn_back_kernel, count, first, span),
        [shape_of((rows, width), BF16)] * span + [hidden_out] * 2,
        [VMEM_SPEC] * (span + 2),
        [place] + list(backs) + [gate_slope, up_slope] + down_parts + gate_up_parts,
        [SMEM_SPEC] + [VMEM_SPEC] * span + [ANY_SPEC] * (2 + 2 * count),
        [
            pltpu.VMEM((span * rows, width), BF16),
            pltpu.VMEM((span * rows, hidden), BF16),
            pltpu.VMEM((span * rows, hidden), BF16),
            pltpu.VMEM((width, hidden), BF16),
            pltpu.VMEM((width, gate_up_parts[0].shape[1]), BF16),
            pltpu.SemaphoreType.DMA((2 * count,)),
            pltpu.SemaphoreType.DMA((2,)),
        ],
        flops=6 * span * rows * hidden * width,
        moved=6 * width * hidden + 12 * span * rows * hidden,
    )


def weight_grad_kernel(left_count, right_count, place_ref, *refs):
    lefts, rights = refs[:left_count], refs[left_count : left_count + right_count]
    refs = refs[left_count + right_count :]
    outs, (left, right, whole, sems) = refs[:-4], refs[-4:]
    tiles = tiles_of(right.shape[1], 512)
    first, start = [], 0
    for piece in lefts:
        size = piece.shape[0]
        first.append(
            pltpu.make_async_copy(piece, left.at[pl.ds(start, size), :], sems.at[len(first)])
        )
        start += size
    waits = []
    for number, (lane, size) in enumerate(tiles):
        copies, start = [], 0
        for piece in rights:
            rows = piece.shape[0]
            copies.append(
                pltpu.make_async_copy(
                    piece.at[:, pl.ds(lane, size)],
                    right.at[pl.ds(start, rows), pl.ds(lane, size)],
                    sems.at[left_count + number * right_count + len(copies)],
                )
            )
            start += rows
        waits.append(copies)
    for copy in first + [copy for copies in waits for copy in copies]:
        copy.start()
    wait_all(first)
    for copies, (lane, size) in zip(waits, tiles):
        wait_all(copies)
        lanes = slice(lane, lane + size)
        whole[:, lanes] = dot_tn(left[...], right[:, lanes]).astype(BF16)
    wait_all(start_cutting(whole, outs, sems, 0, place_ref[0]))


def weight_grad(place, lefts, rights):
    height, width = lefts[0].shape[1], rights[0].shape[1]
    rows = sum(piece.shape[0] for piece in lefts)
    count = lax.axis_size("seq")
    outs = cut_shapes(height, width, count)
    return call(
        functools.partial(weight_grad_kernel, len(lefts), len(rights)),
        outs,
        [ANY_SPEC] * len(outs),
        [place] + list(lefts) + list(rights),
        [SMEM_SPEC] + [ANY_SPEC] * (len(lefts) + len(rights)),
        [
            pltpu.VMEM((rows, height), BF16),
            pltpu.VMEM((rows, width), BF16),
            pltpu.VMEM((height, width), BF16),
            pltpu.SemaphoreType.DMA((count + len(lefts) + 4 * len(rights),)),
        ],
        flops=2 * rows * height * width,
        moved=2 * (rows * (height + width) + height * width),
    )


def attend_back_kernel(
    part_count,
    out_count,
    head_count,
    place_ref,
    own_ref,
    far_ref,
    across_ref,
    along_ref,
    middle_ref,
    upstream_ref,
    attn_out_ref,
    gains_ref,
    small_gains_ref,
    attended_ref,
    attn_in_ref,
    query_lin_ref,
    query_ref,
    keys_ref,
    probs_ref,
    cos_ref,
    sin_ref,
    *refs,
):
    parts, refs = refs[:part_count], refs[part_count:]
    grads, refs = refs[:out_count], refs[out_count:]
    d_middle_ref, d_in_ref, far_halo_ref, back_halo_ref, near_ref, rows_ref, query_gain_ref = refs[:7]
    weights, whole, d_query, d_keys, sems = refs[7:]
    rows, width = middle_ref.shape
    head_dim = keys_ref.shape[1] // 2
    heads_width = head_count * head_dim
    score_scale = head_dim**-0.5
    seq = place_ref[0]
    copies = start_placing(parts, weights, sems, 0, seq)
    out_start = weights.shape[1] - heads_width
    total = own_ref[...].astype(F32) + far_ref[...].astype(F32)
    total = total + across_ref[...].astype(F32) + along_ref[...].astype(F32)
    middle = middle_ref[...]
    scale = inverse_rms(middle)
    back, grad_fn = norm_back(middle * scale, scale, gains_ref[2:3, :], total)
    d_middle = upstream_ref[...].astype(F32) + back
    d_middle_ref[...] = d_middle
    attn_out = attn_out_ref[...]
    scale = inverse_rms(attn_out)
    d_attn_out, grad_ap = norm_back(attn_out * scale, scale, gains_ref[1:2, :], d_middle)
    row = iota((8, width), 0)
    rows_ref[...] = jnp.where(row == 1, grad_ap, 0.0) + jnp.where(row == 2, grad_fn, 0.0)
    d_attn_low = d_attn_out.astype(BF16)
    for start, size in tiles_of(heads_width, 256):
        lanes = slice(start, start + size)
        whole[:, start : start + size] = dot_tn(d_attn_low, attended_ref[:, lanes]).astype(BF16)
    wait_all(copies)
    cosine, sine = cos_ref[2 * rows :, :], sin_ref[2 * rows :, :]
    gain_q = small_gains_ref[4:5, :]
    query_gain = jnp.zeros((1, head_dim), F32)
    for head in range(head_count):
        lanes = slice(head * head_dim, (head + 1) * head_dim)
        out_lanes = slice(out_start + head * head_dim, out_start + (head + 1) * head_dim)
        d_attended = dot(d_attn_low, weights[:, out_lanes]).astype(BF16)
        probs_low = probs_ref[head * rows : (head + 1) * rows, :]
        probs = probs_low.astype(F32)
        d_probs = dot_t(d_attended, keys_ref[:, head_dim:])
        delta = jnp.sum(probs * d_probs, axis=-1, keepdims=True)
        d_scores = (probs * (d_probs - delta) * score_scale).astype(BF16)
        d_rotated = dot(d_scores, keys_ref[:, :head_dim])
        d_key = dot_tn(d_scores, query_ref[:, lanes])
        d_value = dot_tn(probs_low, d_attended)
        if head == 0:
            d_keys[:, :head_dim] = d_key
            d_keys[:, head_dim:] = d_value
        else:
            d_keys[:, :head_dim] += d_key
            d_keys[:, head_dim:] += d_value
        query_lin = query_lin_ref[:, lanes]
        scale = inverse_rms(query_lin)
        d_normed = rotate(d_rotated, cosine, -sine)
        back, gain_grad = norm_back(query_lin * scale, scale, gain_q, d_normed)
        query_gain = query_gain + gain_grad
        d_query[:, lanes] = back.astype(BF16)
    query_gain_ref[...] = query_gain
    far_halo_ref[...] = d_keys[:rows, :].astype(BF16)
    back_halo_ref[...] = d_keys[rows : 2 * rows, :].astype(BF16)
    near_ref[...] = d_keys[2 * rows :, :]
    for start, size in tiles_of(heads_width, 256):
        lanes = slice(start, start + size)
        whole[:, heads_width + start : heads_width + start + size] = dot_tn(
            attn_in_ref[...], d_query[:, lanes]
        ).astype(BF16)
    cuts = start_cutting(whole, grads, sems, part_count, seq)
    for start, size in tiles_of(width, 384):
        lanes = slice(start, start + size)
        d_in_ref[:, lanes] = dot_t(d_query[...], weights[lanes, :heads_width])
    wait_all(cuts)


def attend_back(place, sums, saved, cosine, sine, parts, head_count):
    middle, upstream, attn_out, gains, small_gains, attended, attn_in, query_lin, query, keys, probs = saved
    rows, width = middle.shape
    head_dim = keys.shape[1] // 2
    heads_width = head_count * head_dim
    count = lax.axis_size("seq")
    cuts = cut_shapes(width, 2 * heads_width, count)
    outs = cuts + [
        shape_of((rows, width), F32),
        shape_of((rows, width), F32),
        shape_of((rows, 2 * head_dim), BF16),
        shape_of((rows, 2 * head_dim), BF16),
        shape_of((rows, 2 * head_dim), F32),
        shape_of((8, width), F32),
        shape_of((1, head_dim), F32),
    ]
    ins = [place] + list(sums) + list(saved) + [cosine, sine] + parts
    return call(
        functools.partial(attend_back_kernel, len(parts), len(cuts), head_count),
        outs,
        [ANY_SPEC] * len(cuts) + [VMEM_SPEC] * 7,
        ins,
        [SMEM_SPEC] + [VMEM_SPEC] * 17 + [ANY_SPEC] * len(parts),
        [
            pltpu.VMEM((width, parts[0].shape[1]), BF16),
            pltpu.VMEM((width, 2 * heads_width), BF16),
            pltpu.VMEM((rows, heads_width), BF16),
            pltpu.VMEM((3 * rows, 2 * head_dim), F32),
            pltpu.SemaphoreType.DMA((len(parts) + count,)),
        ],
        flops=8 * rows * width * heads_width + 30 * rows * rows * heads_width,
        moved=12 * width * heads_width + 30 * rows * width,
    )


def finish_kernel(
    first_count,
    out_count,
    narrow_rows,
    wide_rows,
    place_ref,
    near_ref,
    back_ref,
    far_ref,
    key_lin_ref,
    small_gains_ref,
    gains_ref,
    cos_ref,
    sin_ref,
    attn_in_ref,
    tokens_ref,
    d_middle_ref,
    d_in_ref,
    rows_ref,
    ffn_post_ref,
    query_gain_ref,
    *refs,
):
    first_parts, refs = refs[:first_count], refs[first_count:]
    grads, (input_grad_ref, first_w, whole, d_low, sems) = refs[:out_count], refs[out_count:]
    rows, width = tokens_ref.shape
    head_dim = key_lin_ref.shape[1]
    seq = place_ref[0]
    heads_width = parts_width(first_parts[0], key_lin_ref.shape[1])
    copies = start_placing(first_parts, first_w, sems, 0, seq, heads_width, 2 * key_lin_ref.shape[1])
    d_keys = near_ref[...] + back_ref[...].astype(F32) + far_ref[...].astype(F32)
    key_lin = key_lin_ref[...]
    scale = inverse_rms(key_lin)
    d_normed = rotate(d_keys[:, :head_dim], cos_ref[2 * rows :, :], -sin_ref[2 * rows :, :])
    back, key_gain = norm_back(key_lin * scale, scale, small_gains_ref[5:6, :], d_normed)
    d_low[:, :head_dim] = back.astype(BF16)
    d_low[:, head_dim:] = d_keys[:, head_dim:].astype(BF16)
    whole[:, : 2 * head_dim] = dot_tn(attn_in_ref[...], d_low[...]).astype(BF16)
    wait_all(copies)
    d_attn_in = d_in_ref[...] + dot_t(d_low[...], first_w[...])
    inputs = tokens_ref[...].astype(F32)
    scale = inverse_rms(inputs)
    back, grad_an = norm_back(inputs * scale, scale, gains_ref[0:1, :], d_attn_in)
    input_grad_ref[...] = d_middle_ref[...] + back
    row = iota((8, width), 0)
    gain_rows = rows_ref[...] + jnp.where(row == 0, grad_an, 0.0)
    gain_rows = gain_rows + jnp.where(row == 3, ffn_post_ref[...], 0.0)
    small_row = iota((8, head_dim), 0)
    small = jnp.where(small_row == 4, query_gain_ref[...], 0.0)
    small = small + jnp.where(small_row == 5, key_gain, 0.0)
    spread = spread_matrix(head_dim, width, narrow_rows, wide_rows)
    gain_rows = gain_rows + dot(small.astype(BF16), spread)
    pick = unit((8, LANES), iota((8, LANES), 0) == iota((8, LANES), 1))
    whole[:, 2 * head_dim :] = dot_tn(gain_rows.astype(BF16), pick).astype(BF16)
    wait_all(start_cutting(whole, grads, sems, first_count, seq))


def finish(place, ins, parts, narrow_rows, wide_rows):
    tokens, key_lin, first_parts = ins[9], ins[3], parts
    rows, width = tokens.shape
    head_dim = key_lin.shape[1]
    count = lax.axis_size("seq")
    pack = 2 * head_dim + LANES
    cuts = cut_shapes(width, pack, count)
    return call(
        functools.partial(finish_kernel, len(parts), len(cuts), narrow_rows, wide_rows),
        cuts + [shape_of((rows, width), F32)],
        [ANY_SPEC] * len(cuts) + [VMEM_SPEC],
        [place] + list(ins) + first_parts,
        [SMEM_SPEC] + [VMEM_SPEC] * len(ins) + [ANY_SPEC] * len(parts),
        [
            pltpu.VMEM((width, 2 * head_dim), BF16),
            pltpu.VMEM((width, pack), BF16),
            pltpu.VMEM((rows, 2 * head_dim), BF16),
            pltpu.SemaphoreType.DMA((len(parts) + count,)),
        ],
        flops=8 * rows * width * head_dim,
        moved=4 * width * pack + 20 * rows * width,
    )


def layout(lengths, counts, first_slot, row_count):
    starts = jnp.cumsum(lengths) - lengths
    slot_index = first_slot + jnp.arange(row_count, dtype=jnp.int32)
    member = (slot_index[:, None] >= starts[None, :]).astype(jnp.int32)
    document = jnp.sum(member, axis=1) - 1
    onehot = (document[:, None] == jnp.arange(lengths.shape[0], dtype=jnp.int32)[None, :]).astype(
        jnp.int32
    )
    position = slot_index - jnp.sum(onehot * starts[None, :], axis=1)
    padded = jnp.sum(onehot * (lengths - counts)[None, :], axis=1)
    return (position, padded)


def on_device(
    tokens,
    cotangent,
    doc_lengths,
    true_counts,
    w_query,
    w_key,
    w_value,
    w_out,
    w_gate,
    w_up,
    w_down,
    attn_norm_gain,
    query_gain,
    key_gain,
    attn_post_gain,
    ffn_norm_gain,
    ffn_post_gain,
):
    row_count = tokens.shape[1]
    head_dim = w_key.shape[1]
    heads_width = w_query.shape[1]
    head_count = heads_width // head_dim
    seq_index, plane_index = lax.axis_index("seq"), lax.axis_index("fsdp")
    place = jnp.stack([seq_index, plane_index]).astype(jnp.int32)
    inputs, upstream = tokens[0], cotangent[0]
    wide_rows, narrow_rows = attn_norm_gain.shape[0], query_gain.shape[0]

    pack = pack_attn(
        w_query,
        w_key,
        w_value,
        w_out,
        [attn_norm_gain, attn_post_gain, ffn_norm_gain, ffn_post_gain],
        [query_gain, key_gain],
    )
    behind = after(inputs, pack)
    tokens3 = [inputs, from_behind(behind, 1), from_behind(behind, 2)]
    hidden = w_gate.shape[1]
    spare = jnp.zeros((w_gate.shape[0], -hidden % LANES), BF16)
    gate_up_own = jnp.concatenate([w_gate, spare, w_up], axis=1)
    pack_rows = gather_planes(pack, place)
    pack_far = gather_far(pack_rows)
    gate_up_other = swap(after(gate_up_own, pack_rows), "fsdp", 2)
    parts = gather_core(pack_far)

    first_slot = seq_index * row_count
    position, padded = layout(
        doc_lengths[0], true_counts[0], first_slot - WINDOW, row_count + WINDOW
    )
    frequency = ROPE_BASE ** (-2.0 * jnp.arange(head_dim // 2, dtype=F32) / head_dim)
    angles = position.astype(F32)[:, None] * frequency
    cosine, sine = jnp.cos(angles), jnp.sin(angles)
    reach = jnp.clip(position[WINDOW:] - padded[WINDOW:], 0, WINDOW - 1)
    lowest = (WINDOW + jnp.arange(row_count, dtype=jnp.int32) - reach)[:, None]

    gate_up_mine, gate_up_theirs = pick_slices(gate_up_own, gate_up_other)
    attend_place = after(place, gate_up_mine, gate_up_theirs)
    gate_up_near = spread_far({0: gate_up_mine})
    gate_up_crossed = swap(gate_up_theirs, "seq", 2)
    down_other = swap(after(w_down, gate_up_other), "fsdp", 2)
    (
        attn_in,
        query_lin,
        key_lin,
        query,
        keys,
        probs,
        attended,
        gains,
        small_gains,
        attn_out,
        middle,
        ffn_in,
    ) = attend(
        attend_place,
        tokens3,
        cosine,
        sine,
        lowest,
        parts,
        head_count,
        head_dim,
        narrow_rows,
        wide_rows,
    )
    blocks = group_blocks(ffn_in)
    gate_up_far = gate_up_near | spread_far({2: after(gate_up_crossed, ffn_in)})
    gate_up_parts = gather_core({rel: after(part, ffn_in) for rel, part in gate_up_far.items()})
    down_mine, down_theirs = pick_slices(w_down, after(down_other, ffn_in))
    down_near = spread_far({0: down_mine})
    down_crossed = swap(down_theirs, "seq", 2)
    act, gate_slope, up_slope = gate_up(
        after(place, down_crossed), blocks, gate_up_parts, hidden
    )
    down_far = down_near | spread_far({2: down_crossed})
    down_parts = gather_core({rel: after(part, act) for rel, part in down_far.items()})
    far, across, along, own = down(place, act, down_parts)
    far, across, along = diagonal(far), swap(across, "seq", 2), swap(along, "fsdp", 1)
    output, d_ffn_low, grad_fp = turn([own, far, across, along], middle, upstream, gains)

    backs = group_blocks(d_ffn_low)
    slopes = (gate_slope, up_slope, down_parts, gate_up_parts)
    own, own_gate, own_up = ffn_back(place, backs[3:], 3, *slopes)
    far, across, along, side_gate, side_up = ffn_back(
        after(place, own), backs[:3], 0, *slopes
    )
    far, across, along = diagonal(far), swap(across, "seq", 2), swap(along, "fsdp", 1)
    down_pair = weight_grad(after(place, side_up), backs, [act])
    gate_pair = weight_grad(after(place, down_pair[0]), blocks, [side_gate, own_gate])
    down_merged = merge_cores(down_pair)
    up_pair = weight_grad(after(place, gate_pair[0], down_merged), blocks, [side_up, own_up])
    gate_merged = merge_cores(gate_pair)
    down_cross, got = merge_column(down_merged, 1)
    saved = (
        middle,
        upstream,
        attn_out,
        gains,
        small_gains,
        attended,
        attn_in,
        query_lin,
        query,
        keys,
        probs,
    )
    *head_grads, d_middle, d_in, far_halo, back_halo, near, gain_rows, query_gain_grad = attend_back(
        after(place, up_pair[0], gate_merged, down_cross),
        [own, far, across, along],
        saved,
        cosine,
        sine,
        parts,
        head_count,
    )
    down_near, got = merge_column(down_merged, 0, got)
    up_merged = merge_cores(up_pair)
    down_crossed = swap(down_cross, "seq", 2)
    ins = [
        near,
        from_behind(back_halo, -1),
        from_behind(far_halo, -2),
        key_lin,
        small_gains,
        gains,
        cosine,
        sine,
        attn_in,
        inputs,
        d_middle,
        d_in,
        gain_rows,
        grad_fp,
        query_gain_grad,
    ]
    *last_grads, input_grad = finish(
        after(place, down_crossed, down_near, up_merged), ins, parts, narrow_rows, wide_rows
    )
    gate_cross, got = merge_column(gate_merged, 1, got)
    gate_near, got = merge_column(gate_merged, 0, got)
    up_cross, got = merge_column(up_merged, 1, got)
    up_near, got = merge_column(up_merged, 0, got)
    gate_crossed, up_crossed = swap(gate_cross, "seq", 2), swap(up_cross, "seq", 2)
    grad_down, got = merge_planes(down_near, down_crossed)
    grad_gate, got = merge_planes(gate_near, gate_crossed, got)
    grad_up, got = merge_planes(up_near, up_crossed, got)
    head_rows = scatter_attn(head_grads)
    last_rows = scatter_attn(last_grads)
    gain_cols = last_rows[:, 2 * head_dim :]
    return (
        output[None],
        input_grad[None],
        head_rows[:, heads_width:],
        last_rows[:, :head_dim],
        last_rows[:, head_dim : 2 * head_dim],
        head_rows[:, :heads_width],
        grad_gate,
        grad_up,
        grad_down,
        gain_cols[:, 0],
        gain_cols[:narrow_rows, 4],
        gain_cols[:narrow_rows, 5],
        gain_cols[:, 1],
        gain_cols[:, 2],
        gain_cols[:, 3],
    )


def solution(mesh):
    rows = P("fsdp", "seq", None)
    shard, tile, vector = P(("seq", "fsdp"), None), P("seq", "fsdp"), P(("seq", "fsdp"))
    groups = P("fsdp", None)
    return jax.shard_map(
        on_device,
        mesh=mesh,
        in_specs=(rows, rows, groups, groups) + (shard,) * 4 + (tile,) * 3 + (vector,) * 6,
        out_specs=(rows, rows) + (shard,) * 4 + (tile,) * 3 + (vector,) * 6,
        check_vma=False,
    )
```

```python
import functools

import jax
import jax.numpy as jnp
from jax import lax
from jax.experimental import pallas as pl
from jax.experimental.pallas import tpu as pltpu
from jax.sharding import PartitionSpec as P

WINDOW = 512
NORM_EPS = 1e-06
ROPE_BASE = 10000.0
NEGATIVE = -1e30
LANES = 128
VMEM_LIMIT = 56 * 2**20
PIECES = 8
BF16 = jnp.bfloat16
F32 = jnp.float32


def from_behind(value, steps):
    count = lax.axis_size("seq")
    first, last = (max(0, -steps), min(count, count - steps))
    return lax.ppermute(value, "seq", [(source, source + steps) for source in range(first, last)])


def seq_masks():
    return [1 << bit for bit in range(lax.axis_size("seq").bit_length() - 1)]


def swap(value, axis, mask):
    count = lax.axis_size(axis)
    return lax.ppermute(value, axis, [(source, source ^ mask) for source in range(count)])


def shift(value, axis, steps):
    count = lax.axis_size(axis)
    return lax.ppermute(value, axis, [(source, (source + steps) % count) for source in range(count)])


def sync(state):
    return lax.optimization_barrier(state)


class Parts:
    def __init__(self, arrays, where):
        self.arrays, self.where = list(arrays), tuple(where)
        self.width = arrays[0].shape[-1]
        self.rows = arrays[0].shape[-2] * len(where)


def core_stack(parts):
    stack = jnp.stack(list(parts.values())) if len(parts) > 1 else list(parts.values())[0][None]
    return tuple(parts), swap(stack, "seq", 1)


def all_parts(parts, cores, *which):
    arrays, where = [], {}
    for rel, part in parts.items():
        where[rel] = (len(arrays), which)
        arrays.append(part)
    for rels, stack in cores:
        for index, rel in enumerate(rels):
            where[rel ^ 1] = (len(arrays), (index,) + which)
        arrays.append(stack)
    places = [where[rel] for rel in range(len(where))]
    if arrays[0].shape[-2] % 16 == 0:
        return Parts(arrays, places)
    index = jnp.arange(len(places), dtype=jnp.int32) ^ lax.axis_index("seq")
    blocks = [arrays[number][block] for number, block in places]
    whole = jnp.take(jnp.stack(blocks), index, axis=0, mode="clip")
    return Parts([whole.reshape(-1, whole.shape[-1])], [(0, ())])


def add_rounded(first, second):
    return (first.astype(F32) + second.astype(F32)).astype(BF16)


def cut(pair, count):
    if len(pair) == 2:
        return pair
    whole = pair[0]
    index = jnp.arange(count, dtype=jnp.int32) ^ lax.axis_index("seq")
    blocks = whole.reshape(whole.shape[:-2] + (count, -1, whole.shape[-1]))
    blocks = jnp.take(blocks, index, axis=blocks.ndim - 3, mode="clip")
    return blocks[..., 0::2, :, :], blocks[..., 1::2, :, :]


def cores_send(pair):
    keep, send = cut(pair, lax.axis_size("seq"))
    return keep, swap(send, "seq", 1)


def far_step(part):
    masks = [mask for mask in seq_masks() if mask > 2][::-1]
    for mask in masks[:-1]:
        half = part.shape[0] // 2
        part = add_rounded(part[:half], swap(part[half:], "seq", mask))
    half = part.shape[0] // 2
    return part[:half], swap(part[half:], "seq", masks[-1])


def across_step(part):
    part = part.reshape((-1, 2) + part.shape[1:])
    return part[:, 0], swap(part[:, 1], "seq", 2)


def straight(part, *steps):
    return [swap(part[step], "seq", 2 * step) for step in steps]


def planes_send(rows):
    planes = lax.axis_size("fsdp")
    blocks = rows.reshape((planes, -1) + rows.shape[1:])
    mine = lax.axis_index("fsdp")
    sent = [lax.dynamic_index_in_dim(blocks, mine, 0, keepdims=False)]
    for steps in range(1, planes):
        send = lax.dynamic_index_in_dim(blocks, (mine + steps) % planes, 0, keepdims=False)
        sent.append(shift(send, "fsdp", steps))
    return sent


def add_up(terms):
    total = terms[0].astype(F32)
    for term in terms[1:]:
        total = total + term.astype(F32)
    return total


def dot(left, right):
    return jnp.dot(left, right, preferred_element_type=F32)


def dot_t(left, right):
    return lax.dot_general(left, right, (((1,), (1,)), ((), ())), preferred_element_type=F32)


def dot_tn(left, right):
    return lax.dot_general(left, right, (((0,), (0,)), ((), ())), preferred_element_type=F32)


def inverse_rms(values):
    return lax.rsqrt(jnp.mean(values * values, axis=-1, keepdims=True) + NORM_EPS)


def norm_back(normed, scale, gain, upstream):
    scaled = upstream * gain
    back = scale * (scaled - normed * jnp.mean(scaled * normed, axis=-1, keepdims=True))
    return back, jnp.sum(upstream * normed, axis=0, keepdims=True)


def rotate(values, cosine, sine):
    half = values.shape[-1] // 2
    first, second = values[:, :half], values[:, half:]
    return jnp.concatenate(
        [first * cosine - second * sine, second * cosine + first * sine], axis=-1
    )


def iota(shape, dim):
    return lax.broadcasted_iota(jnp.int32, shape, dim)


def unit(shape, hits):
    return jnp.where(hits, 1.0, 0.0).astype(BF16)


def spread_matrix(narrow, wide, narrow_rows, wide_rows):
    row, col = iota((narrow, wide), 0), iota((narrow, wide), 1)
    return unit((narrow, wide), col == (row // narrow_rows) * wide_rows + row % narrow_rows)


def tiles_of(width, step):
    return [(start, min(step, width - start)) for start in range(0, width, step)]


def slots(where):
    return max(PIECES, len(where))


def start_placing(where, refs, dest, sems, base, seq, lane=0, lanes=None):
    copies = []
    if len(where) == 1:
        whole = refs[0] if lanes is None else refs[0].at[:, pl.ds(lane, lanes)]
        count = PIECES if whole.shape[0] % (16 * PIECES) == 0 else 1
        rows = whole.shape[0] // count
        pieces = [(index * rows, whole.at[pl.ds(index * rows, rows), :]) for index in range(count)]
        copies = [
            pltpu.make_async_copy(part, dest.at[pl.ds(start, rows), :], sems.at[base + index])
            for index, (start, part) in enumerate(pieces)
        ]
        for copy in copies:
            copy.start()
        return copies
    for rel, (number, block) in enumerate(where):
        part = refs[number].at[block] if block else refs[number]
        rows = part.shape[0]
        start = pl.multiple_of((seq ^ rel) * rows, 16) if len(where) > 1 else 0
        if lanes is not None:
            part = part.at[:, pl.ds(lane, lanes)]
        copies.append(
            pltpu.make_async_copy(part, dest.at[pl.ds(start, rows), :], sems.at[base + rel])
        )
    for copy in copies:
        copy.start()
    return copies


def start_cutting(whole, outs, sems, base, seq, which=None):
    if which is not None:
        outs = [out.at[which] for out in outs]
    if len(outs) == 1:
        copies = [pltpu.make_async_copy(whole, outs[0], sems.at[base])]
    else:
        half, rows = outs[0].shape[0], outs[0].shape[1]
        copies = []
        for rel in range(2 * half):
            start = pl.multiple_of((seq ^ rel) * rows, 16)
            copies.append(
                pltpu.make_async_copy(
                    whole.at[pl.ds(start, rows), :], outs[rel % 2].at[rel // 2], sems.at[base + rel]
                )
            )
    for copy in copies:
        copy.start()
    return copies


def cut_shapes(height, width, count):
    rows = height // count
    if rows % 16:
        return [jax.ShapeDtypeStruct((height, width), BF16)]
    return [jax.ShapeDtypeStruct((count // 2, rows, width), BF16)] * 2


def wait_all(copies):
    for copy in copies:
        copy.wait()


SMEM_SPEC = pl.BlockSpec(memory_space=pltpu.SMEM)
VMEM_SPEC = pl.BlockSpec(memory_space=pltpu.VMEM)
ANY_SPEC = pl.BlockSpec(memory_space=pl.ANY)


def call(kernel, outs, out_specs, ins, in_specs, scratch=(), flops=0, moved=0, exps=0):
    return pl.pallas_call(
        kernel,
        out_shape=tuple(outs),
        in_specs=list(in_specs),
        out_specs=tuple(out_specs),
        scratch_shapes=list(scratch),
        compiler_params=pltpu.CompilerParams(vmem_limit_bytes=VMEM_LIMIT),
        cost_estimate=pl.CostEstimate(flops=flops, bytes_accessed=moved, transcendentals=exps),
    )(*ins)


def shape_of(dims, dtype):
    return jax.ShapeDtypeStruct(dims, dtype)


def pack_kernel(wq_ref, wk_ref, wv_ref, wo_ref, *refs):
    wide, narrow, out_ref = refs[:4], refs[4:6], refs[6]
    rows, heads_width, head_dim = wq_ref.shape[0], wq_ref.shape[1], wk_ref.shape[1]
    out_ref[:, :heads_width] = wq_ref[...]
    out_ref[:, heads_width : heads_width + head_dim] = wk_ref[...]
    out_ref[:, heads_width + head_dim : heads_width + 2 * head_dim] = wv_ref[...]
    row = iota((16, rows), 0)
    held = jnp.zeros((16, rows), F32)
    for index, ref in enumerate(wide):
        held = held + jnp.where(row == index, ref[...].astype(F32), 0.0)
    small = narrow[0].shape[1]
    fit = unit((small, rows), iota((small, rows), 0) == iota((small, rows), 1))
    for index, ref in enumerate(narrow):
        spread = dot(jnp.broadcast_to(ref[...].astype(F32), (16, small)).astype(BF16), fit)
        held = held + jnp.where(row == 4 + index, spread, 0.0)
    place = unit((16, LANES), iota((16, LANES), 0) == iota((16, LANES), 1))
    gain_start = heads_width + 2 * head_dim
    out_ref[:, gain_start : gain_start + LANES] = dot_tn(held.astype(BF16), place).astype(BF16)
    out_ref[:, gain_start + LANES :] = wo_ref[...]


def pack_attn(w_query, w_key, w_value, w_out, wide, narrow):
    rows = w_query.shape[0]
    width = 2 * w_query.shape[1] + 2 * w_key.shape[1] + LANES
    ins = [w_query, w_key, w_value, w_out] + [vec.reshape(1, -1) for vec in wide + narrow]
    return call(
        pack_kernel,
        [shape_of((rows, width), BF16)],
        [VMEM_SPEC],
        ins,
        [VMEM_SPEC] * len(ins),
    )[0]


def planes_kernel(place_ref, *refs):
    parts, out_ref = refs[:-1], refs[-1]
    count, rows = len(parts), parts[0].shape[0]
    total = None
    for steps, part in enumerate(parts):
        plane = lax.rem(place_ref[1] - steps + count, count)
        row, col = iota((count * rows, rows), 0), iota((count * rows, rows), 1)
        term = dot(unit((count * rows, rows), row == col + plane * rows), part[...])
        total = term if total is None else total + term
    out_ref[...] = total.astype(BF16)


def place_planes(parts, place):
    count = len(parts)
    rows, width = parts[0].shape
    return call(
        planes_kernel,
        [shape_of((count * rows, width), BF16)],
        [VMEM_SPEC],
        [place] + parts,
        [SMEM_SPEC] + [VMEM_SPEC] * count,
        flops=2 * count * count * rows * rows * width,
        moved=4 * count * rows * width,
    )[0]


def attend_kernel(
    where,
    ref_count,
    narrow_rows,
    wide_rows,
    head_count,
    place_ref,
    near_ref,
    back_ref,
    far_ref,
    cos_ref,
    sin_ref,
    low_ref,
    *refs,
):
    parts, refs = refs[:ref_count], refs[ref_count:]
    (
        attn_in_ref,
        query_lin_ref,
        key_lin_ref,
        query_ref,
        keys_ref,
        probs_ref,
        attended_ref,
        gains_ref,
        small_gains_ref,
        attn_out_ref,
        middle_ref,
        ffn_in_ref,
    ) = refs[:12]
    weights, inside, sems = refs[12:]
    copies = start_placing(where, parts, weights, sems, 0, place_ref[0])
    rows, width = near_ref.shape
    head_dim = key_lin_ref.shape[1]
    heads_width = head_count * head_dim
    score_scale = head_dim**-0.5
    blocks = [far_ref, back_ref, near_ref]
    scales = []
    for ref in blocks:
        scales.append(inverse_rms(ref[...].astype(F32)))
    wait_all(copies)
    gain_start = heads_width + 2 * head_dim
    gain_cols = weights[:, gain_start : gain_start + LANES]
    pick = unit((8, LANES), iota((8, LANES), 0) == iota((8, LANES), 1))
    gains = dot_t(pick, gain_cols)
    spread = spread_matrix(head_dim, width, narrow_rows, wide_rows)
    small_gains = dot_t(gains.astype(BF16), spread)
    gains_ref[...] = gains
    small_gains_ref[...] = small_gains
    gain_an, gain_q, gain_k = gains[0:1], small_gains[4:5], small_gains[5:6]
    for index, ref in enumerate(blocks):
        normed = ref[...].astype(F32) * scales[index] * gain_an
        inside[index * rows : (index + 1) * rows, :] = normed.astype(BF16)
    attn_in_ref[...] = inside[2 * rows :, :]
    for index in range(3):
        span = slice(index * rows, (index + 1) * rows)
        part_in = inside[span, :]
        key_lin = dot(part_in, weights[:, heads_width : heads_width + head_dim])
        value = dot(part_in, weights[:, heads_width + head_dim : heads_width + 2 * head_dim])
        key = rotate(key_lin * inverse_rms(key_lin) * gain_k, cos_ref[span, :], sin_ref[span, :])
        keys_ref[span, :head_dim] = key.astype(BF16)
        keys_ref[span, head_dim:] = value.astype(BF16)
        if index == 2:
            key_lin_ref[...] = key_lin
    cosine, sine = cos_ref[2 * rows :, :], sin_ref[2 * rows :, :]
    column = iota((rows, 3 * rows), 1)
    seen = (column >= low_ref[...]) & (column <= iota((rows, 3 * rows), 0) + 2 * rows)
    for head in range(head_count):
        lanes = slice(head * head_dim, (head + 1) * head_dim)
        query_lin = dot(inside[2 * rows :, :], weights[:, lanes])
        query_lin_ref[:, lanes] = query_lin
        query = rotate(query_lin * inverse_rms(query_lin) * gain_q, cosine, sine).astype(BF16)
        query_ref[:, lanes] = query
        scores = jnp.where(seen, dot_t(query, keys_ref[:, :head_dim]) * score_scale, NEGATIVE)
        raised = jnp.exp(scores - jnp.max(scores, axis=-1, keepdims=True))
        probs = (raised / jnp.sum(raised, axis=-1, keepdims=True)).astype(BF16)
        probs_ref[head * rows : (head + 1) * rows, :] = probs
        attended_ref[:, lanes] = dot(probs, keys_ref[:, head_dim:]).astype(BF16)
    for start, size in tiles_of(width, 384):
        attn_out_ref[:, start : start + size] = dot_t(
            attended_ref[...], weights[start : start + size, gain_start + LANES :]
        )
    attn_out = attn_out_ref[...]
    middle = near_ref[...].astype(F32) + attn_out * inverse_rms(attn_out) * gains[1:2]
    middle_ref[...] = middle
    ffn_in_ref[...] = (middle * inverse_rms(middle) * gains[2:3]).astype(BF16)


def attend(place, tokens3, cosine, sine, lowest, parts, head_count, head_dim, narrow_rows, wide_rows):
    rows, width = tokens3[0].shape
    heads_width = head_count * head_dim
    pack = parts.width
    outs = [
        shape_of((rows, width), BF16),
        shape_of((rows, heads_width), F32),
        shape_of((rows, head_dim), F32),
        shape_of((rows, heads_width), BF16),
        shape_of((3 * rows, 2 * head_dim), BF16),
        shape_of((head_count * rows, 3 * rows), BF16),
        shape_of((rows, heads_width), BF16),
        shape_of((8, width), F32),
        shape_of((8, head_dim), F32),
        shape_of((rows, width), F32),
        shape_of((rows, width), F32),
        shape_of((rows, width), BF16),
    ]
    return call(
        functools.partial(
            attend_kernel, parts.where, len(parts.arrays), narrow_rows, wide_rows, head_count
        ),
        outs,
        [VMEM_SPEC] * len(outs),
        [place] + list(tokens3) + [cosine, sine, lowest] + parts.arrays,
        [SMEM_SPEC] + [VMEM_SPEC] * 6 + [ANY_SPEC] * len(parts.arrays),
        [
            pltpu.VMEM((width, pack), BF16),
            pltpu.VMEM((3 * rows, width), BF16),
            pltpu.SemaphoreType.DMA((slots(parts.where),)),
        ],
        flops=2 * rows * width * (heads_width + 6 * head_dim) + 12 * rows * rows * heads_width,
        moved=2 * width * pack + 16 * rows * width,
        exps=3 * head_count * rows * rows,
    )


def gelu_pair(gate):
    square = gate * gate
    tanh = jnp.tanh(gate * (0.7978845608028654 + 0.035677408136300125 * square))
    half = 0.5 + 0.5 * tanh
    value = gate * half
    slope = half + value * (1.0 - tanh) * (0.7978845608028654 + 0.10703222440890037 * square)
    return value, slope


def take_parts(wheres, counts, refs):
    parts = []
    for count in counts:
        parts.append(refs[:count])
        refs = refs[count:]
    bases = [sum(slots(where) for where in wheres[:index]) for index in range(len(wheres))]
    return parts, bases, refs


def parts_of(weights):
    wheres = tuple(parts.where for parts in weights)
    counts = tuple(len(parts.arrays) for parts in weights)
    arrays = [array for parts in weights for array in parts.arrays]
    return wheres, counts, arrays, sum(slots(where) for where in wheres)


def gate_up_body(rows_ref, gate_w, up_w, act_ref, gate_slope_ref, up_slope_ref):
    rows_in = rows_ref[...]
    for start, size in tiles_of(gate_w.shape[1], 256):
        lanes = slice(start, start + size)
        gate = dot(rows_in, gate_w[:, lanes])
        up = dot(rows_in, up_w[:, lanes])
        value, slope = gelu_pair(gate)
        act_ref[:, lanes] = (value * up).astype(BF16)
        gate_slope_ref[:, lanes] = (slope * up).astype(BF16)
        up_slope_ref[:, lanes] = value.astype(BF16)


def down_body(act_ref, down_w, out_ref):
    for start, size in tiles_of(down_w.shape[0], 384):
        lanes = slice(start, start + size)
        out_ref[:, lanes] = dot_t(act_ref[...], down_w[lanes, :]).astype(BF16)


def ffn_kernel(wheres, counts, place_ref, rows_ref, *refs):
    parts, bases, refs = take_parts(wheres, counts, refs)
    act_ref, gate_slope_ref, up_slope_ref, out_ref, gate_w, up_w, down_w, sems = refs
    seq = place_ref[0]
    copies = start_placing(wheres[0], parts[0], gate_w, sems, bases[0], seq)
    copies += start_placing(wheres[1], parts[1], up_w, sems, bases[1], seq)
    later = start_placing(wheres[2], parts[2], down_w, sems, bases[2], seq)
    wait_all(copies)
    gate_up_body(rows_ref, gate_w, up_w, act_ref, gate_slope_ref, up_slope_ref)
    wait_all(later)
    down_body(act_ref, down_w, out_ref)


def gate_up_kernel(wheres, counts, place_ref, rows_ref, *refs):
    parts, bases, refs = take_parts(wheres, counts, refs)
    act_ref, gate_slope_ref, up_slope_ref, gate_w, up_w, sems = refs
    seq = place_ref[0]
    copies = start_placing(wheres[0], parts[0], gate_w, sems, bases[0], seq)
    copies += start_placing(wheres[1], parts[1], up_w, sems, bases[1], seq)
    wait_all(copies)
    gate_up_body(rows_ref, gate_w, up_w, act_ref, gate_slope_ref, up_slope_ref)


def gate_up(place, rows_in, weights):
    rows, width = rows_in.shape
    hidden = weights[0].width
    wheres, counts, arrays, sem_count = parts_of(weights)
    return call(
        functools.partial(gate_up_kernel, wheres, counts),
        [shape_of((rows, hidden), BF16)] * 3,
        [VMEM_SPEC] * 3,
        [place, rows_in] + arrays,
        [SMEM_SPEC, VMEM_SPEC] + [ANY_SPEC] * len(arrays),
        [pltpu.VMEM((width, hidden), BF16)] * 2 + [pltpu.SemaphoreType.DMA((sem_count,))],
        flops=4 * rows * hidden * width,
        moved=4 * width * hidden + 6 * rows * hidden,
    )


def down_kernel(wheres, counts, place_ref, act_ref, *refs):
    parts, bases, refs = take_parts(wheres, counts, refs)
    out_ref, down_w, sems = refs
    wait_all(start_placing(wheres[0], parts[0], down_w, sems, bases[0], place_ref[0]))
    down_body(act_ref, down_w, out_ref)


def down(place, act, weights):
    rows, hidden = act.shape
    width = weights[0].rows
    wheres, counts, arrays, sem_count = parts_of(weights)
    return call(
        functools.partial(down_kernel, wheres, counts),
        [shape_of((rows, width), BF16)],
        [VMEM_SPEC],
        [place, act] + arrays,
        [SMEM_SPEC, VMEM_SPEC] + [ANY_SPEC] * len(arrays),
        [pltpu.VMEM((width, hidden), BF16), pltpu.SemaphoreType.DMA((sem_count,))],
        flops=2 * rows * hidden * width,
        moved=2 * width * hidden + 2 * rows * hidden,
    )[0]


def ffn(place, rows_in, weights):
    rows, width = rows_in.shape
    hidden = weights[0].width
    wheres, counts, arrays, sem_count = parts_of(weights)
    return call(
        functools.partial(ffn_kernel, wheres, counts),
        [shape_of((rows, hidden), BF16)] * 3 + [shape_of((rows, width), BF16)],
        [VMEM_SPEC] * 4,
        [place, rows_in] + arrays,
        [SMEM_SPEC, VMEM_SPEC] + [ANY_SPEC] * len(arrays),
        [pltpu.VMEM((width, hidden), BF16)] * 3 + [pltpu.SemaphoreType.DMA((sem_count,))],
        flops=6 * rows * hidden * width,
        moved=6 * width * hidden + 8 * rows * hidden,
    )


def turn_kernel(own_ref, came_ref, middle_ref, upstream_ref, gains_ref, *outs):
    output_ref, back_ref, gain_grad_ref = outs
    total = own_ref[...].astype(F32) + came_ref[...].astype(F32)
    scale = inverse_rms(total)
    normed = total * scale
    gain = gains_ref[3:4, :]
    output_ref[...] = (middle_ref[...] + normed * gain).astype(BF16)
    back, gain_grad = norm_back(normed, scale, gain, upstream_ref[...].astype(F32))
    back_ref[...] = back.astype(BF16)
    gain_grad_ref[...] = gain_grad


def turn(sums, middle, upstream, gains):
    rows, width = middle.shape
    return call(
        turn_kernel,
        [shape_of((rows, width), BF16), shape_of((rows, width), BF16), shape_of((1, width), F32)],
        [VMEM_SPEC] * 3,
        list(sums) + [middle, upstream, gains],
        [VMEM_SPEC] * 5,
        moved=20 * rows * width,
    )


def ffn_back_kernel(
    wheres, counts, place_ref, back_ref, gate_slope_ref, up_slope_ref, *refs
):
    parts, bases, refs = take_parts(wheres, counts, refs)
    d_gate_ref, d_up_ref, out_ref, gate_w, up_w, down_w, sems = refs
    seq = place_ref[0]
    copies = start_placing(wheres[2], parts[2], down_w, sems, bases[2], seq)
    later = start_placing(wheres[0], parts[0], gate_w, sems, bases[0], seq)
    later += start_placing(wheres[1], parts[1], up_w, sems, bases[1], seq)
    wait_all(copies)
    back = back_ref[...]
    for start, size in tiles_of(down_w.shape[1], 256):
        lanes = slice(start, start + size)
        d_act = dot(back, down_w[:, lanes])
        d_gate_ref[:, lanes] = (d_act * gate_slope_ref[:, lanes].astype(F32)).astype(BF16)
        d_up_ref[:, lanes] = (d_act * up_slope_ref[:, lanes].astype(F32)).astype(BF16)
    wait_all(later)
    for start, size in tiles_of(gate_w.shape[0], 384):
        lanes = slice(start, start + size)
        total = dot_t(d_gate_ref[...], gate_w[lanes, :])
        out_ref[:, lanes] = (total + dot_t(d_up_ref[...], up_w[lanes, :])).astype(BF16)


def ffn_back(place, back, slopes, weights):
    rows, width = back.shape
    hidden = weights[0].width
    wheres, counts, arrays, sem_count = parts_of(weights)
    return call(
        functools.partial(ffn_back_kernel, wheres, counts),
        [shape_of((rows, hidden), BF16)] * 2 + [shape_of((rows, width), BF16)],
        [VMEM_SPEC] * 3,
        [place, back] + list(slopes) + arrays,
        [SMEM_SPEC] + [VMEM_SPEC] * 3 + [ANY_SPEC] * len(arrays),
        [pltpu.VMEM((width, hidden), BF16)] * 3 + [pltpu.SemaphoreType.DMA((sem_count,))],
        flops=6 * rows * hidden * width,
        moved=6 * width * hidden + 12 * rows * hidden,
    )


def ffn_back_and_grad_kernel(in_counts, out_count, back_kernel, grad_kernel, place_ref, *refs):
    back_ins, refs = refs[: in_counts[0]], refs[in_counts[0] :]
    grad_ins, refs = refs[: in_counts[1]], refs[in_counts[1] :]
    back_outs, refs = refs[:3], refs[3:]
    grad_outs, refs = refs[:out_count], refs[out_count:]
    back_kernel(place_ref, *back_ins, *back_outs, *refs[:4])
    grad_kernel(place_ref, *grad_ins, *grad_outs, *refs[4:])


def ffn_back_and_grad(place, back, slopes, weights, lefts, rights):
    rows, width = back.shape
    hidden = weights[0].width
    wheres, counts, arrays, sem_count = parts_of(weights)
    count = lax.axis_size("seq")
    cuts = cut_shapes(width, hidden, count)
    all_rows = sum(piece.shape[0] for piece in lefts)
    grad_ins = list(lefts) + list(rights)
    back_ins = [back] + list(slopes) + arrays
    outs = call(
        functools.partial(
            ffn_back_and_grad_kernel,
            (len(back_ins), len(grad_ins)),
            len(cuts),
            functools.partial(ffn_back_kernel, wheres, counts),
            functools.partial(weight_grad_kernel, len(lefts), (len(rights),), len(cuts)),
        ),
        [shape_of((rows, hidden), BF16)] * 2 + [shape_of((rows, width), BF16)] + cuts,
        [VMEM_SPEC] * 3 + [ANY_SPEC] * len(cuts),
        [place] + back_ins + grad_ins,
        [SMEM_SPEC] + [VMEM_SPEC] * 3 + [ANY_SPEC] * (len(arrays) + len(grad_ins)),
        [pltpu.VMEM((width, hidden), BF16)] * 3
        + [pltpu.SemaphoreType.DMA((sem_count,))]
        + weight_grad_scratch(all_rows, width, hidden, len(lefts), [len(rights)], count),
        flops=2 * all_rows * width * hidden + 6 * rows * width * hidden,
        moved=8 * width * hidden,
    )
    return outs[0], outs[1], outs[2], outs[3:]


def weight_grad_scratch(rows, height, width, left_count, right_counts, count):
    sides, pieces = len(right_counts), sum(right_counts)
    tiles = len(tiles_of(width, 512))
    return [
        pltpu.VMEM((rows, height), BF16),
        pltpu.VMEM((sides, rows, width), BF16),
        pltpu.VMEM((sides, height, width), BF16),
        pltpu.SemaphoreType.DMA((left_count + tiles * pieces,)),
        pltpu.SemaphoreType.DMA((sides, count)),
    ]


def weight_grad_kernel(left_count, right_counts, out_count, place_ref, *refs):
    lefts, refs = refs[:left_count], refs[left_count:]
    rights = []
    for count in right_counts:
        rights.append(refs[:count])
        refs = refs[count:]
    outs, (left, right, whole, sems, out_sems) = refs[:-5], refs[-5:]
    number = 0

    def fetch(pieces, dest, *lanes):
        nonlocal number
        copies, start = [], 0
        for piece in pieces:
            rows = piece.shape[0]
            source = piece.at[:, lanes[0]] if lanes else piece
            target = dest.at[(pl.ds(start, rows),) + lanes]
            copies.append(pltpu.make_async_copy(source, target, sems.at[number]))
            number += 1
            start += rows
        for copy in copies:
            copy.start()
        return copies

    tiles = tiles_of(whole.shape[-1], 512)
    first = fetch(lefts, left)
    waits = [
        [fetch(pieces, right.at[index], pl.ds(lane, size)) for lane, size in tiles]
        for index, pieces in enumerate(rights)
    ]
    wait_all(first)
    cuts = []
    for index, pieces in enumerate(rights):
        for copies, (lane, size) in zip(waits[index], tiles):
            wait_all(copies)
            lanes = slice(lane, lane + size)
            whole[index, :, lanes] = dot_tn(left[...], right[index, :, lanes]).astype(BF16)
        cuts += start_cutting(
            whole.at[index],
            outs[index * out_count : (index + 1) * out_count],
            out_sems.at[index],
            0,
            place_ref[0],
        )
    wait_all(cuts)


def weight_grad(place, lefts, *rights):
    height, width = lefts[0].shape[1], rights[0][0].shape[1]
    rows = sum(piece.shape[0] for piece in lefts)
    count = lax.axis_size("seq")
    cuts = cut_shapes(height, width, count)
    pieces = [piece for side in rights for piece in side]
    sides = [len(side) for side in rights]
    outs = call(
        functools.partial(
            weight_grad_kernel, len(lefts), tuple(len(side) for side in rights), len(cuts)
        ),
        cuts * len(rights),
        [ANY_SPEC] * (len(cuts) * len(rights)),
        [place] + list(lefts) + pieces,
        [SMEM_SPEC] + [ANY_SPEC] * (len(lefts) + len(pieces)),
        weight_grad_scratch(rows, height, width, len(lefts), sides, count),
        flops=2 * rows * height * width * len(rights),
        moved=2 * (rows * (height + width) + height * width) * len(rights),
    )
    return [outs[start : start + len(cuts)] for start in range(0, len(outs), len(cuts))]


def attend_back_kernel(
    where,
    ref_count,
    head_count,
    place_ref,
    own_ref,
    came_ref,
    middle_ref,
    upstream_ref,
    attn_out_ref,
    gains_ref,
    query_ref,
    keys_ref,
    probs_ref,
    *refs,
):
    parts, refs = refs[:ref_count], refs[ref_count:]
    d_middle_ref, d_attn_ref, d_rotated_ref, far_halo_ref, back_halo_ref, near_ref, rows_ref = refs[:7]
    weights, d_keys, sems = refs[7:]
    rows, width = middle_ref.shape
    head_dim = keys_ref.shape[1] // 2
    heads_width = head_count * head_dim
    score_scale = head_dim**-0.5
    out_start = parts[0].shape[-1] - heads_width
    copies = start_placing(where, parts, weights, sems, 0, place_ref[0], out_start, heads_width)
    total = own_ref[...].astype(F32) + came_ref[...].astype(F32)
    middle = middle_ref[...]
    scale = inverse_rms(middle)
    back, grad_fn = norm_back(middle * scale, scale, gains_ref[2:3, :], total)
    d_middle = upstream_ref[...].astype(F32) + back
    d_middle_ref[...] = d_middle
    attn_out = attn_out_ref[...]
    scale = inverse_rms(attn_out)
    d_attn_out, grad_ap = norm_back(attn_out * scale, scale, gains_ref[1:2, :], d_middle)
    row = iota((8, width), 0)
    rows_ref[...] = jnp.where(row == 1, grad_ap, 0.0) + jnp.where(row == 2, grad_fn, 0.0)
    d_attn_low = d_attn_out.astype(BF16)
    d_attn_ref[...] = d_attn_low
    wait_all(copies)
    for head in range(head_count):
        lanes = slice(head * head_dim, (head + 1) * head_dim)
        d_attended = dot(d_attn_low, weights[:, lanes]).astype(BF16)
        probs_low = probs_ref[head * rows : (head + 1) * rows, :]
        probs = probs_low.astype(F32)
        d_probs = dot_t(d_attended, keys_ref[:, head_dim:])
        delta = jnp.sum(probs * d_probs, axis=-1, keepdims=True)
        d_scores = (probs * (d_probs - delta) * score_scale).astype(BF16)
        d_rotated_ref[:, lanes] = dot(d_scores, keys_ref[:, :head_dim])
        d_key = dot_tn(d_scores, query_ref[:, lanes])
        d_value = dot_tn(probs_low, d_attended)
        if head == 0:
            d_keys[:, :head_dim] = d_key
            d_keys[:, head_dim:] = d_value
        else:
            d_keys[:, :head_dim] += d_key
            d_keys[:, head_dim:] += d_value
    far_halo_ref[...] = d_keys[:rows, :].astype(BF16)
    back_halo_ref[...] = d_keys[rows : 2 * rows, :].astype(BF16)
    near_ref[...] = d_keys[2 * rows :, :]


def attend_back(place, sums, saved, parts, head_count):
    middle, upstream, attn_out, gains, query, keys, probs = saved
    rows, width = middle.shape
    head_dim = keys.shape[1] // 2
    heads_width = head_count * head_dim
    outs = [
        shape_of((rows, width), F32),
        shape_of((rows, width), BF16),
        shape_of((rows, heads_width), F32),
        shape_of((rows, 2 * head_dim), BF16),
        shape_of((rows, 2 * head_dim), BF16),
        shape_of((rows, 2 * head_dim), F32),
        shape_of((8, width), F32),
    ]
    ins = [place] + list(sums) + list(saved) + parts.arrays
    return call(
        functools.partial(attend_back_kernel, parts.where, len(parts.arrays), head_count),
        outs,
        [VMEM_SPEC] * 7,
        ins,
        [SMEM_SPEC] + [VMEM_SPEC] * 9 + [ANY_SPEC] * len(parts.arrays),
        [
            pltpu.VMEM((width, heads_width), BF16),
            pltpu.VMEM((3 * rows, 2 * head_dim), F32),
            pltpu.SemaphoreType.DMA((slots(parts.where),)),
        ],
        flops=2 * rows * width * heads_width + 30 * rows * rows * heads_width,
        moved=2 * width * heads_width + 24 * rows * width,
    )


def heads_kernel(
    where,
    ref_count,
    out_count,
    head_count,
    place_ref,
    d_attn_ref,
    attended_ref,
    attn_in_ref,
    d_rotated_ref,
    query_lin_ref,
    small_gains_ref,
    cos_ref,
    sin_ref,
    *refs,
):
    parts, refs = refs[:ref_count], refs[ref_count:]
    grads, refs = refs[:out_count], refs[out_count:]
    d_in_ref, query_gain_ref, weights, whole, d_query, sems, out_sems = refs
    rows, width = attn_in_ref.shape
    heads_width = attended_ref.shape[1]
    head_dim = heads_width // head_count
    seq = place_ref[0]
    copies = start_placing(where, parts, weights, sems, 0, seq, 0, heads_width)
    for start, size in tiles_of(heads_width, 512):
        lanes = slice(start, start + size)
        whole[0, :, lanes] = dot_tn(d_attn_ref[...], attended_ref[:, lanes]).astype(BF16)
    cuts = start_cutting(whole.at[0], grads, out_sems.at[0], 0, seq, 0)
    cosine, sine = cos_ref[2 * rows :, :], sin_ref[2 * rows :, :]
    gain_q = small_gains_ref[4:5, :]
    query_gain = jnp.zeros((1, head_dim), F32)
    for head in range(head_count):
        lanes = slice(head * head_dim, (head + 1) * head_dim)
        query_lin = query_lin_ref[:, lanes]
        scale = inverse_rms(query_lin)
        d_normed = rotate(d_rotated_ref[:, lanes], cosine, -sine)
        back, gain_grad = norm_back(query_lin * scale, scale, gain_q, d_normed)
        query_gain = query_gain + gain_grad
        d_query[:, lanes] = back.astype(BF16)
    query_gain_ref[...] = query_gain
    for start, size in tiles_of(heads_width, 512):
        lanes = slice(start, start + size)
        whole[1, :, lanes] = dot_tn(attn_in_ref[...], d_query[:, lanes]).astype(BF16)
    cuts += start_cutting(whole.at[1], grads, out_sems.at[1], 0, seq, 1)
    wait_all(copies)
    for start, size in tiles_of(width, 384):
        lanes = slice(start, start + size)
        d_in_ref[:, lanes] = dot_t(d_query[...], weights[lanes, :])
    wait_all(cuts)


def heads_back(place, ins, parts, head_count):
    attn_in, attended, small_gains = ins[2], ins[1], ins[5]
    rows, width = attn_in.shape
    heads_width, head_dim = attended.shape[1], small_gains.shape[1]
    count = lax.axis_size("seq")
    cuts = [
        shape_of((2,) + part.shape, BF16) for part in cut_shapes(width, heads_width, count)
    ]
    return call(
        functools.partial(
            heads_kernel, parts.where, len(parts.arrays), len(cuts), head_count
        ),
        cuts + [shape_of((rows, width), F32), shape_of((1, head_dim), F32)],
        [ANY_SPEC] * len(cuts) + [VMEM_SPEC] * 2,
        [place] + list(ins) + parts.arrays,
        [SMEM_SPEC] + [VMEM_SPEC] * 8 + [ANY_SPEC] * len(parts.arrays),
        [
            pltpu.VMEM((width, heads_width), BF16),
            pltpu.VMEM((2, width, heads_width), BF16),
            pltpu.VMEM((rows, heads_width), BF16),
            pltpu.SemaphoreType.DMA((slots(parts.where),)),
            pltpu.SemaphoreType.DMA((2, count)),
        ],
        flops=6 * rows * width * heads_width,
        moved=8 * width * heads_width,
    )


def finish_kernel(
    where,
    ref_count,
    out_count,
    narrow_rows,
    wide_rows,
    place_ref,
    near_ref,
    back_ref,
    far_ref,
    key_lin_ref,
    small_gains_ref,
    gains_ref,
    cos_ref,
    sin_ref,
    attn_in_ref,
    tokens_ref,
    d_middle_ref,
    d_in_ref,
    rows_ref,
    ffn_post_ref,
    query_gain_ref,
    *refs,
):
    parts, refs = refs[:ref_count], refs[ref_count:]
    grads, (input_grad_ref, first_w, whole, d_low, sems) = refs[:out_count], refs[out_count:]
    rows, width = tokens_ref.shape
    head_dim = key_lin_ref.shape[1]
    seq = place_ref[0]
    heads_width = (parts[0].shape[-1] - 2 * head_dim - LANES) // 2
    copies = start_placing(where, parts, first_w, sems, 0, seq, heads_width, 2 * head_dim)
    d_keys = near_ref[...] + back_ref[...].astype(F32) + far_ref[...].astype(F32)
    key_lin = key_lin_ref[...]
    scale = inverse_rms(key_lin)
    d_normed = rotate(d_keys[:, :head_dim], cos_ref[2 * rows :, :], -sin_ref[2 * rows :, :])
    back, key_gain = norm_back(key_lin * scale, scale, small_gains_ref[5:6, :], d_normed)
    d_low[:, :head_dim] = back.astype(BF16)
    d_low[:, head_dim:] = d_keys[:, head_dim:].astype(BF16)
    whole[:, : 2 * head_dim] = dot_tn(attn_in_ref[...], d_low[...]).astype(BF16)
    wait_all(copies)
    d_attn_in = d_in_ref[...] + dot_t(d_low[...], first_w[...])
    inputs = tokens_ref[...].astype(F32)
    scale = inverse_rms(inputs)
    back, grad_an = norm_back(inputs * scale, scale, gains_ref[0:1, :], d_attn_in)
    input_grad_ref[...] = d_middle_ref[...] + back
    row = iota((8, width), 0)
    gain_rows = rows_ref[...] + jnp.where(row == 0, grad_an, 0.0)
    gain_rows = gain_rows + jnp.where(row == 3, ffn_post_ref[...], 0.0)
    small_row = iota((8, head_dim), 0)
    small = jnp.where(small_row == 4, query_gain_ref[...], 0.0)
    small = small + jnp.where(small_row == 5, key_gain, 0.0)
    spread = spread_matrix(head_dim, width, narrow_rows, wide_rows)
    gain_rows = gain_rows + dot(small.astype(BF16), spread)
    pick = unit((8, LANES), iota((8, LANES), 0) == iota((8, LANES), 1))
    whole[:, 2 * head_dim :] = dot_tn(gain_rows.astype(BF16), pick).astype(BF16)
    wait_all(start_cutting(whole, grads, sems, slots(where), seq))


def finish(place, ins, parts, narrow_rows, wide_rows):
    tokens, key_lin = ins[9], ins[3]
    rows, width = tokens.shape
    head_dim = key_lin.shape[1]
    count = lax.axis_size("seq")
    pack = 2 * head_dim + LANES
    cuts = cut_shapes(width, pack, count)
    return call(
        functools.partial(
            finish_kernel, parts.where, len(parts.arrays), len(cuts), narrow_rows, wide_rows
        ),
        cuts + [shape_of((rows, width), F32)],
        [ANY_SPEC] * len(cuts) + [VMEM_SPEC],
        [place] + list(ins) + parts.arrays,
        [SMEM_SPEC] + [VMEM_SPEC] * len(ins) + [ANY_SPEC] * len(parts.arrays),
        [
            pltpu.VMEM((width, 2 * head_dim), BF16),
            pltpu.VMEM((width, pack), BF16),
            pltpu.VMEM((rows, 2 * head_dim), BF16),
            pltpu.SemaphoreType.DMA((slots(parts.where) + count,)),
        ],
        flops=8 * rows * width * head_dim,
        moved=4 * width * pack + 20 * rows * width,
    )


def layout(lengths, counts, first_slot, row_count):
    starts = jnp.cumsum(lengths) - lengths
    slot_index = first_slot + jnp.arange(row_count, dtype=jnp.int32)
    member = (slot_index[:, None] >= starts[None, :]).astype(jnp.int32)
    document = jnp.sum(member, axis=1) - 1
    onehot = (document[:, None] == jnp.arange(lengths.shape[0], dtype=jnp.int32)[None, :]).astype(
        jnp.int32
    )
    position = slot_index - jnp.sum(onehot * starts[None, :], axis=1)
    padded = jnp.sum(onehot * (lengths - counts)[None, :], axis=1)
    return (position, padded)


def on_device(
    tokens,
    cotangent,
    doc_lengths,
    true_counts,
    w_query,
    w_key,
    w_value,
    w_out,
    w_gate,
    w_up,
    w_down,
    attn_norm_gain,
    query_gain,
    key_gain,
    attn_post_gain,
    ffn_norm_gain,
    ffn_post_gain,
):
    row_count = tokens.shape[1]
    head_dim = w_key.shape[1]
    heads_width = w_query.shape[1]
    head_count = heads_width // head_dim
    seq_index, plane_index = lax.axis_index("seq"), lax.axis_index("fsdp")
    place = jnp.stack([seq_index, plane_index]).astype(jnp.int32)
    inputs, upstream = tokens[0], cotangent[0]
    wide_rows, narrow_rows = attn_norm_gain.shape[0], query_gain.shape[0]

    planes_count = lax.axis_size("fsdp")
    far_masks = [mask for mask in seq_masks() if mask > 2]

    def swap_far(parts):
        parts = dict(parts)
        for mask in far_masks:
            parts.update({rel ^ mask: swap(part, "seq", mask) for rel, part in parts.items()})
        return parts

    def swap_both(parts, rel):
        if rel not in far_masks:
            return swap(parts[rel], "seq", 2)
        split = (parts[rel].shape[-2] // 2 + 15) // 16 * 16
        top = swap(parts[rel][..., :split, :], "seq", 2)
        bottom = swap(parts[2][..., split:, :], "seq", rel)
        return jnp.concatenate([top, bottom], axis=-2)

    pack = pack_attn(
        w_query,
        w_key,
        w_value,
        w_out,
        [attn_norm_gain, attn_post_gain, ffn_norm_gain, ffn_post_gain],
        [query_gain, key_gain],
    )
    gate_up_own = jnp.stack([w_gate, w_up])
    pack, gate_up_own, inputs, w_down = sync((pack, gate_up_own, inputs, w_down))

    planes = [pack] + [shift(pack, "fsdp", steps) for steps in range(1, planes_count)]
    gate_up_far = swap_far({0: gate_up_own})
    gate_up_half = gate_up_far | {2: swap(gate_up_own, "seq", 2)}
    first_slot = seq_index * row_count
    position, padded = layout(
        doc_lengths[0], true_counts[0], first_slot - WINDOW, row_count + WINDOW
    )
    frequency = ROPE_BASE ** (-2.0 * jnp.arange(head_dim // 2, dtype=F32) / head_dim)
    angles = position.astype(F32)[:, None] * frequency
    cosine, sine = jnp.cos(angles), jnp.sin(angles)
    reach = jnp.clip(position[WINDOW:] - padded[WINDOW:], 0, WINDOW - 1)
    lowest = (WINDOW + jnp.arange(row_count, dtype=jnp.int32) - reach)[:, None]
    state = (planes, gate_up_half, cosine, sine, lowest, inputs, w_down)
    planes, gate_up_half, cosine, sine, lowest, inputs, w_down = sync(state)
    pack_rows, gate_up_half, inputs, w_down = sync(
        (place_planes(planes, place), gate_up_half, inputs, w_down)
    )

    rows_far = swap_far({0: pack_rows})
    rows_half = rows_far | {2: swap(pack_rows, "seq", 2)}
    behind = from_behind(inputs, 1)
    gate_up_rels, gate_up_core = core_stack(gate_up_half)
    state = (rows_half, behind, gate_up_half, gate_up_core, w_down)
    rows_half, behind, gate_up_half, gate_up_core, w_down = sync(state)
    rows_rest = {rel ^ 2: swap_both(rows_half, rel) for rel in rows_far if rel}
    half_rels, half_core = core_stack(rows_half)
    tokens3 = [inputs, behind, from_behind(behind, 1)]
    state = (rows_half, rows_rest, half_core, tokens3, gate_up_half, w_down)
    rows_half, rows_rest, half_core, tokens3, gate_up_half, w_down = sync(state)
    rest_rels, rest_core = core_stack(rows_rest)
    rest_core, gate_up_half, w_down = sync((rest_core, gate_up_half, w_down))
    parts = all_parts(rows_half | rows_rest, [(half_rels, half_core), (rest_rels, rest_core)])

    gate_up_rest = {rel ^ 2: swap_both(gate_up_half, rel) for rel in gate_up_far if rel}
    (
        attn_in,
        query_lin,
        key_lin,
        query,
        keys,
        probs,
        attended,
        gains,
        small_gains,
        attn_out,
        middle,
        ffn_in,
    ) = attend(
        place,
        tokens3,
        cosine,
        sine,
        lowest,
        parts,
        head_count,
        head_dim,
        narrow_rows,
        wide_rows,
    )
    ffn_in, gate_up_rest, w_down = sync((ffn_in, gate_up_rest, w_down))

    rest_rels, rest_core = core_stack(gate_up_rest)
    down_far = swap_far({0: w_down})
    down_half = down_far | {2: swap(w_down, "seq", 2)}
    state = (shift(ffn_in, "fsdp", 1), rest_core, down_half)
    block, rest_core, down_half = sync(state)
    cores = [(gate_up_rels, gate_up_core), (rest_rels, rest_core)]
    weights = [all_parts(gate_up_half | gate_up_rest, cores, index) for index in range(2)]
    blocks = [ffn_in, block]
    down_rest = {rel ^ 2: swap_both(down_half, rel) for rel in down_far if rel}
    half_rels, half_core = core_stack(down_half)
    act, gate_slope, up_slope = gate_up(place, blocks[1], weights)
    state = (shift(blocks[1], "fsdp", 1), act, down_rest, half_core)
    block, act, down_rest, half_core = sync(state)
    blocks.append(block)
    rest_rels, rest_core = core_stack(down_rest)
    act, rest_core = sync((act, rest_core))
    weights.append(
        all_parts(down_half | down_rest, [(half_rels, half_core), (rest_rels, rest_core)])
    )
    acts, slopes = {1: act}, {1: (gate_slope, up_slope)}
    partials = {1: sync(down(place, act, weights[2:]))}
    carried = None
    for step in range(2, planes_count + 1):
        state = {}
        if step < planes_count - 1:
            state["block"] = shift(blocks[step], "fsdp", 1)
        leaving = partials[step - 1]
        if carried is not None:
            leaving = add_rounded(leaving, carried)
        index = step % planes_count
        acts[index], gate_slope, up_slope, partials[index] = ffn(place, blocks[index], weights)
        slopes[index] = (gate_slope, up_slope)
        state["carried"] = shift(leaving, "fsdp", 1)
        state, partials = sync((state, partials))
        carried = state["carried"]
        if "block" in state:
            blocks.append(state["block"])
    output, d_ffn_low, grad_fp = turn([partials[0], carried], middle, upstream, gains)

    backs, partials, d_gates, d_ups = [sync(d_ffn_low)], {}, [], []
    carried, down_pair, down_sent = None, None, None
    all_acts = [acts[index] for index in range(planes_count)]
    for step in range(planes_count):
        state = {}
        if step < planes_count - 2:
            state["block"] = shift(backs[step], "fsdp", 1)
        if step == planes_count - 3:
            state["last"] = shift(backs[0], "fsdp", -1)
        if step >= 2:
            leaving = partials[step - 1]
            if carried is not None:
                leaving = add_rounded(leaving, carried)
            state["carried"] = shift(leaving, "fsdp", 1)
        if step == planes_count - 2:
            d_gate, d_up, partials[step], down_pair = ffn_back_and_grad(
                place, backs[step], slopes[step], weights, backs, all_acts
            )
        else:
            d_gate, d_up, partials[step] = ffn_back(place, backs[step], slopes[step], weights)
        if step == planes_count - 1:
            state["down"] = cores_send(down_pair)
        d_gates.append(d_gate)
        d_ups.append(d_up)
        state, partials, d_gates, d_ups, down_pair = sync(
            (state, partials, d_gates, d_ups, down_pair)
        )
        carried = state.get("carried", carried)
        backs += [state[name] for name in ("block", "last") if name in state]
        down_sent = state.get("down")
    carried = shift(add_rounded(partials[planes_count - 1], carried), "fsdp", 1)
    down_part = add_rounded(*down_sent)
    down_terms = [down_part[0]] + straight(down_part, 1, 2)
    gate_pair, up_pair = weight_grad(place, blocks, d_gates, d_ups)
    carried, gate_pair, up_pair, down_terms, down_part = sync(
        (carried, gate_pair, up_pair, down_terms, down_part)
    )

    gate_sent, up_sent = cores_send(gate_pair), cores_send(up_pair)
    down_terms += straight(down_part, *range(3, down_part.shape[0]))
    saved = (middle, upstream, attn_out, gains, query, keys, probs)
    d_middle, d_attn, d_rotated, far_halo, back_halo, near, gain_rows = attend_back(
        place, [partials[0], carried], saved, parts, head_count
    )
    state = (far_halo, back_halo, d_attn, d_rotated, gate_sent, up_sent, down_terms)
    far_halo, back_halo, d_attn, d_rotated, gate_sent, up_sent, down_terms = sync(state)
    halos = [from_behind(back_halo, -1), from_behind(far_halo, -2)]
    gate_part, up_part = add_rounded(*gate_sent), add_rounded(*up_sent)
    quarter = up_part.shape[0] // 2
    gate_columns = gate_part.reshape((-1, 2) + gate_part.shape[1:])
    gate_second = far_step(gate_columns[:, 1])
    up_second = across_step(up_part[quarter:])
    ins = [d_attn, attended, attn_in, d_rotated, query_lin, small_gains, cosine, sine]
    *head_grads, d_in, query_gain_grad = heads_back(place, ins, parts, head_count)
    state = (halos, head_grads, gate_columns, gate_second, up_part, up_second)
    halos, head_grads, gate_columns, gate_second, up_part, up_second = sync(state)
    head_sent = cores_send(head_grads)
    gate_first = far_step(gate_columns[:, 0])
    up_first = across_step(up_part[:quarter])
    ins = [
        near,
        *halos,
        key_lin,
        small_gains,
        gains,
        cosine,
        sine,
        attn_in,
        inputs,
        d_middle,
        d_in,
        gain_rows,
        grad_fp,
        query_gain_grad,
    ]
    *last_grads, input_grad = finish(place, ins, parts, narrow_rows, wide_rows)
    state = (last_grads, head_sent, gate_first, gate_second, up_first, up_second)
    last_grads, head_sent, gate_first, gate_second, up_first, up_second = sync(state)
    last_sent = cores_send(last_grads)
    head_part = add_rounded(*head_sent)
    out_sides = far_step(head_part[0])
    query_sides = across_step(head_part[1])
    gate_came = swap(add_rounded(*gate_second)[0], "seq", 2)
    up_sides = far_step(jnp.concatenate([add_rounded(*up_first), add_rounded(*up_second)], axis=0))
    state = (last_sent, out_sides, query_sides, gate_came, gate_first, up_sides)
    last_sent, out_sides, query_sides, gate_came, gate_first, up_sides = sync(state)
    out_part = add_rounded(*out_sides)
    out_came = swap(out_part[1], "seq", 2)
    query_sides = far_step(add_rounded(*query_sides))
    last_part = add_rounded(*last_sent)
    last_terms = [last_part[0]] + straight(last_part, *range(1, last_part.shape[0]))
    state = (out_part, out_came, query_sides, last_terms)
    out_part, out_came, query_sides, last_terms = sync(state)
    grad_gate = add_up([add_up(gate_first)[0], gate_came])
    grad_up = add_up(up_sides)[0]
    reduced = jnp.concatenate(
        [
            add_rounded(out_part[0], out_came),
            add_rounded(*query_sides)[0],
            add_up(last_terms).astype(BF16),
        ],
        axis=1,
    )
    rows = add_up(planes_send(reduced))
    last_start = 2 * heads_width
    gain_cols = rows[:, last_start + 2 * head_dim :]
    return (
        output[None],
        input_grad[None],
        rows[:, heads_width:last_start],
        rows[:, last_start : last_start + head_dim],
        rows[:, last_start + head_dim : last_start + 2 * head_dim],
        rows[:, :heads_width],
        grad_gate,
        grad_up,
        add_up(down_terms),
        gain_cols[:, 0],
        gain_cols[:narrow_rows, 4],
        gain_cols[:narrow_rows, 5],
        gain_cols[:, 1],
        gain_cols[:, 2],
        gain_cols[:, 3],
    )


def solution(mesh):
    rows = P("fsdp", "seq", None)
    shard, tile, vector = P(("seq", "fsdp"), None), P("seq", "fsdp"), P(("seq", "fsdp"))
    groups = P("fsdp", None)
    return jax.shard_map(
        on_device,
        mesh=mesh,
        in_specs=(rows, rows, groups, groups) + (shard,) * 4 + (tile,) * 3 + (vector,) * 6,
        out_specs=(rows, rows) + (shard,) * 4 + (tile,) * 3 + (vector,) * 6,
        check_vma=False,
    )
```

```python
import functools

import jax
import jax.numpy as jnp
from jax import lax
from jax.experimental import pallas as pl
from jax.experimental.pallas import tpu as pltpu
from jax.sharding import PartitionSpec as P

WINDOW = 512
NORM_EPS = 1e-06
ROPE_BASE = 10000.0
NEGATIVE = -1e30
LANES = 128
VMEM_LIMIT = 56 * 2**20
PIECES = 8
BF16 = jnp.bfloat16
F32 = jnp.float32


def from_behind(value, steps):
    count = lax.axis_size("seq")
    first, last = (max(0, -steps), min(count, count - steps))
    return lax.ppermute(value, "seq", [(source, source + steps) for source in range(first, last)])


def seq_masks():
    return [1 << bit for bit in range(lax.axis_size("seq").bit_length() - 1)]


def swap(value, axis, mask):
    count = lax.axis_size(axis)
    return lax.ppermute(value, axis, [(source, source ^ mask) for source in range(count)])


def shift(value, axis, steps):
    count = lax.axis_size(axis)
    return lax.ppermute(value, axis, [(source, (source + steps) % count) for source in range(count)])


def sync(state):
    return lax.optimization_barrier(state)


class Parts:
    def __init__(self, arrays, where):
        self.arrays, self.where = list(arrays), tuple(where)
        self.width = arrays[0].shape[-1]
        self.rows = arrays[0].shape[-2] * len(where)


def core_stack(parts):
    stack = jnp.stack(list(parts.values())) if len(parts) > 1 else list(parts.values())[0][None]
    return tuple(parts), swap(stack, "seq", 1)


def with_cores(entries, cores):
    for rels, stack in cores:
        entries = entries | {rel ^ 1: (stack, (index,)) for index, rel in enumerate(rels)}
    return entries


def all_parts(entries):
    arrays, places = [], []
    for rel in range(len(entries)):
        array, index = entries[rel]
        number = next((n for n, other in enumerate(arrays) if other is array), len(arrays))
        if number == len(arrays):
            arrays.append(array)
        places.append((number, index))
    if arrays[0].shape[-2] % 16 == 0:
        return Parts(arrays, places)
    index = jnp.arange(len(places), dtype=jnp.int32) ^ lax.axis_index("seq")
    blocks = [arrays[number][block] for number, block in places]
    whole = jnp.take(jnp.stack(blocks), index, axis=0, mode="clip")
    return Parts([whole.reshape(-1, whole.shape[-1])], [(0, ())])


def plain(parts):
    return {rel: (part, ()) for rel, part in parts.items()}


def add_rounded(first, second):
    return (first.astype(F32) + second.astype(F32)).astype(BF16)


def cut(pair, count):
    if len(pair) == 2:
        return pair
    whole = pair[0]
    index = jnp.arange(count, dtype=jnp.int32) ^ lax.axis_index("seq")
    blocks = whole.reshape(whole.shape[:-2] + (count, -1, whole.shape[-1]))
    blocks = jnp.take(blocks, index, axis=blocks.ndim - 3, mode="clip")
    return blocks[..., 0::2, :, :], blocks[..., 1::2, :, :]


def cores_send(pair):
    keep, send = cut(pair, lax.axis_size("seq"))
    return keep, swap(send, "seq", 1)


def far_step(part):
    masks = [mask for mask in seq_masks() if mask > 2][::-1]
    for mask in masks[:-1]:
        half = part.shape[0] // 2
        part = add_rounded(part[:half], swap(part[half:], "seq", mask))
    half = part.shape[0] // 2
    return part[:half], swap(part[half:], "seq", masks[-1])


def across_step(part):
    part = part.reshape((-1, 2) + part.shape[1:])
    return part[:, 0], swap(part[:, 1], "seq", 2)


def straight(part, *steps):
    return [swap(part[step], "seq", 2 * step) for step in steps]


def planes_send(rows):
    planes = lax.axis_size("fsdp")
    blocks = rows.reshape((planes, -1) + rows.shape[1:])
    mine = lax.axis_index("fsdp")
    sent = [lax.dynamic_index_in_dim(blocks, mine, 0, keepdims=False)]
    for steps in range(1, planes):
        send = lax.dynamic_index_in_dim(blocks, (mine + steps) % planes, 0, keepdims=False)
        sent.append(shift(send, "fsdp", steps))
    return sent


def add_up(terms):
    total = terms[0].astype(F32)
    for term in terms[1:]:
        total = total + term.astype(F32)
    return total


def dot(left, right):
    return jnp.dot(left, right, preferred_element_type=F32)


def dot_t(left, right):
    return lax.dot_general(left, right, (((1,), (1,)), ((), ())), preferred_element_type=F32)


def dot_tn(left, right):
    return lax.dot_general(left, right, (((0,), (0,)), ((), ())), preferred_element_type=F32)


def inverse_rms(values):
    return lax.rsqrt(jnp.mean(values * values, axis=-1, keepdims=True) + NORM_EPS)


def norm_back(normed, scale, gain, upstream):
    scaled = upstream * gain
    back = scale * (scaled - normed * jnp.mean(scaled * normed, axis=-1, keepdims=True))
    return back, jnp.sum(upstream * normed, axis=0, keepdims=True)


def rotate(values, cosine, sine):
    half = values.shape[-1] // 2
    first, second = values[:, :half], values[:, half:]
    return jnp.concatenate(
        [first * cosine - second * sine, second * cosine + first * sine], axis=-1
    )


def iota(shape, dim):
    return lax.broadcasted_iota(jnp.int32, shape, dim)


def unit(shape, hits):
    return jnp.where(hits, 1.0, 0.0).astype(BF16)


def spread_matrix(narrow, wide, narrow_rows, wide_rows):
    row, col = iota((narrow, wide), 0), iota((narrow, wide), 1)
    return unit((narrow, wide), col == (row // narrow_rows) * wide_rows + row % narrow_rows)


def tiles_of(width, step):
    return [(start, min(step, width - start)) for start in range(0, width, step)]


def slots(where):
    return max(PIECES, len(where))


def start_placing(where, refs, dest, sems, base, seq, lane=0, lanes=None):
    copies = []
    if len(where) == 1:
        whole = refs[0] if lanes is None else refs[0].at[:, pl.ds(lane, lanes)]
        count = PIECES if whole.shape[0] % (16 * PIECES) == 0 else 1
        rows = whole.shape[0] // count
        pieces = [(index * rows, whole.at[pl.ds(index * rows, rows), :]) for index in range(count)]
        copies = [
            pltpu.make_async_copy(part, dest.at[pl.ds(start, rows), :], sems.at[base + index])
            for index, (start, part) in enumerate(pieces)
        ]
        for copy in copies:
            copy.start()
        return copies
    for rel, (number, block) in enumerate(where):
        part = refs[number].at[block] if block else refs[number]
        rows = part.shape[0]
        start = pl.multiple_of((seq ^ rel) * rows, 16) if len(where) > 1 else 0
        if lanes is not None:
            part = part.at[:, pl.ds(lane, lanes)]
        copies.append(
            pltpu.make_async_copy(part, dest.at[pl.ds(start, rows), :], sems.at[base + rel])
        )
    for copy in copies:
        copy.start()
    return copies


def start_cutting(whole, outs, sems, base, seq, which=None):
    if which is not None:
        outs = [out.at[which] for out in outs]
    if len(outs) == 1:
        copies = [pltpu.make_async_copy(whole, outs[0], sems.at[base])]
    else:
        half, rows = outs[0].shape[0], outs[0].shape[1]
        copies = []
        for rel in range(2 * half):
            start = pl.multiple_of((seq ^ rel) * rows, 16)
            copies.append(
                pltpu.make_async_copy(
                    whole.at[pl.ds(start, rows), :], outs[rel % 2].at[rel // 2], sems.at[base + rel]
                )
            )
    for copy in copies:
        copy.start()
    return copies


def cut_shapes(height, width, count):
    rows = height // count
    if rows % 16:
        return [jax.ShapeDtypeStruct((height, width), BF16)]
    return [jax.ShapeDtypeStruct((count // 2, rows, width), BF16)] * 2


def wait_all(copies):
    for copy in copies:
        copy.wait()


SMEM_SPEC = pl.BlockSpec(memory_space=pltpu.SMEM)
VMEM_SPEC = pl.BlockSpec(memory_space=pltpu.VMEM)
ANY_SPEC = pl.BlockSpec(memory_space=pl.ANY)


def call(kernel, outs, out_specs, ins, in_specs, scratch=(), flops=0, moved=0, exps=0):
    return pl.pallas_call(
        kernel,
        out_shape=tuple(outs),
        in_specs=list(in_specs),
        out_specs=tuple(out_specs),
        scratch_shapes=list(scratch),
        compiler_params=pltpu.CompilerParams(vmem_limit_bytes=VMEM_LIMIT),
        cost_estimate=pl.CostEstimate(flops=flops, bytes_accessed=moved, transcendentals=exps),
    )(*ins)


def shape_of(dims, dtype):
    return jax.ShapeDtypeStruct(dims, dtype)


def pack_kernel(wq_ref, wk_ref, wv_ref, wo_ref, *refs):
    wide, narrow, out_ref = refs[:4], refs[4:6], refs[6]
    rows, heads_width, head_dim = wq_ref.shape[0], wq_ref.shape[1], wk_ref.shape[1]
    out_ref[:, :heads_width] = wq_ref[...]
    out_ref[:, heads_width : heads_width + head_dim] = wk_ref[...]
    out_ref[:, heads_width + head_dim : heads_width + 2 * head_dim] = wv_ref[...]
    row = iota((16, rows), 0)
    held = jnp.zeros((16, rows), F32)
    for index, ref in enumerate(wide):
        held = held + jnp.where(row == index, ref[...].astype(F32), 0.0)
    small = narrow[0].shape[1]
    fit = unit((small, rows), iota((small, rows), 0) == iota((small, rows), 1))
    for index, ref in enumerate(narrow):
        spread = dot(jnp.broadcast_to(ref[...].astype(F32), (16, small)).astype(BF16), fit)
        held = held + jnp.where(row == 4 + index, spread, 0.0)
    place = unit((16, LANES), iota((16, LANES), 0) == iota((16, LANES), 1))
    gain_start = heads_width + 2 * head_dim
    out_ref[:, gain_start : gain_start + LANES] = dot_tn(held.astype(BF16), place).astype(BF16)
    out_ref[:, gain_start + LANES :] = wo_ref[...]


def pack_attn(w_query, w_key, w_value, w_out, wide, narrow):
    rows = w_query.shape[0]
    width = 2 * w_query.shape[1] + 2 * w_key.shape[1] + LANES
    ins = [w_query, w_key, w_value, w_out] + [vec.reshape(1, -1) for vec in wide + narrow]
    return call(
        pack_kernel,
        [shape_of((rows, width), BF16)],
        [VMEM_SPEC],
        ins,
        [VMEM_SPEC] * len(ins),
    )[0]


def planes_kernel(place_ref, *refs):
    parts, out_ref = refs[:-1], refs[-1]
    count, rows = len(parts), parts[0].shape[0]
    total = None
    for steps, part in enumerate(parts):
        plane = lax.rem(place_ref[1] - steps + count, count)
        row, col = iota((count * rows, rows), 0), iota((count * rows, rows), 1)
        term = dot(unit((count * rows, rows), row == col + plane * rows), part[...])
        total = term if total is None else total + term
    out_ref[...] = total.astype(BF16)


def place_planes(parts, place):
    count = len(parts)
    rows, width = parts[0].shape
    return call(
        planes_kernel,
        [shape_of((count * rows, width), BF16)],
        [VMEM_SPEC],
        [place] + parts,
        [SMEM_SPEC] + [VMEM_SPEC] * count,
        flops=2 * count * count * rows * rows * width,
        moved=4 * count * rows * width,
    )[0]


def attend_kernel(
    where,
    ref_count,
    narrow_rows,
    wide_rows,
    head_count,
    place_ref,
    near_ref,
    back_ref,
    far_ref,
    cos_ref,
    sin_ref,
    low_ref,
    *refs,
):
    parts, refs = refs[:ref_count], refs[ref_count:]
    (
        attn_in_ref,
        query_lin_ref,
        key_lin_ref,
        query_ref,
        keys_ref,
        probs_ref,
        attended_ref,
        gains_ref,
        small_gains_ref,
        attn_out_ref,
        middle_ref,
        ffn_in_ref,
    ) = refs[:12]
    weights, inside, sems = refs[12:]
    copies = start_placing(where, parts, weights, sems, 0, place_ref[0])
    rows, width = near_ref.shape
    head_dim = key_lin_ref.shape[1]
    heads_width = head_count * head_dim
    score_scale = head_dim**-0.5
    blocks = [far_ref, back_ref, near_ref]
    scales = []
    for ref in blocks:
        scales.append(inverse_rms(ref[...].astype(F32)))
    wait_all(copies)
    gain_start = heads_width + 2 * head_dim
    gain_cols = weights[:, gain_start : gain_start + LANES]
    pick = unit((8, LANES), iota((8, LANES), 0) == iota((8, LANES), 1))
    gains = dot_t(pick, gain_cols)
    spread = spread_matrix(head_dim, width, narrow_rows, wide_rows)
    small_gains = dot_t(gains.astype(BF16), spread)
    gains_ref[...] = gains
    small_gains_ref[...] = small_gains
    gain_an, gain_q, gain_k = gains[0:1], small_gains[4:5], small_gains[5:6]
    for index, ref in enumerate(blocks):
        normed = ref[...].astype(F32) * scales[index] * gain_an
        inside[index * rows : (index + 1) * rows, :] = normed.astype(BF16)
    attn_in_ref[...] = inside[2 * rows :, :]
    for index in range(3):
        span = slice(index * rows, (index + 1) * rows)
        part_in = inside[span, :]
        key_lin = dot(part_in, weights[:, heads_width : heads_width + head_dim])
        value = dot(part_in, weights[:, heads_width + head_dim : heads_width + 2 * head_dim])
        key = rotate(key_lin * inverse_rms(key_lin) * gain_k, cos_ref[span, :], sin_ref[span, :])
        keys_ref[span, :head_dim] = key.astype(BF16)
        keys_ref[span, head_dim:] = value.astype(BF16)
        if index == 2:
            key_lin_ref[...] = key_lin
    cosine, sine = cos_ref[2 * rows :, :], sin_ref[2 * rows :, :]
    column = iota((rows, 3 * rows), 1)
    seen = (column >= low_ref[:, :1]) & (column <= iota((rows, 3 * rows), 0) + 2 * rows)
    for head in range(head_count):
        lanes = slice(head * head_dim, (head + 1) * head_dim)
        query_lin = dot(inside[2 * rows :, :], weights[:, lanes])
        query_lin_ref[:, lanes] = query_lin
        query = rotate(query_lin * inverse_rms(query_lin) * gain_q, cosine, sine).astype(BF16)
        query_ref[:, lanes] = query
        scores = jnp.where(seen, dot_t(query, keys_ref[:, :head_dim]) * score_scale, NEGATIVE)
        raised = jnp.exp(scores - jnp.max(scores, axis=-1, keepdims=True))
        probs = (raised / jnp.sum(raised, axis=-1, keepdims=True)).astype(BF16)
        probs_ref[head * rows : (head + 1) * rows, :] = probs
        attended_ref[:, lanes] = dot(probs, keys_ref[:, head_dim:]).astype(BF16)
    for start, size in tiles_of(width, 384):
        attn_out_ref[:, start : start + size] = dot_t(
            attended_ref[...], weights[start : start + size, gain_start + LANES :]
        )
    attn_out = attn_out_ref[...]
    middle = near_ref[...].astype(F32) + attn_out * inverse_rms(attn_out) * gains[1:2]
    middle_ref[...] = middle
    ffn_in_ref[...] = (middle * inverse_rms(middle) * gains[2:3]).astype(BF16)


def attend(place, tokens3, cosine, sine, lowest, parts, head_count, head_dim, narrow_rows, wide_rows):
    rows, width = tokens3[0].shape
    heads_width = head_count * head_dim
    pack = parts.width
    outs = [
        shape_of((rows, width), BF16),
        shape_of((rows, heads_width), F32),
        shape_of((rows, head_dim), F32),
        shape_of((rows, heads_width), BF16),
        shape_of((3 * rows, 2 * head_dim), BF16),
        shape_of((head_count * rows, 3 * rows), BF16),
        shape_of((rows, heads_width), BF16),
        shape_of((8, width), F32),
        shape_of((8, head_dim), F32),
        shape_of((rows, width), F32),
        shape_of((rows, width), F32),
        shape_of((rows, width), BF16),
    ]
    return call(
        functools.partial(
            attend_kernel, parts.where, len(parts.arrays), narrow_rows, wide_rows, head_count
        ),
        outs,
        [VMEM_SPEC] * len(outs),
        [place] + list(tokens3) + [cosine, sine, lowest] + parts.arrays,
        [SMEM_SPEC] + [VMEM_SPEC] * 6 + [ANY_SPEC] * len(parts.arrays),
        [
            pltpu.VMEM((width, pack), BF16),
            pltpu.VMEM((3 * rows, width), BF16),
            pltpu.SemaphoreType.DMA((slots(parts.where),)),
        ],
        flops=2 * rows * width * (heads_width + 6 * head_dim) + 12 * rows * rows * heads_width,
        moved=2 * width * pack + 16 * rows * width,
        exps=3 * head_count * rows * rows,
    )


def gelu_pair(gate):
    square = gate * gate
    tanh = jnp.tanh(gate * (0.7978845608028654 + 0.035677408136300125 * square))
    half = 0.5 + 0.5 * tanh
    value = gate * half
    slope = half + value * (1.0 - tanh) * (0.7978845608028654 + 0.10703222440890037 * square)
    return value, slope


def take_parts(wheres, counts, refs):
    parts = []
    for count in counts:
        parts.append(refs[:count])
        refs = refs[count:]
    bases = [sum(slots(where) for where in wheres[:index]) for index in range(len(wheres))]
    return parts, bases, refs


def parts_of(weights):
    wheres = tuple(parts.where for parts in weights)
    counts = tuple(len(parts.arrays) for parts in weights)
    arrays = [array for parts in weights for array in parts.arrays]
    return wheres, counts, arrays, sum(slots(where) for where in wheres)


def gate_up_body(rows_ref, gate_w, up_w, act_ref, gate_slope_ref, up_slope_ref):
    rows_in = rows_ref[...]
    for start, size in tiles_of(gate_w.shape[1], 256):
        lanes = slice(start, start + size)
        gate = dot(rows_in, gate_w[:, lanes])
        up = dot(rows_in, up_w[:, lanes])
        value, slope = gelu_pair(gate)
        act_ref[:, lanes] = (value * up).astype(BF16)
        gate_slope_ref[:, lanes] = (slope * up).astype(BF16)
        up_slope_ref[:, lanes] = value.astype(BF16)


def down_body(act_ref, down_w, out_ref):
    for start, size in tiles_of(down_w.shape[0], 384):
        lanes = slice(start, start + size)
        out_ref[:, lanes] = dot_t(act_ref[...], down_w[lanes, :]).astype(BF16)


def ffn_kernel(wheres, counts, place_ref, rows_ref, *refs):
    parts, bases, refs = take_parts(wheres, counts, refs)
    act_ref, gate_slope_ref, up_slope_ref, out_ref, gate_w, up_w, down_w, sems = refs
    seq = place_ref[0]
    copies = start_placing(wheres[0], parts[0], gate_w, sems, bases[0], seq)
    copies += start_placing(wheres[1], parts[1], up_w, sems, bases[1], seq)
    later = start_placing(wheres[2], parts[2], down_w, sems, bases[2], seq)
    wait_all(copies)
    gate_up_body(rows_ref, gate_w, up_w, act_ref, gate_slope_ref, up_slope_ref)
    wait_all(later)
    down_body(act_ref, down_w, out_ref)


def gate_up_kernel(wheres, counts, place_ref, rows_ref, *refs):
    parts, bases, refs = take_parts(wheres, counts, refs)
    act_ref, gate_slope_ref, up_slope_ref, gate_w, up_w, sems = refs
    seq = place_ref[0]
    copies = start_placing(wheres[0], parts[0], gate_w, sems, bases[0], seq)
    copies += start_placing(wheres[1], parts[1], up_w, sems, bases[1], seq)
    wait_all(copies)
    gate_up_body(rows_ref, gate_w, up_w, act_ref, gate_slope_ref, up_slope_ref)


def gate_up(place, rows_in, weights):
    rows, width = rows_in.shape
    hidden = weights[0].width
    wheres, counts, arrays, sem_count = parts_of(weights)
    return call(
        functools.partial(gate_up_kernel, wheres, counts),
        [shape_of((rows, hidden), BF16)] * 3,
        [VMEM_SPEC] * 3,
        [place, rows_in] + arrays,
        [SMEM_SPEC, VMEM_SPEC] + [ANY_SPEC] * len(arrays),
        [pltpu.VMEM((width, hidden), BF16)] * 2 + [pltpu.SemaphoreType.DMA((sem_count,))],
        flops=4 * rows * hidden * width,
        moved=4 * width * hidden + 6 * rows * hidden,
    )


def down_kernel(wheres, counts, place_ref, act_ref, *refs):
    parts, bases, refs = take_parts(wheres, counts, refs)
    out_ref, down_w, sems = refs
    wait_all(start_placing(wheres[0], parts[0], down_w, sems, bases[0], place_ref[0]))
    down_body(act_ref, down_w, out_ref)


def down(place, act, weights):
    rows, hidden = act.shape
    width = weights[0].rows
    wheres, counts, arrays, sem_count = parts_of(weights)
    return call(
        functools.partial(down_kernel, wheres, counts),
        [shape_of((rows, width), BF16)],
        [VMEM_SPEC],
        [place, act] + arrays,
        [SMEM_SPEC, VMEM_SPEC] + [ANY_SPEC] * len(arrays),
        [pltpu.VMEM((width, hidden), BF16), pltpu.SemaphoreType.DMA((sem_count,))],
        flops=2 * rows * hidden * width,
        moved=2 * width * hidden + 2 * rows * hidden,
    )[0]


def ffn(place, rows_in, weights):
    rows, width = rows_in.shape
    hidden = weights[0].width
    wheres, counts, arrays, sem_count = parts_of(weights)
    return call(
        functools.partial(ffn_kernel, wheres, counts),
        [shape_of((rows, hidden), BF16)] * 3 + [shape_of((rows, width), BF16)],
        [VMEM_SPEC] * 4,
        [place, rows_in] + arrays,
        [SMEM_SPEC, VMEM_SPEC] + [ANY_SPEC] * len(arrays),
        [pltpu.VMEM((width, hidden), BF16)] * 3 + [pltpu.SemaphoreType.DMA((sem_count,))],
        flops=6 * rows * hidden * width,
        moved=6 * width * hidden + 8 * rows * hidden,
    )


def turn_kernel(own_ref, came_ref, middle_ref, upstream_ref, gains_ref, *outs):
    output_ref, back_ref, gain_grad_ref = outs
    total = own_ref[...].astype(F32) + came_ref[...].astype(F32)
    scale = inverse_rms(total)
    normed = total * scale
    gain = gains_ref[3:4, :]
    output_ref[...] = (middle_ref[...] + normed * gain).astype(BF16)
    back, gain_grad = norm_back(normed, scale, gain, upstream_ref[...].astype(F32))
    back_ref[...] = back.astype(BF16)
    gain_grad_ref[...] = gain_grad


def turn(sums, middle, upstream, gains):
    rows, width = middle.shape
    return call(
        turn_kernel,
        [shape_of((rows, width), BF16), shape_of((rows, width), BF16), shape_of((1, width), F32)],
        [VMEM_SPEC] * 3,
        list(sums) + [middle, upstream, gains],
        [VMEM_SPEC] * 5,
        moved=20 * rows * width,
    )


def ffn_back_kernel(
    wheres, counts, place_ref, back_ref, gate_slope_ref, up_slope_ref, *refs
):
    parts, bases, refs = take_parts(wheres, counts, refs)
    d_gate_ref, d_up_ref, out_ref, gate_w, up_w, down_w, sems = refs
    seq = place_ref[0]
    copies = start_placing(wheres[2], parts[2], down_w, sems, bases[2], seq)
    later = start_placing(wheres[0], parts[0], gate_w, sems, bases[0], seq)
    later += start_placing(wheres[1], parts[1], up_w, sems, bases[1], seq)
    wait_all(copies)
    back = back_ref[...]
    for start, size in tiles_of(down_w.shape[1], 256):
        lanes = slice(start, start + size)
        d_act = dot(back, down_w[:, lanes])
        d_gate_ref[:, lanes] = (d_act * gate_slope_ref[:, lanes].astype(F32)).astype(BF16)
        d_up_ref[:, lanes] = (d_act * up_slope_ref[:, lanes].astype(F32)).astype(BF16)
    wait_all(later)
    for start, size in tiles_of(gate_w.shape[0], 384):
        lanes = slice(start, start + size)
        total = dot_t(d_gate_ref[...], gate_w[lanes, :])
        out_ref[:, lanes] = (total + dot_t(d_up_ref[...], up_w[lanes, :])).astype(BF16)


def ffn_back(place, back, slopes, weights):
    rows, width = back.shape
    hidden = weights[0].width
    wheres, counts, arrays, sem_count = parts_of(weights)
    return call(
        functools.partial(ffn_back_kernel, wheres, counts),
        [shape_of((rows, hidden), BF16)] * 2 + [shape_of((rows, width), BF16)],
        [VMEM_SPEC] * 3,
        [place, back] + list(slopes) + arrays,
        [SMEM_SPEC] + [VMEM_SPEC] * 3 + [ANY_SPEC] * len(arrays),
        [pltpu.VMEM((width, hidden), BF16)] * 3 + [pltpu.SemaphoreType.DMA((sem_count,))],
        flops=6 * rows * hidden * width,
        moved=6 * width * hidden + 12 * rows * hidden,
    )


def ffn_back_and_grad_kernel(in_counts, out_count, back_kernel, grad_kernel, place_ref, *refs):
    back_ins, refs = refs[: in_counts[0]], refs[in_counts[0] :]
    grad_ins, refs = refs[: in_counts[1]], refs[in_counts[1] :]
    back_outs, refs = refs[:3], refs[3:]
    grad_outs, refs = refs[:out_count], refs[out_count:]
    back_kernel(place_ref, *back_ins, *back_outs, *refs[:4])
    grad_kernel(place_ref, *grad_ins, *grad_outs, *refs[4:])


def ffn_back_and_grad(place, back, slopes, weights, lefts, rights):
    rows, width = back.shape
    hidden = weights[0].width
    wheres, counts, arrays, sem_count = parts_of(weights)
    count = lax.axis_size("seq")
    cuts = cut_shapes(width, hidden, count)
    all_rows = sum(piece.shape[0] for piece in lefts)
    grad_ins = list(lefts) + list(rights)
    back_ins = [back] + list(slopes) + arrays
    outs = call(
        functools.partial(
            ffn_back_and_grad_kernel,
            (len(back_ins), len(grad_ins)),
            len(cuts),
            functools.partial(ffn_back_kernel, wheres, counts),
            functools.partial(weight_grad_kernel, len(lefts), (len(rights),), len(cuts)),
        ),
        [shape_of((rows, hidden), BF16)] * 2 + [shape_of((rows, width), BF16)] + cuts,
        [VMEM_SPEC] * 3 + [ANY_SPEC] * len(cuts),
        [place] + back_ins + grad_ins,
        [SMEM_SPEC] + [VMEM_SPEC] * 3 + [ANY_SPEC] * (len(arrays) + len(grad_ins)),
        [pltpu.VMEM((width, hidden), BF16)] * 3
        + [pltpu.SemaphoreType.DMA((sem_count,))]
        + weight_grad_scratch(all_rows, width, hidden, len(lefts), [len(rights)], count),
        flops=2 * all_rows * width * hidden + 6 * rows * width * hidden,
        moved=8 * width * hidden,
    )
    return outs[0], outs[1], outs[2], outs[3:]


def weight_grad_scratch(rows, height, width, left_count, right_counts, count):
    sides, pieces = len(right_counts), sum(right_counts)
    tiles = len(tiles_of(width, 512))
    return [
        pltpu.VMEM((rows, height), BF16),
        pltpu.VMEM((sides, rows, width), BF16),
        pltpu.VMEM((sides, height, width), BF16),
        pltpu.SemaphoreType.DMA((left_count + tiles * pieces,)),
        pltpu.SemaphoreType.DMA((sides, count)),
    ]


def weight_grad_kernel(left_count, right_counts, out_count, place_ref, *refs):
    lefts, refs = refs[:left_count], refs[left_count:]
    rights = []
    for count in right_counts:
        rights.append(refs[:count])
        refs = refs[count:]
    outs, (left, right, whole, sems, out_sems) = refs[:-5], refs[-5:]
    number = 0

    def fetch(pieces, dest, *lanes):
        nonlocal number
        copies, start = [], 0
        for piece in pieces:
            rows = piece.shape[0]
            source = piece.at[:, lanes[0]] if lanes else piece
            target = dest.at[(pl.ds(start, rows),) + lanes]
            copies.append(pltpu.make_async_copy(source, target, sems.at[number]))
            number += 1
            start += rows
        for copy in copies:
            copy.start()
        return copies

    tiles = tiles_of(whole.shape[-1], 512)
    first = fetch(lefts, left)
    waits = [
        [fetch(pieces, right.at[index], pl.ds(lane, size)) for lane, size in tiles]
        for index, pieces in enumerate(rights)
    ]
    wait_all(first)
    cuts = []
    for index, pieces in enumerate(rights):
        for copies, (lane, size) in zip(waits[index], tiles):
            wait_all(copies)
            lanes = slice(lane, lane + size)
            whole[index, :, lanes] = dot_tn(left[...], right[index, :, lanes]).astype(BF16)
        cuts += start_cutting(
            whole.at[index],
            outs[index * out_count : (index + 1) * out_count],
            out_sems.at[index],
            0,
            place_ref[0],
        )
    wait_all(cuts)


def weight_grad(place, lefts, *rights):
    height, width = lefts[0].shape[1], rights[0][0].shape[1]
    rows = sum(piece.shape[0] for piece in lefts)
    count = lax.axis_size("seq")
    cuts = cut_shapes(height, width, count)
    pieces = [piece for side in rights for piece in side]
    sides = [len(side) for side in rights]
    outs = call(
        functools.partial(
            weight_grad_kernel, len(lefts), tuple(len(side) for side in rights), len(cuts)
        ),
        cuts * len(rights),
        [ANY_SPEC] * (len(cuts) * len(rights)),
        [place] + list(lefts) + pieces,
        [SMEM_SPEC] + [ANY_SPEC] * (len(lefts) + len(pieces)),
        weight_grad_scratch(rows, height, width, len(lefts), sides, count),
        flops=2 * rows * height * width * len(rights),
        moved=2 * (rows * (height + width) + height * width) * len(rights),
    )
    return [outs[start : start + len(cuts)] for start in range(0, len(outs), len(cuts))]


def attend_back_kernel(
    where,
    ref_count,
    head_count,
    place_ref,
    own_ref,
    came_ref,
    middle_ref,
    upstream_ref,
    attn_out_ref,
    gains_ref,
    query_ref,
    keys_ref,
    probs_ref,
    *refs,
):
    parts, refs = refs[:ref_count], refs[ref_count:]
    d_middle_ref, d_attn_ref, d_rotated_ref, far_halo_ref, back_halo_ref, near_ref, rows_ref = refs[:7]
    weights, d_keys, sems = refs[7:]
    rows, width = middle_ref.shape
    head_dim = keys_ref.shape[1] // 2
    heads_width = head_count * head_dim
    score_scale = head_dim**-0.5
    out_start = parts[0].shape[-1] - heads_width
    copies = start_placing(where, parts, weights, sems, 0, place_ref[0], out_start, heads_width)
    total = own_ref[...].astype(F32) + came_ref[...].astype(F32)
    middle = middle_ref[...]
    scale = inverse_rms(middle)
    back, grad_fn = norm_back(middle * scale, scale, gains_ref[2:3, :], total)
    d_middle = upstream_ref[...].astype(F32) + back
    d_middle_ref[...] = d_middle
    attn_out = attn_out_ref[...]
    scale = inverse_rms(attn_out)
    d_attn_out, grad_ap = norm_back(attn_out * scale, scale, gains_ref[1:2, :], d_middle)
    row = iota((8, width), 0)
    rows_ref[...] = jnp.where(row == 1, grad_ap, 0.0) + jnp.where(row == 2, grad_fn, 0.0)
    d_attn_low = d_attn_out.astype(BF16)
    d_attn_ref[...] = d_attn_low
    wait_all(copies)
    for head in range(head_count):
        lanes = slice(head * head_dim, (head + 1) * head_dim)
        d_attended = dot(d_attn_low, weights[:, lanes]).astype(BF16)
        probs_low = probs_ref[head * rows : (head + 1) * rows, :]
        probs = probs_low.astype(F32)
        d_probs = dot_t(d_attended, keys_ref[:, head_dim:])
        delta = jnp.sum(probs * d_probs, axis=-1, keepdims=True)
        d_scores = (probs * (d_probs - delta) * score_scale).astype(BF16)
        d_rotated_ref[:, lanes] = dot(d_scores, keys_ref[:, :head_dim])
        d_key = dot_tn(d_scores, query_ref[:, lanes])
        d_value = dot_tn(probs_low, d_attended)
        if head == 0:
            d_keys[:, :head_dim] = d_key
            d_keys[:, head_dim:] = d_value
        else:
            d_keys[:, :head_dim] += d_key
            d_keys[:, head_dim:] += d_value
    far_halo_ref[...] = d_keys[:rows, :].astype(BF16)
    back_halo_ref[...] = d_keys[rows : 2 * rows, :].astype(BF16)
    near_ref[...] = d_keys[2 * rows :, :]


def attend_back(place, sums, saved, parts, head_count):
    middle, upstream, attn_out, gains, query, keys, probs = saved
    rows, width = middle.shape
    head_dim = keys.shape[1] // 2
    heads_width = head_count * head_dim
    outs = [
        shape_of((rows, width), F32),
        shape_of((rows, width), BF16),
        shape_of((rows, heads_width), F32),
        shape_of((rows, 2 * head_dim), BF16),
        shape_of((rows, 2 * head_dim), BF16),
        shape_of((rows, 2 * head_dim), F32),
        shape_of((8, width), F32),
    ]
    ins = [place] + list(sums) + list(saved) + parts.arrays
    return call(
        functools.partial(attend_back_kernel, parts.where, len(parts.arrays), head_count),
        outs,
        [VMEM_SPEC] * 7,
        ins,
        [SMEM_SPEC] + [VMEM_SPEC] * 9 + [ANY_SPEC] * len(parts.arrays),
        [
            pltpu.VMEM((width, heads_width), BF16),
            pltpu.VMEM((3 * rows, 2 * head_dim), F32),
            pltpu.SemaphoreType.DMA((slots(parts.where),)),
        ],
        flops=2 * rows * width * heads_width + 30 * rows * rows * heads_width,
        moved=2 * width * heads_width + 24 * rows * width,
    )


def heads_kernel(
    where,
    ref_count,
    out_count,
    head_count,
    place_ref,
    d_attn_ref,
    attended_ref,
    attn_in_ref,
    d_rotated_ref,
    query_lin_ref,
    small_gains_ref,
    cos_ref,
    sin_ref,
    *refs,
):
    parts, refs = refs[:ref_count], refs[ref_count:]
    grads, refs = refs[:out_count], refs[out_count:]
    d_in_ref, query_gain_ref, weights, whole, d_query, sems, out_sems = refs
    rows, width = attn_in_ref.shape
    heads_width = attended_ref.shape[1]
    head_dim = heads_width // head_count
    seq = place_ref[0]
    copies = start_placing(where, parts, weights, sems, 0, seq, 0, heads_width)
    for start, size in tiles_of(heads_width, 512):
        lanes = slice(start, start + size)
        whole[0, :, lanes] = dot_tn(d_attn_ref[...], attended_ref[:, lanes]).astype(BF16)
    cuts = start_cutting(whole.at[0], grads, out_sems.at[0], 0, seq, 0)
    cosine, sine = cos_ref[2 * rows :, :], sin_ref[2 * rows :, :]
    gain_q = small_gains_ref[4:5, :]
    query_gain = jnp.zeros((1, head_dim), F32)
    for head in range(head_count):
        lanes = slice(head * head_dim, (head + 1) * head_dim)
        query_lin = query_lin_ref[:, lanes]
        scale = inverse_rms(query_lin)
        d_normed = rotate(d_rotated_ref[:, lanes], cosine, -sine)
        back, gain_grad = norm_back(query_lin * scale, scale, gain_q, d_normed)
        query_gain = query_gain + gain_grad
        d_query[:, lanes] = back.astype(BF16)
    query_gain_ref[...] = query_gain
    for start, size in tiles_of(heads_width, 512):
        lanes = slice(start, start + size)
        whole[1, :, lanes] = dot_tn(attn_in_ref[...], d_query[:, lanes]).astype(BF16)
    cuts += start_cutting(whole.at[1], grads, out_sems.at[1], 0, seq, 1)
    wait_all(copies)
    for start, size in tiles_of(width, 384):
        lanes = slice(start, start + size)
        d_in_ref[:, lanes] = dot_t(d_query[...], weights[lanes, :])
    wait_all(cuts)


def heads_back(place, ins, parts, head_count):
    attn_in, attended, small_gains = ins[2], ins[1], ins[5]
    rows, width = attn_in.shape
    heads_width, head_dim = attended.shape[1], small_gains.shape[1]
    count = lax.axis_size("seq")
    cuts = [
        shape_of((2,) + part.shape, BF16) for part in cut_shapes(width, heads_width, count)
    ]
    return call(
        functools.partial(
            heads_kernel, parts.where, len(parts.arrays), len(cuts), head_count
        ),
        cuts + [shape_of((rows, width), F32), shape_of((1, head_dim), F32)],
        [ANY_SPEC] * len(cuts) + [VMEM_SPEC] * 2,
        [place] + list(ins) + parts.arrays,
        [SMEM_SPEC] + [VMEM_SPEC] * 8 + [ANY_SPEC] * len(parts.arrays),
        [
            pltpu.VMEM((width, heads_width), BF16),
            pltpu.VMEM((2, width, heads_width), BF16),
            pltpu.VMEM((rows, heads_width), BF16),
            pltpu.SemaphoreType.DMA((slots(parts.where),)),
            pltpu.SemaphoreType.DMA((2, count)),
        ],
        flops=6 * rows * width * heads_width,
        moved=8 * width * heads_width,
    )


def finish_kernel(
    where,
    ref_count,
    out_count,
    narrow_rows,
    wide_rows,
    place_ref,
    near_ref,
    back_ref,
    far_ref,
    key_lin_ref,
    small_gains_ref,
    gains_ref,
    cos_ref,
    sin_ref,
    attn_in_ref,
    tokens_ref,
    d_middle_ref,
    d_in_ref,
    rows_ref,
    ffn_post_ref,
    query_gain_ref,
    *refs,
):
    parts, refs = refs[:ref_count], refs[ref_count:]
    grads, (input_grad_ref, first_w, whole, d_low, sems) = refs[:out_count], refs[out_count:]
    rows, width = tokens_ref.shape
    head_dim = key_lin_ref.shape[1]
    seq = place_ref[0]
    heads_width = (parts[0].shape[-1] - 2 * head_dim - LANES) // 2
    copies = start_placing(where, parts, first_w, sems, 0, seq, heads_width, 2 * head_dim)
    d_keys = near_ref[...] + back_ref[...].astype(F32) + far_ref[...].astype(F32)
    key_lin = key_lin_ref[...]
    scale = inverse_rms(key_lin)
    d_normed = rotate(d_keys[:, :head_dim], cos_ref[2 * rows :, :], -sin_ref[2 * rows :, :])
    back, key_gain = norm_back(key_lin * scale, scale, small_gains_ref[5:6, :], d_normed)
    d_low[:, :head_dim] = back.astype(BF16)
    d_low[:, head_dim:] = d_keys[:, head_dim:].astype(BF16)
    whole[:, : 2 * head_dim] = dot_tn(attn_in_ref[...], d_low[...]).astype(BF16)
    wait_all(copies)
    d_attn_in = d_in_ref[...] + dot_t(d_low[...], first_w[...])
    inputs = tokens_ref[...].astype(F32)
    scale = inverse_rms(inputs)
    back, grad_an = norm_back(inputs * scale, scale, gains_ref[0:1, :], d_attn_in)
    input_grad_ref[...] = d_middle_ref[...] + back
    row = iota((8, width), 0)
    gain_rows = rows_ref[...] + jnp.where(row == 0, grad_an, 0.0)
    gain_rows = gain_rows + jnp.where(row == 3, ffn_post_ref[...], 0.0)
    small_row = iota((8, head_dim), 0)
    small = jnp.where(small_row == 4, query_gain_ref[...], 0.0)
    small = small + jnp.where(small_row == 5, key_gain, 0.0)
    spread = spread_matrix(head_dim, width, narrow_rows, wide_rows)
    gain_rows = gain_rows + dot(small.astype(BF16), spread)
    pick = unit((8, LANES), iota((8, LANES), 0) == iota((8, LANES), 1))
    whole[:, 2 * head_dim :] = dot_tn(gain_rows.astype(BF16), pick).astype(BF16)
    wait_all(start_cutting(whole, grads, sems, slots(where), seq))


def finish(place, ins, parts, narrow_rows, wide_rows):
    tokens, key_lin = ins[9], ins[3]
    rows, width = tokens.shape
    head_dim = key_lin.shape[1]
    count = lax.axis_size("seq")
    pack = 2 * head_dim + LANES
    cuts = cut_shapes(width, pack, count)
    return call(
        functools.partial(
            finish_kernel, parts.where, len(parts.arrays), len(cuts), narrow_rows, wide_rows
        ),
        cuts + [shape_of((rows, width), F32)],
        [ANY_SPEC] * len(cuts) + [VMEM_SPEC],
        [place] + list(ins) + parts.arrays,
        [SMEM_SPEC] + [VMEM_SPEC] * len(ins) + [ANY_SPEC] * len(parts.arrays),
        [
            pltpu.VMEM((width, 2 * head_dim), BF16),
            pltpu.VMEM((width, pack), BF16),
            pltpu.VMEM((rows, 2 * head_dim), BF16),
            pltpu.SemaphoreType.DMA((slots(parts.where) + count,)),
        ],
        flops=8 * rows * width * head_dim,
        moved=4 * width * pack + 20 * rows * width,
    )


def layout(lengths, counts, first_slot, row_count):
    starts = jnp.cumsum(lengths) - lengths
    slot_index = first_slot + jnp.arange(row_count, dtype=jnp.int32)
    member = (slot_index[:, None] >= starts[None, :]).astype(jnp.int32)
    document = jnp.sum(member, axis=1) - 1
    onehot = (document[:, None] == jnp.arange(lengths.shape[0], dtype=jnp.int32)[None, :]).astype(
        jnp.int32
    )
    position = slot_index - jnp.sum(onehot * starts[None, :], axis=1)
    padded = jnp.sum(onehot * (lengths - counts)[None, :], axis=1)
    return (position, padded)


def on_device(
    tokens,
    cotangent,
    doc_lengths,
    true_counts,
    w_query,
    w_key,
    w_value,
    w_out,
    w_gate,
    w_up,
    w_down,
    attn_norm_gain,
    query_gain,
    key_gain,
    attn_post_gain,
    ffn_norm_gain,
    ffn_post_gain,
):
    row_count = tokens.shape[1]
    head_dim = w_key.shape[1]
    heads_width = w_query.shape[1]
    head_count = heads_width // head_dim
    seq_index, plane_index = lax.axis_index("seq"), lax.axis_index("fsdp")
    place = jnp.stack([seq_index, plane_index]).astype(jnp.int32)
    inputs, upstream = tokens[0], cotangent[0]
    wide_rows, narrow_rows = attn_norm_gain.shape[0], query_gain.shape[0]

    planes_count = lax.axis_size("fsdp")
    far_masks = [mask for mask in seq_masks() if mask > 2]

    def swap_far(parts):
        parts = dict(parts)
        for mask in far_masks:
            parts.update({rel ^ mask: swap(part, "seq", mask) for rel, part in parts.items()})
        return parts

    def swap_both(parts, rel):
        if rel not in far_masks:
            return swap(parts[rel], "seq", 2)
        split = (parts[rel].shape[-2] // 2 + 15) // 16 * 16
        top = swap(parts[rel][..., :split, :], "seq", 2)
        bottom = swap(parts[2][..., split:, :], "seq", rel)
        return jnp.concatenate([top, bottom], axis=-2)

    pack = pack_attn(
        w_query,
        w_key,
        w_value,
        w_out,
        [attn_norm_gain, attn_post_gain, ffn_norm_gain, ffn_post_gain],
        [query_gain, key_gain],
    )
    gate_up_own = jnp.stack([w_gate, w_up])
    pack, gate_up_own, inputs, w_down = sync((pack, gate_up_own, inputs, w_down))

    planes = [pack] + [shift(pack, "fsdp", steps) for steps in range(1, planes_count)]
    gate_up_far = swap_far({0: gate_up_own})
    gate_up_half = gate_up_far | {2: swap(gate_up_own, "seq", 2)}
    first_slot = seq_index * row_count
    position, padded = layout(
        doc_lengths[0], true_counts[0], first_slot - WINDOW, row_count + WINDOW
    )
    frequency = ROPE_BASE ** (-2.0 * jnp.arange(head_dim // 2, dtype=F32) / head_dim)
    angles = position.astype(F32)[:, None] * frequency
    cosine, sine = jnp.cos(angles), jnp.sin(angles)
    reach = jnp.clip(position[WINDOW:] - padded[WINDOW:], 0, WINDOW - 1)
    lowest = (WINDOW + jnp.arange(row_count, dtype=jnp.int32) - reach)[:, None]
    lowest = jnp.broadcast_to(lowest, (row_count, LANES))
    state = (planes, cosine, sine, lowest, inputs, w_down)
    planes, cosine, sine, lowest, inputs, w_down = sync(state)
    pack_rows, gate_up_half, inputs, w_down = sync(
        (place_planes(planes, place), gate_up_half, inputs, w_down)
    )

    rows_far = swap_far({0: pack_rows})
    rows_half = rows_far | {2: swap(pack_rows, "seq", 2)}
    behind = from_behind(inputs, 1)
    gate_up_rels, gate_up_core = core_stack(gate_up_half)
    state = (rows_half, behind, gate_up_half, gate_up_core, w_down)
    rows_half, behind, gate_up_half, gate_up_core, w_down = sync(state)
    rows_rest = {rel ^ 2: swap_both(rows_half, rel) for rel in rows_far if rel}
    half_rels, half_core = core_stack(rows_half)
    tokens3 = [inputs, behind, from_behind(behind, 1)]
    state = (rows_half, rows_rest, half_core, tokens3, gate_up_half, w_down)
    rows_half, rows_rest, half_core, tokens3, gate_up_half, w_down = sync(state)
    rest_rels, rest_core = core_stack(rows_rest)
    rest_core, gate_up_half, w_down = sync((rest_core, gate_up_half, w_down))
    cores = [(half_rels, half_core), (rest_rels, rest_core)]
    parts = all_parts(with_cores(plain(rows_half | rows_rest), cores))

    gate_rest = {rel ^ 2: swap(gate_up_half[rel][0], "seq", 2) for rel in gate_up_far if rel}
    up_rest = swap_far({2: gate_up_half[2][1]})
    up_rest = {rel: up_rest[rel] for rel in gate_rest}
    (
        attn_in,
        query_lin,
        key_lin,
        query,
        keys,
        probs,
        attended,
        gains,
        small_gains,
        attn_out,
        middle,
        ffn_in,
    ) = attend(
        place,
        tokens3,
        cosine,
        sine,
        lowest,
        parts,
        head_count,
        head_dim,
        narrow_rows,
        wide_rows,
    )
    ffn_in, gate_rest, up_rest, w_down = sync((ffn_in, gate_rest, up_rest, w_down))

    rest_rels, rest_core = core_stack(
        {rel: jnp.stack([gate_rest[rel], up_rest[rel]]) for rel in gate_rest}
    )
    down_far = swap_far({0: w_down})
    down_half = down_far | {2: swap(w_down, "seq", 2)}
    state = (shift(ffn_in, "fsdp", 1), rest_core, down_half)
    block, rest_core, down_half = sync(state)
    weights = []
    for index, rest in enumerate((gate_rest, up_rest)):
        entries = {rel: (part, (index,)) for rel, part in gate_up_half.items()} | plain(rest)
        for rels, stack in ((gate_up_rels, gate_up_core), (rest_rels, rest_core)):
            entries |= {rel ^ 1: (stack, (place_in, index)) for place_in, rel in enumerate(rels)}
        weights.append(all_parts(entries))
    blocks = [ffn_in, block]
    down_rest = {rel ^ 2: swap_both(down_half, rel) for rel in down_far if rel}
    half_rels, half_core = core_stack(down_half)
    act, gate_slope, up_slope = gate_up(place, blocks[1], weights)
    state = (shift(blocks[1], "fsdp", 1), act, down_rest, half_core)
    block, act, down_rest, half_core = sync(state)
    blocks.append(block)
    rest_rels, rest_core = core_stack(down_rest)
    act, rest_core = sync((act, rest_core))
    cores = [(half_rels, half_core), (rest_rels, rest_core)]
    weights.append(all_parts(with_cores(plain(down_half | down_rest), cores)))
    acts, slopes = {1: act}, {1: (gate_slope, up_slope)}
    partials = {1: sync(down(place, act, weights[2:]))}
    carried = None
    for step in range(2, planes_count + 1):
        state = {}
        if step < planes_count - 1:
            state["block"] = shift(blocks[step], "fsdp", 1)
        leaving = partials[step - 1]
        if carried is not None:
            leaving = add_rounded(leaving, carried)
        index = step % planes_count
        acts[index], gate_slope, up_slope, partials[index] = ffn(place, blocks[index], weights)
        slopes[index] = (gate_slope, up_slope)
        state["carried"] = shift(leaving, "fsdp", 1)
        state, partials = sync((state, partials))
        carried = state["carried"]
        if "block" in state:
            blocks.append(state["block"])
    output, d_ffn_low, grad_fp = turn([partials[0], carried], middle, upstream, gains)

    backs, partials, d_gates, d_ups = [sync(d_ffn_low)], {}, [], []
    carried, down_pair, down_sent = None, None, None
    all_acts = [acts[index] for index in range(planes_count)]
    for step in range(planes_count):
        state = {}
        if step < planes_count - 2:
            state["block"] = shift(backs[step], "fsdp", 1)
        if step == planes_count - 3:
            state["last"] = shift(backs[0], "fsdp", -1)
        if step >= 2:
            leaving = partials[step - 1]
            if carried is not None:
                leaving = add_rounded(leaving, carried)
            state["carried"] = shift(leaving, "fsdp", 1)
        if step == planes_count - 2:
            d_gate, d_up, partials[step], down_pair = ffn_back_and_grad(
                place, backs[step], slopes[step], weights, backs, all_acts
            )
        else:
            d_gate, d_up, partials[step] = ffn_back(place, backs[step], slopes[step], weights)
        if step == planes_count - 1:
            state["down"] = cores_send(down_pair)
        d_gates.append(d_gate)
        d_ups.append(d_up)
        state, partials, d_gates, d_ups, down_pair = sync(
            (state, partials, d_gates, d_ups, down_pair)
        )
        carried = state.get("carried", carried)
        backs += [state[name] for name in ("block", "last") if name in state]
        down_sent = state.get("down")
    carried = shift(add_rounded(partials[planes_count - 1], carried), "fsdp", 1)
    down_part = add_rounded(*down_sent)
    down_terms = [down_part[0]] + straight(down_part, 1, 2)
    gate_pair, up_pair = weight_grad(place, blocks, d_gates, d_ups)
    carried, gate_pair, up_pair, down_terms, down_part = sync(
        (carried, gate_pair, up_pair, down_terms, down_part)
    )

    gate_sent, up_sent = cores_send(gate_pair), cores_send(up_pair)
    down_terms += straight(down_part, *range(3, down_part.shape[0]))
    saved = (middle, upstream, attn_out, gains, query, keys, probs)
    d_middle, d_attn, d_rotated, far_halo, back_halo, near, gain_rows = attend_back(
        place, [partials[0], carried], saved, parts, head_count
    )
    state = (far_halo, back_halo, d_attn, d_rotated, gate_sent, up_sent)
    far_halo, back_halo, d_attn, d_rotated, gate_sent, up_sent = sync(state)
    halos = [from_behind(back_halo, -1), from_behind(far_halo, -2)]
    ins = [d_attn, attended, attn_in, d_rotated, query_lin, small_gains, cosine, sine]
    *head_grads, d_in, query_gain_grad = heads_back(place, ins, parts, head_count)
    state = (halos, head_grads, gate_sent, up_sent, down_terms)
    halos, head_grads, gate_sent, up_sent, down_terms = sync(state)
    head_sent = cores_send(head_grads)
    gate_sides = far_step(add_rounded(*gate_sent))
    up_sides = across_step(add_rounded(*up_sent))
    ins = [
        near,
        *halos,
        key_lin,
        small_gains,
        gains,
        cosine,
        sine,
        attn_in,
        inputs,
        d_middle,
        d_in,
        gain_rows,
        grad_fp,
        query_gain_grad,
    ]
    *last_grads, input_grad = finish(place, ins, parts, narrow_rows, wide_rows)
    last_grads, head_sent = sync((last_grads, head_sent))
    last_sent = cores_send(last_grads)
    head_part = add_rounded(*head_sent)
    out_sides = far_step(head_part[0])
    query_sides = across_step(head_part[1])
    state = (last_sent, out_sides, query_sides, gate_sides, up_sides)
    last_sent, out_sides, query_sides, gate_sides, up_sides = sync(state)
    out_part = add_rounded(*out_sides)
    out_came = swap(out_part[1], "seq", 2)
    query_sides = far_step(add_rounded(*query_sides))
    last_part = add_rounded(*last_sent)
    last_terms = [last_part[0]] + straight(last_part, *range(1, last_part.shape[0]))
    gate_part, up_part = add_rounded(*gate_sides), add_rounded(*up_sides)
    state = (out_part, out_came, query_sides, last_terms, gate_part, up_part)
    out_part, out_came, query_sides, last_terms, gate_part, up_part = sync(state)
    reduced = jnp.concatenate(
        [
            add_rounded(out_part[0], out_came),
            add_rounded(*query_sides)[0],
            add_up(last_terms).astype(BF16),
        ],
        axis=1,
    )
    terms = planes_send(reduced)
    gate_came = swap(gate_part[1], "seq", 2)
    up_sides = far_step(up_part)
    terms, gate_part, gate_came, up_sides = sync((terms, gate_part, gate_came, up_sides))
    rows = add_up(terms)
    grad_gate = add_up([gate_part[0], gate_came])
    grad_up = add_up(up_sides)[0]
    last_start = 2 * heads_width
    gain_cols = rows[:, last_start + 2 * head_dim :]
    return (
        output[None],
        input_grad[None],
        rows[:, heads_width:last_start],
        rows[:, last_start : last_start + head_dim],
        rows[:, last_start + head_dim : last_start + 2 * head_dim],
        rows[:, :heads_width],
        grad_gate,
        grad_up,
        add_up(down_terms),
        gain_cols[:, 0],
        gain_cols[:narrow_rows, 4],
        gain_cols[:narrow_rows, 5],
        gain_cols[:, 1],
        gain_cols[:, 2],
        gain_cols[:, 3],
    )


def solution(mesh):
    rows = P("fsdp", "seq", None)
    shard, tile, vector = P(("seq", "fsdp"), None), P("seq", "fsdp"), P(("seq", "fsdp"))
    groups = P("fsdp", None)
    return jax.shard_map(
        on_device,
        mesh=mesh,
        in_specs=(rows, rows, groups, groups) + (shard,) * 4 + (tile,) * 3 + (vector,) * 6,
        out_specs=(rows, rows) + (shard,) * 4 + (tile,) * 3 + (vector,) * 6,
        check_vma=False,
    )
```

```python
import functools

import jax
import jax.numpy as jnp
from jax import lax
from jax.experimental import pallas as pl
from jax.experimental.pallas import tpu as pltpu
from jax.sharding import PartitionSpec as P

WINDOW = 512
NORM_EPS = 1e-06
ROPE_BASE = 10000.0
NEGATIVE = -1e30
LANES = 128
VMEM_LIMIT = 56 * 2**20
PIECES = 8
BF16 = jnp.bfloat16
F32 = jnp.float32


def from_behind(value, steps):
    count = lax.axis_size("seq")
    first, last = (max(0, -steps), min(count, count - steps))
    return lax.ppermute(value, "seq", [(source, source + steps) for source in range(first, last)])


def seq_masks():
    return [1 << bit for bit in range(lax.axis_size("seq").bit_length() - 1)]


def swap(value, axis, mask):
    count = lax.axis_size(axis)
    return lax.ppermute(value, axis, [(source, source ^ mask) for source in range(count)])


def shift(value, axis, steps):
    count = lax.axis_size(axis)
    return lax.ppermute(value, axis, [(source, (source + steps) % count) for source in range(count)])


def sync(state):
    return lax.optimization_barrier(state)


class Parts:
    def __init__(self, arrays, where):
        self.arrays, self.where = list(arrays), tuple(where)
        self.width = arrays[0].shape[-1]
        self.rows = arrays[0].shape[-2] * len(where)


def core_stack(parts):
    stack = jnp.stack(list(parts.values())) if len(parts) > 1 else list(parts.values())[0][None]
    return tuple(parts), swap(stack, "seq", 1)


def with_cores(entries, cores):
    for rels, stack in cores:
        entries = entries | {rel ^ 1: (stack, (index,)) for index, rel in enumerate(rels)}
    return entries


def all_parts(entries):
    arrays, places = [], []
    for rel in range(len(entries)):
        array, index = entries[rel]
        number = next((n for n, other in enumerate(arrays) if other is array), len(arrays))
        if number == len(arrays):
            arrays.append(array)
        places.append((number, index))
    if arrays[0].shape[-2] % 16 == 0:
        return Parts(arrays, places)
    index = jnp.arange(len(places), dtype=jnp.int32) ^ lax.axis_index("seq")
    blocks = [arrays[number][block] for number, block in places]
    whole = jnp.take(jnp.stack(blocks), index, axis=0, mode="clip")
    return Parts([whole.reshape(-1, whole.shape[-1])], [(0, ())])


def plain(parts):
    return {rel: (part, ()) for rel, part in parts.items()}


def add_rounded(first, second):
    return (first.astype(F32) + second.astype(F32)).astype(BF16)


def cut(pair, count):
    if len(pair) == 2:
        return pair
    whole = pair[0]
    index = jnp.arange(count, dtype=jnp.int32) ^ lax.axis_index("seq")
    blocks = whole.reshape(whole.shape[:-2] + (count, -1, whole.shape[-1]))
    blocks = jnp.take(blocks, index, axis=blocks.ndim - 3, mode="clip")
    return blocks[..., 0::2, :, :], blocks[..., 1::2, :, :]


def cores_send(pair):
    keep, send = cut(pair, lax.axis_size("seq"))
    return keep, swap(send, "seq", 1)


def far_step(part):
    masks = [mask for mask in seq_masks() if mask > 2][::-1]
    for mask in masks[:-1]:
        half = part.shape[0] // 2
        part = add_rounded(part[:half], swap(part[half:], "seq", mask))
    half = part.shape[0] // 2
    return part[:half], swap(part[half:], "seq", masks[-1])


def across_cut(part):
    part = part.reshape((-1, 2) + part.shape[1:])
    return part[:, 0], part[:, 1]


def across_step(part):
    stays, leaves = across_cut(part)
    return stays, swap(leaves, "seq", 2)


def far_cut(part):
    masks = [mask for mask in seq_masks() if mask > 2][::-1]
    for mask in masks[:-1]:
        half = part.shape[0] // 2
        part = add_rounded(part[:half], swap(part[half:], "seq", mask))
    half = part.shape[0] // 2
    return part[:half], part[half:]


def straight(part, *steps):
    return [swap(part[step], "seq", 2 * step) for step in steps]


def planes_send(rows):
    planes = lax.axis_size("fsdp")
    blocks = rows.reshape((planes, -1) + rows.shape[1:])
    mine = lax.axis_index("fsdp")
    sent = [lax.dynamic_index_in_dim(blocks, mine, 0, keepdims=False)]
    for steps in range(1, planes):
        send = lax.dynamic_index_in_dim(blocks, (mine + steps) % planes, 0, keepdims=False)
        sent.append(shift(send, "fsdp", steps))
    return sent


def add_up(terms):
    total = terms[0].astype(F32)
    for term in terms[1:]:
        total = total + term.astype(F32)
    return total


def dot(left, right):
    return jnp.dot(left, right, preferred_element_type=F32)


def dot_t(left, right):
    return lax.dot_general(left, right, (((1,), (1,)), ((), ())), preferred_element_type=F32)


def dot_tn(left, right):
    return lax.dot_general(left, right, (((0,), (0,)), ((), ())), preferred_element_type=F32)


def inverse_rms(values):
    return lax.rsqrt(jnp.mean(values * values, axis=-1, keepdims=True) + NORM_EPS)


def norm_back(normed, scale, gain, upstream):
    scaled = upstream * gain
    back = scale * (scaled - normed * jnp.mean(scaled * normed, axis=-1, keepdims=True))
    return back, jnp.sum(upstream * normed, axis=0, keepdims=True)


def rotate(values, cosine, sine):
    half = values.shape[-1] // 2
    first, second = values[:, :half], values[:, half:]
    return jnp.concatenate(
        [first * cosine - second * sine, second * cosine + first * sine], axis=-1
    )


def iota(shape, dim):
    return lax.broadcasted_iota(jnp.int32, shape, dim)


def unit(shape, hits):
    return jnp.where(hits, 1.0, 0.0).astype(BF16)


def spread_matrix(narrow, wide, narrow_rows, wide_rows):
    row, col = iota((narrow, wide), 0), iota((narrow, wide), 1)
    return unit((narrow, wide), col == (row // narrow_rows) * wide_rows + row % narrow_rows)


def tiles_of(width, step):
    return [(start, min(step, width - start)) for start in range(0, width, step)]


def slots(where):
    return max(PIECES, len(where))


def start_placing(where, refs, dest, sems, base, seq, lane=0, lanes=None, same=False):
    if same:
        dest = dest.at[:, pl.ds(lane, lanes)]
    copies = []
    if len(where) == 1:
        whole = refs[0] if lanes is None else refs[0].at[:, pl.ds(lane, lanes)]
        count = PIECES if whole.shape[0] % (16 * PIECES) == 0 else 1
        rows = whole.shape[0] // count
        pieces = [(index * rows, whole.at[pl.ds(index * rows, rows), :]) for index in range(count)]
        copies = [
            pltpu.make_async_copy(part, dest.at[pl.ds(start, rows), :], sems.at[base + index])
            for index, (start, part) in enumerate(pieces)
        ]
        for copy in copies:
            copy.start()
        return copies
    for rel, (number, block) in enumerate(where):
        part = refs[number].at[block] if block else refs[number]
        rows = part.shape[0]
        start = pl.multiple_of((seq ^ rel) * rows, 16) if len(where) > 1 else 0
        if lanes is not None:
            part = part.at[:, pl.ds(lane, lanes)]
        copies.append(
            pltpu.make_async_copy(part, dest.at[pl.ds(start, rows), :], sems.at[base + rel])
        )
    for copy in copies:
        copy.start()
    return copies


def start_cutting(whole, outs, sems, base, seq, which=None):
    if which is not None:
        outs = [out.at[which] for out in outs]
    if len(outs) == 1:
        copies = [pltpu.make_async_copy(whole, outs[0], sems.at[base])]
    else:
        half, rows = outs[0].shape[0], outs[0].shape[1]
        copies = []
        for rel in range(2 * half):
            start = pl.multiple_of((seq ^ rel) * rows, 16)
            copies.append(
                pltpu.make_async_copy(
                    whole.at[pl.ds(start, rows), :], outs[rel % 2].at[rel // 2], sems.at[base + rel]
                )
            )
    for copy in copies:
        copy.start()
    return copies


def cut_shapes(height, width, count):
    rows = height // count
    if rows % 16:
        return [jax.ShapeDtypeStruct((height, width), BF16)]
    return [jax.ShapeDtypeStruct((count // 2, rows, width), BF16)] * 2


def wait_all(copies):
    for copy in copies:
        copy.wait()


SMEM_SPEC = pl.BlockSpec(memory_space=pltpu.SMEM)
VMEM_SPEC = pl.BlockSpec(memory_space=pltpu.VMEM)
ANY_SPEC = pl.BlockSpec(memory_space=pl.ANY)


def call(kernel, outs, out_specs, ins, in_specs, scratch=(), flops=0, moved=0, exps=0):
    return pl.pallas_call(
        kernel,
        out_shape=tuple(outs),
        in_specs=list(in_specs),
        out_specs=tuple(out_specs),
        scratch_shapes=list(scratch),
        compiler_params=pltpu.CompilerParams(vmem_limit_bytes=VMEM_LIMIT),
        cost_estimate=pl.CostEstimate(flops=flops, bytes_accessed=moved, transcendentals=exps),
    )(*ins)


def shape_of(dims, dtype):
    return jax.ShapeDtypeStruct(dims, dtype)


def pack_kernel(wq_ref, wk_ref, wv_ref, wo_ref, *refs):
    wide, narrow, out_ref = refs[:4], refs[4:6], refs[6]
    rows, heads_width, head_dim = wq_ref.shape[0], wq_ref.shape[1], wk_ref.shape[1]
    out_ref[:, :heads_width] = wq_ref[...]
    out_ref[:, heads_width : heads_width + head_dim] = wk_ref[...]
    out_ref[:, heads_width + head_dim : heads_width + 2 * head_dim] = wv_ref[...]
    row = iota((16, rows), 0)
    held = jnp.zeros((16, rows), F32)
    for index, ref in enumerate(wide):
        held = held + jnp.where(row == index, ref[...].astype(F32), 0.0)
    small = narrow[0].shape[1]
    fit = unit((small, rows), iota((small, rows), 0) == iota((small, rows), 1))
    for index, ref in enumerate(narrow):
        spread = dot(jnp.broadcast_to(ref[...].astype(F32), (16, small)).astype(BF16), fit)
        held = held + jnp.where(row == 4 + index, spread, 0.0)
    place = unit((16, LANES), iota((16, LANES), 0) == iota((16, LANES), 1))
    gain_start = heads_width + 2 * head_dim
    out_ref[:, gain_start : gain_start + LANES] = dot_tn(held.astype(BF16), place).astype(BF16)
    out_ref[:, gain_start + LANES :] = wo_ref[...]


def pack_attn(w_query, w_key, w_value, w_out, wide, narrow):
    rows = w_query.shape[0]
    width = 2 * w_query.shape[1] + 2 * w_key.shape[1] + LANES
    ins = [w_query, w_key, w_value, w_out] + [vec.reshape(1, -1) for vec in wide + narrow]
    return call(
        pack_kernel,
        [shape_of((rows, width), BF16)],
        [VMEM_SPEC],
        ins,
        [VMEM_SPEC] * len(ins),
    )[0]


def planes_kernel(place_ref, *refs):
    parts, out_ref = refs[:-1], refs[-1]
    count, rows = len(parts), parts[0].shape[0]
    total = None
    for steps, part in enumerate(parts):
        plane = lax.rem(place_ref[1] - steps + count, count)
        row, col = iota((count * rows, rows), 0), iota((count * rows, rows), 1)
        term = dot(unit((count * rows, rows), row == col + plane * rows), part[...])
        total = term if total is None else total + term
    out_ref[...] = total.astype(BF16)


def place_planes(parts, place):
    count = len(parts)
    rows, width = parts[0].shape
    return call(
        planes_kernel,
        [shape_of((count * rows, width), BF16)],
        [VMEM_SPEC],
        [place] + parts,
        [SMEM_SPEC] + [VMEM_SPEC] * count,
        flops=2 * count * count * rows * rows * width,
        moved=4 * count * rows * width,
    )[0]


def attend_kernel(
    where,
    ref_count,
    narrow_rows,
    wide_rows,
    head_count,
    place_ref,
    near_ref,
    back_ref,
    far_ref,
    cos_ref,
    sin_ref,
    low_ref,
    *refs,
):
    parts, refs = refs[:ref_count], refs[ref_count:]
    (
        attn_in_ref,
        query_lin_ref,
        key_lin_ref,
        query_ref,
        keys_ref,
        probs_ref,
        attended_ref,
        gains_ref,
        small_gains_ref,
        attn_out_ref,
        middle_ref,
        ffn_in_ref,
    ) = refs[:12]
    weights, inside, sems = refs[12:]
    rows, width = near_ref.shape
    head_dim = key_lin_ref.shape[1]
    heads_width = head_count * head_dim
    rest = heads_width + 2 * head_dim + LANES
    groups = [(heads_width, rest - heads_width), (0, heads_width), (rest, heads_width)]
    first, second, third = [
        start_placing(
            where, parts, weights, sems, index * slots(where), place_ref[0], lane, lanes, True
        )
        for index, (lane, lanes) in enumerate(groups)
    ]
    score_scale = head_dim**-0.5
    blocks = [far_ref, back_ref, near_ref]
    scales = []
    for ref in blocks:
        scales.append(inverse_rms(ref[...].astype(F32)))
    wait_all(first)
    gain_start = heads_width + 2 * head_dim
    gain_cols = weights[:, gain_start : gain_start + LANES]
    pick = unit((8, LANES), iota((8, LANES), 0) == iota((8, LANES), 1))
    gains = dot_t(pick, gain_cols)
    spread = spread_matrix(head_dim, width, narrow_rows, wide_rows)
    small_gains = dot_t(gains.astype(BF16), spread)
    gains_ref[...] = gains
    small_gains_ref[...] = small_gains
    gain_an, gain_q, gain_k = gains[0:1], small_gains[4:5], small_gains[5:6]
    for index, ref in enumerate(blocks):
        normed = ref[...].astype(F32) * scales[index] * gain_an
        inside[index * rows : (index + 1) * rows, :] = normed.astype(BF16)
    attn_in_ref[...] = inside[2 * rows :, :]
    for index in range(3):
        span = slice(index * rows, (index + 1) * rows)
        part_in = inside[span, :]
        key_lin = dot(part_in, weights[:, heads_width : heads_width + head_dim])
        value = dot(part_in, weights[:, heads_width + head_dim : heads_width + 2 * head_dim])
        key = rotate(key_lin * inverse_rms(key_lin) * gain_k, cos_ref[span, :], sin_ref[span, :])
        keys_ref[span, :head_dim] = key.astype(BF16)
        keys_ref[span, head_dim:] = value.astype(BF16)
        if index == 2:
            key_lin_ref[...] = key_lin
    cosine, sine = cos_ref[2 * rows :, :], sin_ref[2 * rows :, :]
    column = iota((rows, 3 * rows), 1)
    seen = (column >= low_ref[:, :1]) & (column <= iota((rows, 3 * rows), 0) + 2 * rows)
    wait_all(second)
    for start, size in tiles_of(heads_width, 512):
        lanes = slice(start, start + size)
        query_lin_ref[:, lanes] = dot(inside[2 * rows :, :], weights[:, lanes])
    for head in range(head_count):
        lanes = slice(head * head_dim, (head + 1) * head_dim)
        query_lin = query_lin_ref[:, lanes]
        query = rotate(query_lin * inverse_rms(query_lin) * gain_q, cosine, sine).astype(BF16)
        query_ref[:, lanes] = query
        scores = jnp.where(seen, dot_t(query, keys_ref[:, :head_dim]) * score_scale, NEGATIVE)
        raised = jnp.exp(scores - jnp.max(scores, axis=-1, keepdims=True))
        probs = (raised * (1.0 / jnp.sum(raised, axis=-1, keepdims=True))).astype(BF16)
        probs_ref[head * rows : (head + 1) * rows, :] = probs
        attended_ref[:, lanes] = dot(probs, keys_ref[:, head_dim:]).astype(BF16)
    wait_all(third)
    for start, size in tiles_of(width, 384):
        attn_out_ref[:, start : start + size] = dot_t(
            attended_ref[...], weights[start : start + size, gain_start + LANES :]
        )
    attn_out = attn_out_ref[...]
    middle = near_ref[...].astype(F32) + attn_out * inverse_rms(attn_out) * gains[1:2]
    middle_ref[...] = middle
    ffn_in_ref[...] = (middle * inverse_rms(middle) * gains[2:3]).astype(BF16)


def attend(place, tokens3, cosine, sine, lowest, parts, head_count, head_dim, narrow_rows, wide_rows):
    rows, width = tokens3[0].shape
    heads_width = head_count * head_dim
    pack = parts.width
    outs = [
        shape_of((rows, width), BF16),
        shape_of((rows, heads_width), F32),
        shape_of((rows, head_dim), F32),
        shape_of((rows, heads_width), BF16),
        shape_of((3 * rows, 2 * head_dim), BF16),
        shape_of((head_count * rows, 3 * rows), BF16),
        shape_of((rows, heads_width), BF16),
        shape_of((8, width), F32),
        shape_of((8, head_dim), F32),
        shape_of((rows, width), F32),
        shape_of((rows, width), F32),
        shape_of((rows, width), BF16),
    ]
    return call(
        functools.partial(
            attend_kernel, parts.where, len(parts.arrays), narrow_rows, wide_rows, head_count
        ),
        outs,
        [VMEM_SPEC] * len(outs),
        [place] + list(tokens3) + [cosine, sine, lowest] + parts.arrays,
        [SMEM_SPEC] + [VMEM_SPEC] * 6 + [ANY_SPEC] * len(parts.arrays),
        [
            pltpu.VMEM((width, pack), BF16),
            pltpu.VMEM((3 * rows, width), BF16),
            pltpu.SemaphoreType.DMA((3 * slots(parts.where),)),
        ],
        flops=2 * rows * width * (heads_width + 6 * head_dim) + 12 * rows * rows * heads_width,
        moved=2 * width * pack + 16 * rows * width,
        exps=3 * head_count * rows * rows,
    )


def gelu_pair(gate):
    square = gate * gate
    tanh = jnp.tanh(gate * (0.7978845608028654 + 0.035677408136300125 * square))
    half = 0.5 + 0.5 * tanh
    value = gate * half
    slope = half + value * (1.0 - tanh) * (0.7978845608028654 + 0.10703222440890037 * square)
    return value, slope


def take_parts(wheres, counts, refs):
    parts = []
    for count in counts:
        parts.append(refs[:count])
        refs = refs[count:]
    bases = [sum(slots(where) for where in wheres[:index]) for index in range(len(wheres))]
    return parts, bases, refs


def parts_of(weights):
    wheres = tuple(parts.where for parts in weights)
    counts = tuple(len(parts.arrays) for parts in weights)
    arrays = [array for parts in weights for array in parts.arrays]
    return wheres, counts, arrays, sum(slots(where) for where in wheres)


def gate_up_body(rows_ref, gate_w, up_w, act_ref, gate_slope_ref, up_slope_ref):
    rows_in = rows_ref[...]
    for start, size in tiles_of(gate_w.shape[1], 256):
        lanes = slice(start, start + size)
        gate = dot(rows_in, gate_w[:, lanes])
        up = dot(rows_in, up_w[:, lanes])
        value, slope = gelu_pair(gate)
        act_ref[:, lanes] = (value * up).astype(BF16)
        gate_slope_ref[:, lanes] = (slope * up).astype(BF16)
        up_slope_ref[:, lanes] = value.astype(BF16)


def down_body(act_ref, down_w, out_ref):
    for start, size in tiles_of(down_w.shape[0], 384):
        lanes = slice(start, start + size)
        out_ref[:, lanes] = dot_t(act_ref[...], down_w[lanes, :]).astype(BF16)


def ffn_kernel(wheres, counts, place_ref, rows_ref, *refs):
    parts, bases, refs = take_parts(wheres, counts, refs)
    act_ref, gate_slope_ref, up_slope_ref, out_ref, gate_w, up_w, down_w, sems = refs
    seq = place_ref[0]
    copies = start_placing(wheres[0], parts[0], gate_w, sems, bases[0], seq)
    copies += start_placing(wheres[1], parts[1], up_w, sems, bases[1], seq)
    later = start_placing(wheres[2], parts[2], down_w, sems, bases[2], seq)
    wait_all(copies)
    gate_up_body(rows_ref, gate_w, up_w, act_ref, gate_slope_ref, up_slope_ref)
    wait_all(later)
    down_body(act_ref, down_w, out_ref)


def gate_up_kernel(wheres, counts, place_ref, rows_ref, *refs):
    parts, bases, refs = take_parts(wheres, counts, refs)
    act_ref, gate_slope_ref, up_slope_ref, gate_w, up_w, sems = refs
    seq = place_ref[0]
    copies = start_placing(wheres[0], parts[0], gate_w, sems, bases[0], seq)
    copies += start_placing(wheres[1], parts[1], up_w, sems, bases[1], seq)
    wait_all(copies)
    gate_up_body(rows_ref, gate_w, up_w, act_ref, gate_slope_ref, up_slope_ref)


def gate_up(place, rows_in, weights):
    rows, width = rows_in.shape
    hidden = weights[0].width
    wheres, counts, arrays, sem_count = parts_of(weights)
    return call(
        functools.partial(gate_up_kernel, wheres, counts),
        [shape_of((rows, hidden), BF16)] * 3,
        [VMEM_SPEC] * 3,
        [place, rows_in] + arrays,
        [SMEM_SPEC, VMEM_SPEC] + [ANY_SPEC] * len(arrays),
        [pltpu.VMEM((width, hidden), BF16)] * 2 + [pltpu.SemaphoreType.DMA((sem_count,))],
        flops=4 * rows * hidden * width,
        moved=4 * width * hidden + 6 * rows * hidden,
    )


def down_kernel(wheres, counts, place_ref, act_ref, *refs):
    parts, bases, refs = take_parts(wheres, counts, refs)
    out_ref, down_w, sems = refs
    wait_all(start_placing(wheres[0], parts[0], down_w, sems, bases[0], place_ref[0]))
    down_body(act_ref, down_w, out_ref)


def down(place, act, weights):
    rows, hidden = act.shape
    width = weights[0].rows
    wheres, counts, arrays, sem_count = parts_of(weights)
    return call(
        functools.partial(down_kernel, wheres, counts),
        [shape_of((rows, width), BF16)],
        [VMEM_SPEC],
        [place, act] + arrays,
        [SMEM_SPEC, VMEM_SPEC] + [ANY_SPEC] * len(arrays),
        [pltpu.VMEM((width, hidden), BF16), pltpu.SemaphoreType.DMA((sem_count,))],
        flops=2 * rows * hidden * width,
        moved=2 * width * hidden + 2 * rows * hidden,
    )[0]


def ffn(place, rows_in, weights):
    rows, width = rows_in.shape
    hidden = weights[0].width
    wheres, counts, arrays, sem_count = parts_of(weights)
    return call(
        functools.partial(ffn_kernel, wheres, counts),
        [shape_of((rows, hidden), BF16)] * 3 + [shape_of((rows, width), BF16)],
        [VMEM_SPEC] * 4,
        [place, rows_in] + arrays,
        [SMEM_SPEC, VMEM_SPEC] + [ANY_SPEC] * len(arrays),
        [pltpu.VMEM((width, hidden), BF16)] * 3 + [pltpu.SemaphoreType.DMA((sem_count,))],
        flops=6 * rows * hidden * width,
        moved=6 * width * hidden + 8 * rows * hidden,
    )


def turn_kernel(own_ref, came_ref, middle_ref, upstream_ref, gains_ref, *outs):
    output_ref, back_ref, gain_grad_ref = outs
    total = own_ref[...].astype(F32) + came_ref[...].astype(F32)
    scale = inverse_rms(total)
    normed = total * scale
    gain = gains_ref[3:4, :]
    output_ref[...] = (middle_ref[...] + normed * gain).astype(BF16)
    back, gain_grad = norm_back(normed, scale, gain, upstream_ref[...].astype(F32))
    back_ref[...] = back.astype(BF16)
    gain_grad_ref[...] = gain_grad


def turn(sums, middle, upstream, gains):
    rows, width = middle.shape
    return call(
        turn_kernel,
        [shape_of((rows, width), BF16), shape_of((rows, width), BF16), shape_of((1, width), F32)],
        [VMEM_SPEC] * 3,
        list(sums) + [middle, upstream, gains],
        [VMEM_SPEC] * 5,
        moved=20 * rows * width,
    )


def ffn_back_kernel(
    wheres, counts, place_ref, back_ref, gate_slope_ref, up_slope_ref, *refs
):
    parts, bases, refs = take_parts(wheres, counts, refs)
    d_gate_ref, d_up_ref, out_ref, gate_w, up_w, down_w, sems = refs
    seq = place_ref[0]
    copies = start_placing(wheres[2], parts[2], down_w, sems, bases[2], seq)
    later = start_placing(wheres[0], parts[0], gate_w, sems, bases[0], seq)
    later += start_placing(wheres[1], parts[1], up_w, sems, bases[1], seq)
    wait_all(copies)
    back = back_ref[...]
    for start, size in tiles_of(down_w.shape[1], 256):
        lanes = slice(start, start + size)
        d_act = dot(back, down_w[:, lanes])
        d_gate_ref[:, lanes] = (d_act * gate_slope_ref[:, lanes].astype(F32)).astype(BF16)
        d_up_ref[:, lanes] = (d_act * up_slope_ref[:, lanes].astype(F32)).astype(BF16)
    wait_all(later)
    for start, size in tiles_of(gate_w.shape[0], 384):
        lanes = slice(start, start + size)
        total = dot_t(d_gate_ref[...], gate_w[lanes, :])
        out_ref[:, lanes] = (total + dot_t(d_up_ref[...], up_w[lanes, :])).astype(BF16)


def ffn_back(place, back, slopes, weights):
    rows, width = back.shape
    hidden = weights[0].width
    wheres, counts, arrays, sem_count = parts_of(weights)
    return call(
        functools.partial(ffn_back_kernel, wheres, counts),
        [shape_of((rows, hidden), BF16)] * 2 + [shape_of((rows, width), BF16)],
        [VMEM_SPEC] * 3,
        [place, back] + list(slopes) + arrays,
        [SMEM_SPEC] + [VMEM_SPEC] * 3 + [ANY_SPEC] * len(arrays),
        [pltpu.VMEM((width, hidden), BF16)] * 3 + [pltpu.SemaphoreType.DMA((sem_count,))],
        flops=6 * rows * hidden * width,
        moved=6 * width * hidden + 12 * rows * hidden,
    )


def ffn_back_and_grad_kernel(in_counts, out_count, back_kernel, grad_kernel, place_ref, *refs):
    back_ins, refs = refs[: in_counts[0]], refs[in_counts[0] :]
    grad_ins, refs = refs[: in_counts[1]], refs[in_counts[1] :]
    back_outs, refs = refs[:3], refs[3:]
    grad_outs, refs = refs[:out_count], refs[out_count:]
    back_kernel(place_ref, *back_ins, *back_outs, *refs[:4])
    grad_kernel(place_ref, *grad_ins, *grad_outs, *refs[4:])


def ffn_back_and_grad(place, back, slopes, weights, lefts, rights):
    rows, width = back.shape
    hidden = weights[0].width
    wheres, counts, arrays, sem_count = parts_of(weights)
    count = lax.axis_size("seq")
    cuts = cut_shapes(width, hidden, count)
    all_rows = sum(piece.shape[0] for piece in lefts)
    grad_ins = list(lefts) + list(rights)
    back_ins = [back] + list(slopes) + arrays
    outs = call(
        functools.partial(
            ffn_back_and_grad_kernel,
            (len(back_ins), len(grad_ins)),
            len(cuts),
            functools.partial(ffn_back_kernel, wheres, counts),
            functools.partial(weight_grad_kernel, len(lefts), (len(rights),), len(cuts)),
        ),
        [shape_of((rows, hidden), BF16)] * 2 + [shape_of((rows, width), BF16)] + cuts,
        [VMEM_SPEC] * 3 + [ANY_SPEC] * len(cuts),
        [place] + back_ins + grad_ins,
        [SMEM_SPEC] + [VMEM_SPEC] * 3 + [ANY_SPEC] * (len(arrays) + len(grad_ins)),
        [pltpu.VMEM((width, hidden), BF16)] * 3
        + [pltpu.SemaphoreType.DMA((sem_count,))]
        + weight_grad_scratch(all_rows, width, hidden, len(lefts), [len(rights)], count),
        flops=2 * all_rows * width * hidden + 6 * rows * width * hidden,
        moved=8 * width * hidden,
    )
    return outs[0], outs[1], outs[2], outs[3:]


def weight_grad_scratch(rows, height, width, left_count, right_counts, count):
    sides, pieces = len(right_counts), sum(right_counts)
    tiles = len(tiles_of(width, 512))
    return [
        pltpu.VMEM((rows, height), BF16),
        pltpu.VMEM((sides, rows, width), BF16),
        pltpu.VMEM((sides, height, width), BF16),
        pltpu.SemaphoreType.DMA((left_count + tiles * pieces,)),
        pltpu.SemaphoreType.DMA((sides, count)),
    ]


def weight_grad_kernel(left_count, right_counts, out_count, place_ref, *refs):
    lefts, refs = refs[:left_count], refs[left_count:]
    rights = []
    for count in right_counts:
        rights.append(refs[:count])
        refs = refs[count:]
    outs, (left, right, whole, sems, out_sems) = refs[:-5], refs[-5:]
    number = 0

    def fetch(pieces, dest, *lanes):
        nonlocal number
        copies, start = [], 0
        for piece in pieces:
            rows = piece.shape[0]
            source = piece.at[:, lanes[0]] if lanes else piece
            target = dest.at[(pl.ds(start, rows),) + lanes]
            copies.append(pltpu.make_async_copy(source, target, sems.at[number]))
            number += 1
            start += rows
        for copy in copies:
            copy.start()
        return copies

    tiles = tiles_of(whole.shape[-1], 512)
    first = fetch(lefts, left)
    waits = [
        [fetch(pieces, right.at[index], pl.ds(lane, size)) for lane, size in tiles]
        for index, pieces in enumerate(rights)
    ]
    wait_all(first)
    cuts = []
    for index, pieces in enumerate(rights):
        for copies, (lane, size) in zip(waits[index], tiles):
            wait_all(copies)
            lanes = slice(lane, lane + size)
            whole[index, :, lanes] = dot_tn(left[...], right[index, :, lanes]).astype(BF16)
        cuts += start_cutting(
            whole.at[index],
            outs[index * out_count : (index + 1) * out_count],
            out_sems.at[index],
            0,
            place_ref[0],
        )
    wait_all(cuts)


def weight_grad(place, lefts, *rights):
    height, width = lefts[0].shape[1], rights[0][0].shape[1]
    rows = sum(piece.shape[0] for piece in lefts)
    count = lax.axis_size("seq")
    cuts = cut_shapes(height, width, count)
    pieces = [piece for side in rights for piece in side]
    sides = [len(side) for side in rights]
    outs = call(
        functools.partial(
            weight_grad_kernel, len(lefts), tuple(len(side) for side in rights), len(cuts)
        ),
        cuts * len(rights),
        [ANY_SPEC] * (len(cuts) * len(rights)),
        [place] + list(lefts) + pieces,
        [SMEM_SPEC] + [ANY_SPEC] * (len(lefts) + len(pieces)),
        weight_grad_scratch(rows, height, width, len(lefts), sides, count),
        flops=2 * rows * height * width * len(rights),
        moved=2 * (rows * (height + width) + height * width) * len(rights),
    )
    return [outs[start : start + len(cuts)] for start in range(0, len(outs), len(cuts))]


def attend_back_kernel(
    where,
    ref_count,
    head_count,
    place_ref,
    own_ref,
    came_ref,
    middle_ref,
    upstream_ref,
    attn_out_ref,
    gains_ref,
    query_ref,
    keys_ref,
    probs_ref,
    *refs,
):
    parts, refs = refs[:ref_count], refs[ref_count:]
    d_middle_ref, d_attn_ref, d_rotated_ref, far_halo_ref, back_halo_ref, near_ref, rows_ref = refs[:7]
    weights, d_keys, sems = refs[7:]
    rows, width = middle_ref.shape
    head_dim = keys_ref.shape[1] // 2
    heads_width = head_count * head_dim
    score_scale = head_dim**-0.5
    out_start = parts[0].shape[-1] - heads_width
    copies = start_placing(where, parts, weights, sems, 0, place_ref[0], out_start, heads_width)
    total = own_ref[...].astype(F32) + came_ref[...].astype(F32)
    middle = middle_ref[...]
    scale = inverse_rms(middle)
    back, grad_fn = norm_back(middle * scale, scale, gains_ref[2:3, :], total)
    d_middle = upstream_ref[...].astype(F32) + back
    d_middle_ref[...] = d_middle
    attn_out = attn_out_ref[...]
    scale = inverse_rms(attn_out)
    d_attn_out, grad_ap = norm_back(attn_out * scale, scale, gains_ref[1:2, :], d_middle)
    row = iota((8, width), 0)
    rows_ref[...] = jnp.where(row == 1, grad_ap, 0.0) + jnp.where(row == 2, grad_fn, 0.0)
    d_attn_low = d_attn_out.astype(BF16)
    d_attn_ref[...] = d_attn_low
    wait_all(copies)
    for head in range(head_count):
        lanes = slice(head * head_dim, (head + 1) * head_dim)
        d_attended = dot(d_attn_low, weights[:, lanes]).astype(BF16)
        probs_low = probs_ref[head * rows : (head + 1) * rows, :]
        probs = probs_low.astype(F32)
        d_probs = dot_t(d_attended, keys_ref[:, head_dim:])
        delta = jnp.sum(probs * d_probs, axis=-1, keepdims=True)
        d_scores = (probs * (d_probs - delta) * score_scale).astype(BF16)
        d_rotated_ref[:, lanes] = dot(d_scores, keys_ref[:, :head_dim])
        d_key = dot_tn(d_scores, query_ref[:, lanes])
        d_value = dot_tn(probs_low, d_attended)
        if head == 0:
            d_keys[:, :head_dim] = d_key
            d_keys[:, head_dim:] = d_value
        else:
            d_keys[:, :head_dim] += d_key
            d_keys[:, head_dim:] += d_value
    far_halo_ref[...] = d_keys[:rows, :].astype(BF16)
    back_halo_ref[...] = d_keys[rows : 2 * rows, :].astype(BF16)
    near_ref[...] = d_keys[2 * rows :, :]


def attend_back(place, sums, saved, parts, head_count):
    middle, upstream, attn_out, gains, query, keys, probs = saved
    rows, width = middle.shape
    head_dim = keys.shape[1] // 2
    heads_width = head_count * head_dim
    outs = [
        shape_of((rows, width), F32),
        shape_of((rows, width), BF16),
        shape_of((rows, heads_width), F32),
        shape_of((rows, 2 * head_dim), BF16),
        shape_of((rows, 2 * head_dim), BF16),
        shape_of((rows, 2 * head_dim), F32),
        shape_of((8, width), F32),
    ]
    ins = [place] + list(sums) + list(saved) + parts.arrays
    return call(
        functools.partial(attend_back_kernel, parts.where, len(parts.arrays), head_count),
        outs,
        [VMEM_SPEC] * 7,
        ins,
        [SMEM_SPEC] + [VMEM_SPEC] * 9 + [ANY_SPEC] * len(parts.arrays),
        [
            pltpu.VMEM((width, heads_width), BF16),
            pltpu.VMEM((3 * rows, 2 * head_dim), F32),
            pltpu.SemaphoreType.DMA((slots(parts.where),)),
        ],
        flops=2 * rows * width * heads_width + 30 * rows * rows * heads_width,
        moved=2 * width * heads_width + 24 * rows * width,
    )


def heads_kernel(
    where,
    ref_count,
    out_count,
    head_count,
    place_ref,
    d_attn_ref,
    attended_ref,
    attn_in_ref,
    d_rotated_ref,
    query_lin_ref,
    small_gains_ref,
    cos_ref,
    sin_ref,
    *refs,
):
    parts, refs = refs[:ref_count], refs[ref_count:]
    grads, refs = refs[:out_count], refs[out_count:]
    d_in_ref, query_gain_ref, weights, whole, d_query, sems, out_sems = refs
    rows, width = attn_in_ref.shape
    heads_width = attended_ref.shape[1]
    head_dim = heads_width // head_count
    seq = place_ref[0]
    copies = start_placing(where, parts, weights, sems, 0, seq, 0, heads_width)
    for start, size in tiles_of(heads_width, 512):
        lanes = slice(start, start + size)
        whole[0, :, lanes] = dot_tn(d_attn_ref[...], attended_ref[:, lanes]).astype(BF16)
    cuts = start_cutting(whole.at[0], grads, out_sems.at[0], 0, seq, 0)
    cosine, sine = cos_ref[2 * rows :, :], sin_ref[2 * rows :, :]
    gain_q = small_gains_ref[4:5, :]
    query_gain = jnp.zeros((1, head_dim), F32)
    for head in range(head_count):
        lanes = slice(head * head_dim, (head + 1) * head_dim)
        query_lin = query_lin_ref[:, lanes]
        scale = inverse_rms(query_lin)
        d_normed = rotate(d_rotated_ref[:, lanes], cosine, -sine)
        back, gain_grad = norm_back(query_lin * scale, scale, gain_q, d_normed)
        query_gain = query_gain + gain_grad
        d_query[:, lanes] = back.astype(BF16)
    query_gain_ref[...] = query_gain
    for start, size in tiles_of(heads_width, 512):
        lanes = slice(start, start + size)
        whole[1, :, lanes] = dot_tn(attn_in_ref[...], d_query[:, lanes]).astype(BF16)
    cuts += start_cutting(whole.at[1], grads, out_sems.at[1], 0, seq, 1)
    wait_all(copies)
    for start, size in tiles_of(width, 384):
        lanes = slice(start, start + size)
        d_in_ref[:, lanes] = dot_t(d_query[...], weights[lanes, :])
    wait_all(cuts)


def heads_back(place, ins, parts, head_count):
    attn_in, attended, small_gains = ins[2], ins[1], ins[5]
    rows, width = attn_in.shape
    heads_width, head_dim = attended.shape[1], small_gains.shape[1]
    count = lax.axis_size("seq")
    cuts = [
        shape_of((2,) + part.shape, BF16) for part in cut_shapes(width, heads_width, count)
    ]
    return call(
        functools.partial(
            heads_kernel, parts.where, len(parts.arrays), len(cuts), head_count
        ),
        cuts + [shape_of((rows, width), F32), shape_of((1, head_dim), F32)],
        [ANY_SPEC] * len(cuts) + [VMEM_SPEC] * 2,
        [place] + list(ins) + parts.arrays,
        [SMEM_SPEC] + [VMEM_SPEC] * 8 + [ANY_SPEC] * len(parts.arrays),
        [
            pltpu.VMEM((width, heads_width), BF16),
            pltpu.VMEM((2, width, heads_width), BF16),
            pltpu.VMEM((rows, heads_width), BF16),
            pltpu.SemaphoreType.DMA((slots(parts.where),)),
            pltpu.SemaphoreType.DMA((2, count)),
        ],
        flops=6 * rows * width * heads_width,
        moved=8 * width * heads_width,
    )


def finish_kernel(
    where,
    ref_count,
    out_count,
    narrow_rows,
    wide_rows,
    place_ref,
    near_ref,
    back_ref,
    far_ref,
    key_lin_ref,
    small_gains_ref,
    gains_ref,
    cos_ref,
    sin_ref,
    attn_in_ref,
    tokens_ref,
    d_middle_ref,
    d_in_ref,
    rows_ref,
    ffn_post_ref,
    query_gain_ref,
    *refs,
):
    parts, refs = refs[:ref_count], refs[ref_count:]
    grads, (input_grad_ref, first_w, whole, d_low, sems) = refs[:out_count], refs[out_count:]
    rows, width = tokens_ref.shape
    head_dim = key_lin_ref.shape[1]
    seq = place_ref[0]
    heads_width = (parts[0].shape[-1] - 2 * head_dim - LANES) // 2
    copies = start_placing(where, parts, first_w, sems, 0, seq, heads_width, 2 * head_dim)
    d_keys = near_ref[...] + back_ref[...].astype(F32) + far_ref[...].astype(F32)
    key_lin = key_lin_ref[...]
    scale = inverse_rms(key_lin)
    d_normed = rotate(d_keys[:, :head_dim], cos_ref[2 * rows :, :], -sin_ref[2 * rows :, :])
    back, key_gain = norm_back(key_lin * scale, scale, small_gains_ref[5:6, :], d_normed)
    d_low[:, :head_dim] = back.astype(BF16)
    d_low[:, head_dim:] = d_keys[:, head_dim:].astype(BF16)
    whole[:, : 2 * head_dim] = dot_tn(attn_in_ref[...], d_low[...]).astype(BF16)
    wait_all(copies)
    d_attn_in = d_in_ref[...] + dot_t(d_low[...], first_w[...])
    inputs = tokens_ref[...].astype(F32)
    scale = inverse_rms(inputs)
    back, grad_an = norm_back(inputs * scale, scale, gains_ref[0:1, :], d_attn_in)
    input_grad_ref[...] = d_middle_ref[...] + back
    row = iota((8, width), 0)
    gain_rows = rows_ref[...] + jnp.where(row == 0, grad_an, 0.0)
    gain_rows = gain_rows + jnp.where(row == 3, ffn_post_ref[...], 0.0)
    small_row = iota((8, head_dim), 0)
    small = jnp.where(small_row == 4, query_gain_ref[...], 0.0)
    small = small + jnp.where(small_row == 5, key_gain, 0.0)
    spread = spread_matrix(head_dim, width, narrow_rows, wide_rows)
    gain_rows = gain_rows + dot(small.astype(BF16), spread)
    pick = unit((8, LANES), iota((8, LANES), 0) == iota((8, LANES), 1))
    whole[:, 2 * head_dim :] = dot_tn(gain_rows.astype(BF16), pick).astype(BF16)
    wait_all(start_cutting(whole, grads, sems, slots(where), seq))


def finish(place, ins, parts, narrow_rows, wide_rows):
    tokens, key_lin = ins[9], ins[3]
    rows, width = tokens.shape
    head_dim = key_lin.shape[1]
    count = lax.axis_size("seq")
    pack = 2 * head_dim + LANES
    cuts = cut_shapes(width, pack, count)
    return call(
        functools.partial(
            finish_kernel, parts.where, len(parts.arrays), len(cuts), narrow_rows, wide_rows
        ),
        cuts + [shape_of((rows, width), F32)],
        [ANY_SPEC] * len(cuts) + [VMEM_SPEC],
        [place] + list(ins) + parts.arrays,
        [SMEM_SPEC] + [VMEM_SPEC] * len(ins) + [ANY_SPEC] * len(parts.arrays),
        [
            pltpu.VMEM((width, 2 * head_dim), BF16),
            pltpu.VMEM((width, pack), BF16),
            pltpu.VMEM((rows, 2 * head_dim), BF16),
            pltpu.SemaphoreType.DMA((slots(parts.where) + count,)),
        ],
        flops=8 * rows * width * head_dim,
        moved=4 * width * pack + 20 * rows * width,
    )


def layout(lengths, counts, first_slot, row_count):
    starts = jnp.cumsum(lengths) - lengths
    slot_index = first_slot + jnp.arange(row_count, dtype=jnp.int32)
    member = (slot_index[:, None] >= starts[None, :]).astype(jnp.int32)
    document = jnp.sum(member, axis=1) - 1
    onehot = (document[:, None] == jnp.arange(lengths.shape[0], dtype=jnp.int32)[None, :]).astype(
        jnp.int32
    )
    position = slot_index - jnp.sum(onehot * starts[None, :], axis=1)
    padded = jnp.sum(onehot * (lengths - counts)[None, :], axis=1)
    return (position, padded)


def on_device(
    tokens,
    cotangent,
    doc_lengths,
    true_counts,
    w_query,
    w_key,
    w_value,
    w_out,
    w_gate,
    w_up,
    w_down,
    attn_norm_gain,
    query_gain,
    key_gain,
    attn_post_gain,
    ffn_norm_gain,
    ffn_post_gain,
):
    row_count = tokens.shape[1]
    head_dim = w_key.shape[1]
    heads_width = w_query.shape[1]
    head_count = heads_width // head_dim
    seq_index, plane_index = lax.axis_index("seq"), lax.axis_index("fsdp")
    place = jnp.stack([seq_index, plane_index]).astype(jnp.int32)
    inputs, upstream = tokens[0], cotangent[0]
    wide_rows, narrow_rows = attn_norm_gain.shape[0], query_gain.shape[0]

    planes_count = lax.axis_size("fsdp")
    far_masks = [mask for mask in seq_masks() if mask > 2]

    def swap_far(parts):
        parts = dict(parts)
        for mask in far_masks:
            parts.update({rel ^ mask: swap(part, "seq", mask) for rel, part in parts.items()})
        return parts

    def swap_both(parts, rel):
        if rel not in far_masks:
            return swap(parts[rel], "seq", 2)
        split = (parts[rel].shape[-2] // 2 + 15) // 16 * 16
        top = swap(parts[rel][..., :split, :], "seq", 2)
        bottom = swap(parts[2][..., split:, :], "seq", rel)
        return jnp.concatenate([top, bottom], axis=-2)

    pack = pack_attn(
        w_query,
        w_key,
        w_value,
        w_out,
        [attn_norm_gain, attn_post_gain, ffn_norm_gain, ffn_post_gain],
        [query_gain, key_gain],
    )
    gate_up_own = jnp.stack([w_gate, w_up])
    pack, gate_up_own, inputs, w_down = sync((pack, gate_up_own, inputs, w_down))

    planes = [pack] + [shift(pack, "fsdp", steps) for steps in range(1, planes_count)]
    gate_up_far = swap_far({0: gate_up_own})
    gate_up_half = gate_up_far | {2: swap(gate_up_own, "seq", 2)}
    first_slot = seq_index * row_count
    position, padded = layout(
        doc_lengths[0], true_counts[0], first_slot - WINDOW, row_count + WINDOW
    )
    frequency = ROPE_BASE ** (-2.0 * jnp.arange(head_dim // 2, dtype=F32) / head_dim)
    angles = position.astype(F32)[:, None] * frequency
    cosine, sine = jnp.cos(angles), jnp.sin(angles)
    reach = jnp.clip(position[WINDOW:] - padded[WINDOW:], 0, WINDOW - 1)
    lowest = (WINDOW + jnp.arange(row_count, dtype=jnp.int32) - reach)[:, None]
    lowest = jnp.broadcast_to(lowest, (row_count, LANES))
    state = (planes, cosine, sine, lowest, inputs, w_down)
    planes, cosine, sine, lowest, inputs, w_down = sync(state)
    pack_rows, gate_up_half, inputs, w_down = sync(
        (place_planes(planes, place), gate_up_half, inputs, w_down)
    )

    rows_far = swap_far({0: pack_rows})
    rows_half = rows_far | {2: swap(pack_rows, "seq", 2)}
    behind = from_behind(inputs, 1)
    gate_up_rels, gate_up_core = core_stack(gate_up_half)
    state = (rows_half, behind, gate_up_half, gate_up_core, w_down)
    rows_half, behind, gate_up_half, gate_up_core, w_down = sync(state)
    rows_rest = {rel ^ 2: swap_both(rows_half, rel) for rel in rows_far if rel}
    half_rels, half_core = core_stack(rows_half)
    tokens3 = [inputs, behind, from_behind(behind, 1)]
    state = (rows_half, rows_rest, half_core, tokens3, gate_up_half, w_down)
    rows_half, rows_rest, half_core, tokens3, gate_up_half, w_down = sync(state)
    rest_rels, rest_core = core_stack(rows_rest)
    rest_core, gate_up_half, w_down = sync((rest_core, gate_up_half, w_down))
    cores = [(half_rels, half_core), (rest_rels, rest_core)]
    parts = all_parts(with_cores(plain(rows_half | rows_rest), cores))

    gate_rest = {rel ^ 2: swap(gate_up_half[rel][0], "seq", 2) for rel in gate_up_far if rel}
    up_rest = swap_far({2: gate_up_half[2][1]})
    up_rest = {rel: up_rest[rel] for rel in gate_rest}
    (
        attn_in,
        query_lin,
        key_lin,
        query,
        keys,
        probs,
        attended,
        gains,
        small_gains,
        attn_out,
        middle,
        ffn_in,
    ) = attend(
        place,
        tokens3,
        cosine,
        sine,
        lowest,
        parts,
        head_count,
        head_dim,
        narrow_rows,
        wide_rows,
    )
    ffn_in, gate_rest, up_rest, w_down = sync((ffn_in, gate_rest, up_rest, w_down))

    rest_rels, rest_core = core_stack(
        {rel: jnp.stack([gate_rest[rel], up_rest[rel]]) for rel in gate_rest}
    )
    down_far = swap_far({0: w_down})
    down_half = down_far | {2: swap(w_down, "seq", 2)}
    state = (shift(ffn_in, "fsdp", 1), rest_core, down_half)
    block, rest_core, down_half = sync(state)
    weights = []
    for index, rest in enumerate((gate_rest, up_rest)):
        entries = {rel: (part, (index,)) for rel, part in gate_up_half.items()} | plain(rest)
        for rels, stack in ((gate_up_rels, gate_up_core), (rest_rels, rest_core)):
            entries |= {rel ^ 1: (stack, (place_in, index)) for place_in, rel in enumerate(rels)}
        weights.append(all_parts(entries))
    blocks = [ffn_in, block]
    down_rest = {rel ^ 2: swap_both(down_half, rel) for rel in down_far if rel}
    half_rels, half_core = core_stack(down_half)
    act, gate_slope, up_slope = gate_up(place, blocks[1], weights)
    state = (shift(blocks[1], "fsdp", 1), act, down_rest, half_core)
    block, act, down_rest, half_core = sync(state)
    blocks.append(block)
    rest_rels, rest_core = core_stack(down_rest)
    act, rest_core = sync((act, rest_core))
    cores = [(half_rels, half_core), (rest_rels, rest_core)]
    weights.append(all_parts(with_cores(plain(down_half | down_rest), cores)))
    acts, slopes = {1: act}, {1: (gate_slope, up_slope)}
    partials = {1: sync(down(place, act, weights[2:]))}
    carried = None
    for step in range(2, planes_count + 1):
        state = {}
        if step < planes_count - 1:
            state["block"] = shift(blocks[step], "fsdp", 1)
        leaving = partials[step - 1]
        if carried is not None:
            leaving = add_rounded(leaving, carried)
        index = step % planes_count
        acts[index], gate_slope, up_slope, partials[index] = ffn(place, blocks[index], weights)
        slopes[index] = (gate_slope, up_slope)
        state["carried"] = shift(leaving, "fsdp", 1)
        state, partials = sync((state, partials))
        carried = state["carried"]
        if "block" in state:
            blocks.append(state["block"])
    output, d_ffn_low, grad_fp = turn([partials[0], carried], middle, upstream, gains)

    backs, partials, d_gates, d_ups = [sync(d_ffn_low)], {}, [], []
    carried, down_pair, down_sent = None, None, None
    all_acts = [acts[index] for index in range(planes_count)]
    for step in range(planes_count):
        state = {}
        if step < planes_count - 2:
            state["block"] = shift(backs[step], "fsdp", 1)
        if step == planes_count - 3:
            state["last"] = shift(backs[0], "fsdp", -1)
        if step >= 2:
            leaving = partials[step - 1]
            if carried is not None:
                leaving = add_rounded(leaving, carried)
            state["carried"] = shift(leaving, "fsdp", 1)
        if step == planes_count - 2:
            d_gate, d_up, partials[step], down_pair = ffn_back_and_grad(
                place, backs[step], slopes[step], weights, backs, all_acts
            )
        else:
            d_gate, d_up, partials[step] = ffn_back(place, backs[step], slopes[step], weights)
        if step == planes_count - 1:
            state["down"] = cores_send(down_pair)
        d_gates.append(d_gate)
        d_ups.append(d_up)
        state, partials, d_gates, d_ups, down_pair = sync(
            (state, partials, d_gates, d_ups, down_pair)
        )
        carried = state.get("carried", carried)
        backs += [state[name] for name in ("block", "last") if name in state]
        down_sent = state.get("down")
    carried = shift(add_rounded(partials[planes_count - 1], carried), "fsdp", 1)
    down_part = add_rounded(*down_sent)
    down_terms = [down_part[0]] + straight(down_part, 1, 2)
    gate_pair, up_pair = weight_grad(place, blocks, d_gates, d_ups)
    carried, gate_pair, up_pair, down_terms, down_part = sync(
        (carried, gate_pair, up_pair, down_terms, down_part)
    )

    gate_sent, up_sent = cores_send(gate_pair), cores_send(up_pair)
    down_terms += straight(down_part, *range(3, down_part.shape[0]))
    saved = (middle, upstream, attn_out, gains, query, keys, probs)
    d_middle, d_attn, d_rotated, far_halo, back_halo, near, gain_rows = attend_back(
        place, [partials[0], carried], saved, parts, head_count
    )
    state = (far_halo, back_halo, d_attn, d_rotated, gate_sent, up_sent)
    far_halo, back_halo, d_attn, d_rotated, gate_sent, up_sent = sync(state)
    halos = [from_behind(back_halo, -1), from_behind(far_halo, -2)]
    ins = [d_attn, attended, attn_in, d_rotated, query_lin, small_gains, cosine, sine]
    *head_grads, d_in, query_gain_grad = heads_back(place, ins, parts, head_count)
    gate_cut, up_cut = far_cut(add_rounded(*gate_sent)), across_cut(add_rounded(*up_sent))
    state = (halos, head_grads, gate_cut, up_cut, down_terms)
    halos, head_grads, gate_cut, up_cut, down_terms = sync(state)
    head_sent = cores_send(head_grads)
    gate_sides = (gate_cut[0], swap(gate_cut[1], "seq", far_masks[0]))
    up_sides = (up_cut[0], swap(up_cut[1], "seq", 2))
    ins = [
        near,
        *halos,
        key_lin,
        small_gains,
        gains,
        cosine,
        sine,
        attn_in,
        inputs,
        d_middle,
        d_in,
        gain_rows,
        grad_fp,
        query_gain_grad,
    ]
    *last_grads, input_grad = finish(place, ins, parts, narrow_rows, wide_rows)
    head_part = add_rounded(*head_sent)
    out_cut, query_cut = far_cut(head_part[0]), across_cut(head_part[1])
    last_grads, out_cut, query_cut = sync((last_grads, out_cut, query_cut))
    last_sent = cores_send(last_grads)
    out_sides = (out_cut[0], swap(out_cut[1], "seq", far_masks[0]))
    query_sides = (query_cut[0], swap(query_cut[1], "seq", 2))
    state = (last_sent, out_sides, query_sides, gate_sides, up_sides)
    last_sent, out_sides, query_sides, gate_sides, up_sides = sync(state)
    out_part = add_rounded(*out_sides)
    out_came = swap(out_part[1], "seq", 2)
    query_sides = far_step(add_rounded(*query_sides))
    last_part = add_rounded(*last_sent)
    last_terms = [last_part[0]] + straight(last_part, *range(1, last_part.shape[0]))
    gate_part, up_part = add_rounded(*gate_sides), add_rounded(*up_sides)
    state = (out_part, out_came, query_sides, last_terms, gate_part, up_part)
    out_part, out_came, query_sides, last_terms, gate_part, up_part = sync(state)
    reduced = jnp.concatenate(
        [
            add_rounded(out_part[0], out_came),
            add_rounded(*query_sides)[0],
            add_up(last_terms).astype(BF16),
        ],
        axis=1,
    )
    terms = planes_send(reduced)
    gate_came = swap(gate_part[1], "seq", 2)
    up_sides = far_step(up_part)
    grad_gate = add_up([gate_part[0], gate_came])
    grad_up = add_up(up_sides)[0]
    terms, grad_gate, grad_up = sync((terms, grad_gate, grad_up))
    rows = add_up(terms)
    last_start = 2 * heads_width
    gain_cols = rows[:, last_start + 2 * head_dim :]
    return (
        output[None],
        input_grad[None],
        rows[:, heads_width:last_start],
        rows[:, last_start : last_start + head_dim],
        rows[:, last_start + head_dim : last_start + 2 * head_dim],
        rows[:, :heads_width],
        grad_gate,
        grad_up,
        add_up(down_terms),
        gain_cols[:, 0],
        gain_cols[:narrow_rows, 4],
        gain_cols[:narrow_rows, 5],
        gain_cols[:, 1],
        gain_cols[:, 2],
        gain_cols[:, 3],
    )


def solution(mesh):
    rows = P("fsdp", "seq", None)
    shard, tile, vector = P(("seq", "fsdp"), None), P("seq", "fsdp"), P(("seq", "fsdp"))
    groups = P("fsdp", None)
    return jax.shard_map(
        on_device,
        mesh=mesh,
        in_specs=(rows, rows, groups, groups) + (shard,) * 4 + (tile,) * 3 + (vector,) * 6,
        out_specs=(rows, rows) + (shard,) * 4 + (tile,) * 3 + (vector,) * 6,
        check_vma=False,
    )
```

```python
import functools

import jax
import jax.numpy as jnp
from jax import lax
from jax.experimental import pallas as pl
from jax.experimental.pallas import tpu as pltpu
from jax.sharding import PartitionSpec as P

WINDOW = 512
NORM_EPS = 1e-06
ROPE_BASE = 10000.0
NEGATIVE = -1e30
LANES = 128
VMEM_LIMIT = 32 * 2**20
PIECES = 8
BF16 = jnp.bfloat16
F32 = jnp.float32


def from_behind(value, steps):
    count = lax.axis_size("seq")
    first, last = (max(0, -steps), min(count, count - steps))
    return lax.ppermute(value, "seq", [(source, source + steps) for source in range(first, last)])


def seq_masks():
    return [1 << bit for bit in range(lax.axis_size("seq").bit_length() - 1)]


def swap(value, axis, mask):
    count = lax.axis_size(axis)
    return lax.ppermute(value, axis, [(source, source ^ mask) for source in range(count)])


def shift(value, axis, steps):
    count = lax.axis_size(axis)
    return lax.ppermute(value, axis, [(source, (source + steps) % count) for source in range(count)])


def sync(state):
    return lax.optimization_barrier(state)


class Parts:
    def __init__(self, arrays, where):
        self.arrays, self.where = list(arrays), tuple(where)
        self.width = arrays[0].shape[-1]
        self.rows = arrays[0].shape[-2] * len(where)


def core_stack(parts):
    stack = jnp.stack(list(parts.values())) if len(parts) > 1 else list(parts.values())[0][None]
    return tuple(parts), swap(stack, "seq", 1)


def with_cores(entries, cores):
    for rels, stack in cores:
        entries = entries | {rel ^ 1: (stack, (index,)) for index, rel in enumerate(rels)}
    return entries


def all_parts(entries):
    arrays, places = [], []
    for rel in range(len(entries)):
        array, index = entries[rel]
        number = next((n for n, other in enumerate(arrays) if other is array), len(arrays))
        if number == len(arrays):
            arrays.append(array)
        places.append((number, index))
    if arrays[0].shape[-2] % 16 == 0:
        return Parts(arrays, places)
    index = jnp.arange(len(places), dtype=jnp.int32) ^ lax.axis_index("seq")
    blocks = [arrays[number][block] for number, block in places]
    whole = jnp.take(jnp.stack(blocks), index, axis=0, mode="clip")
    return Parts([whole.reshape(-1, whole.shape[-1])], [(0, ())])


def plain(parts):
    return {rel: (part, ()) for rel, part in parts.items()}


def add_rounded(first, second):
    return (first.astype(F32) + second.astype(F32)).astype(BF16)


def cut(pair, count):
    if len(pair) == 2:
        return pair
    whole = pair[0]
    index = jnp.arange(count, dtype=jnp.int32) ^ lax.axis_index("seq")
    blocks = whole.reshape(whole.shape[:-2] + (count, -1, whole.shape[-1]))
    blocks = jnp.take(blocks, index, axis=blocks.ndim - 3, mode="clip")
    return blocks[..., 0::2, :, :], blocks[..., 1::2, :, :]


def cores_send(pair):
    keep, send = cut(pair, lax.axis_size("seq"))
    return keep, swap(send, "seq", 1)


def far_step(part):
    masks = [mask for mask in seq_masks() if mask > 2][::-1]
    for mask in masks[:-1]:
        half = part.shape[0] // 2
        part = add_rounded(part[:half], swap(part[half:], "seq", mask))
    half = part.shape[0] // 2
    return part[:half], swap(part[half:], "seq", masks[-1])


def across_cut(part):
    part = part.reshape((-1, 2) + part.shape[1:])
    return part[:, 0], part[:, 1]


def across_step(part):
    stays, leaves = across_cut(part)
    return stays, swap(leaves, "seq", 2)


def far_cut(part):
    masks = [mask for mask in seq_masks() if mask > 2][::-1]
    for mask in masks[:-1]:
        half = part.shape[0] // 2
        part = add_rounded(part[:half], swap(part[half:], "seq", mask))
    half = part.shape[0] // 2
    return part[:half], part[half:]


def straight(part, *steps):
    return [swap(part[step], "seq", 2 * step) for step in steps]


def planes_send(rows):
    planes = lax.axis_size("fsdp")
    blocks = rows.reshape((planes, -1) + rows.shape[1:])
    mine = lax.axis_index("fsdp")
    sent = [lax.dynamic_index_in_dim(blocks, mine, 0, keepdims=False)]
    for steps in range(1, planes):
        send = lax.dynamic_index_in_dim(blocks, (mine + steps) % planes, 0, keepdims=False)
        sent.append(shift(send, "fsdp", steps))
    return sent


def add_up(terms):
    total = terms[0].astype(F32)
    for term in terms[1:]:
        total = total + term.astype(F32)
    return total


def dot(left, right):
    return jnp.dot(left, right, preferred_element_type=F32)


def dot_t(left, right):
    return lax.dot_general(left, right, (((1,), (1,)), ((), ())), preferred_element_type=F32)


def dot_tn(left, right):
    return lax.dot_general(left, right, (((0,), (0,)), ((), ())), preferred_element_type=F32)


def inverse_rms(values):
    return lax.rsqrt(jnp.mean(values * values, axis=-1, keepdims=True) + NORM_EPS)


def norm_back(normed, scale, gain, upstream):
    scaled = upstream * gain
    back = scale * (scaled - normed * jnp.mean(scaled * normed, axis=-1, keepdims=True))
    return back, jnp.sum(upstream * normed, axis=0, keepdims=True)


def rotate(values, cosine, sine):
    half = values.shape[-1] // 2
    first, second = values[:, :half], values[:, half:]
    return jnp.concatenate(
        [first * cosine - second * sine, second * cosine + first * sine], axis=-1
    )


def iota(shape, dim):
    return lax.broadcasted_iota(jnp.int32, shape, dim)


def unit(shape, hits):
    return jnp.where(hits, 1.0, 0.0).astype(BF16)


def spread_matrix(narrow, wide, narrow_rows, wide_rows):
    row, col = iota((narrow, wide), 0), iota((narrow, wide), 1)
    return unit((narrow, wide), col == (row // narrow_rows) * wide_rows + row % narrow_rows)


def tiles_of(width, step):
    return [(start, min(step, width - start)) for start in range(0, width, step)]


def slots(where):
    return max(PIECES, len(where))


def start_placing(where, refs, dest, sems, base, seq, lane=0, lanes=None, same=False):
    if same:
        dest = dest.at[:, pl.ds(lane, lanes)]
    copies = []
    if len(where) == 1:
        whole = refs[0] if lanes is None else refs[0].at[:, pl.ds(lane, lanes)]
        count = PIECES if whole.shape[0] % (16 * PIECES) == 0 else 1
        rows = whole.shape[0] // count
        pieces = [(index * rows, whole.at[pl.ds(index * rows, rows), :]) for index in range(count)]
        copies = [
            pltpu.make_async_copy(part, dest.at[pl.ds(start, rows), :], sems.at[base + index])
            for index, (start, part) in enumerate(pieces)
        ]
        for copy in copies:
            copy.start()
        return copies
    for rel, (number, block) in enumerate(where):
        part = refs[number].at[block] if block else refs[number]
        rows = part.shape[0]
        start = pl.multiple_of((seq ^ rel) * rows, 16) if len(where) > 1 else 0
        if lanes is not None:
            part = part.at[:, pl.ds(lane, lanes)]
        copies.append(
            pltpu.make_async_copy(part, dest.at[pl.ds(start, rows), :], sems.at[base + rel])
        )
    for copy in copies:
        copy.start()
    return copies


def start_cutting(whole, outs, sems, base, seq, which=None):
    if which is not None:
        outs = [out.at[which] for out in outs]
    if len(outs) == 1:
        copies = [pltpu.make_async_copy(whole, outs[0], sems.at[base])]
    else:
        half, rows = outs[0].shape[0], outs[0].shape[1]
        copies = []
        for rel in range(2 * half):
            start = pl.multiple_of((seq ^ rel) * rows, 16)
            copies.append(
                pltpu.make_async_copy(
                    whole.at[pl.ds(start, rows), :], outs[rel % 2].at[rel // 2], sems.at[base + rel]
                )
            )
    for copy in copies:
        copy.start()
    return copies


def cut_shapes(height, width, count):
    rows = height // count
    if rows % 16:
        return [jax.ShapeDtypeStruct((height, width), BF16)]
    return [jax.ShapeDtypeStruct((count // 2, rows, width), BF16)] * 2


def wait_all(copies):
    for copy in copies:
        copy.wait()


SMEM_SPEC = pl.BlockSpec(memory_space=pltpu.SMEM)
VMEM_SPEC = pl.BlockSpec(memory_space=pltpu.VMEM)
ANY_SPEC = pl.BlockSpec(memory_space=pl.ANY)


def call(kernel, outs, out_specs, ins, in_specs, scratch=(), flops=0, moved=0, exps=0):
    return pl.pallas_call(
        kernel,
        out_shape=tuple(outs),
        in_specs=list(in_specs),
        out_specs=tuple(out_specs),
        scratch_shapes=list(scratch),
        compiler_params=pltpu.CompilerParams(vmem_limit_bytes=VMEM_LIMIT),
        cost_estimate=pl.CostEstimate(flops=flops, bytes_accessed=moved, transcendentals=exps),
    )(*ins)


def shape_of(dims, dtype):
    return jax.ShapeDtypeStruct(dims, dtype)


def pack_kernel(wq_ref, wk_ref, wv_ref, wo_ref, *refs):
    wide, narrow, out_ref = refs[:4], refs[4:6], refs[6]
    rows, heads_width, head_dim = wq_ref.shape[0], wq_ref.shape[1], wk_ref.shape[1]
    out_ref[:, :heads_width] = wq_ref[...]
    out_ref[:, heads_width : heads_width + head_dim] = wk_ref[...]
    out_ref[:, heads_width + head_dim : heads_width + 2 * head_dim] = wv_ref[...]
    row = iota((16, rows), 0)
    held = jnp.zeros((16, rows), F32)
    for index, ref in enumerate(wide):
        held = held + jnp.where(row == index, ref[...].astype(F32), 0.0)
    small = narrow[0].shape[1]
    fit = unit((small, rows), iota((small, rows), 0) == iota((small, rows), 1))
    for index, ref in enumerate(narrow):
        spread = dot(jnp.broadcast_to(ref[...].astype(F32), (16, small)).astype(BF16), fit)
        held = held + jnp.where(row == 4 + index, spread, 0.0)
    place = unit((16, LANES), iota((16, LANES), 0) == iota((16, LANES), 1))
    gain_start = heads_width + 2 * head_dim
    out_ref[:, gain_start : gain_start + LANES] = dot_tn(held.astype(BF16), place).astype(BF16)
    out_ref[:, gain_start + LANES :] = wo_ref[...]


def pack_attn(w_query, w_key, w_value, w_out, wide, narrow):
    rows = w_query.shape[0]
    width = 2 * w_query.shape[1] + 2 * w_key.shape[1] + LANES
    ins = [w_query, w_key, w_value, w_out] + [vec.reshape(1, -1) for vec in wide + narrow]
    return call(
        pack_kernel,
        [shape_of((rows, width), BF16)],
        [VMEM_SPEC],
        ins,
        [VMEM_SPEC] * len(ins),
    )[0]


def planes_kernel(place_ref, *refs):
    parts, out_ref = refs[:-1], refs[-1]
    count, rows = len(parts), parts[0].shape[0]
    total = None
    for steps, part in enumerate(parts):
        plane = lax.rem(place_ref[1] - steps + count, count)
        row, col = iota((count * rows, rows), 0), iota((count * rows, rows), 1)
        term = dot(unit((count * rows, rows), row == col + plane * rows), part[...])
        total = term if total is None else total + term
    out_ref[...] = total.astype(BF16)


def place_planes(parts, place):
    count = len(parts)
    rows, width = parts[0].shape
    return call(
        planes_kernel,
        [shape_of((count * rows, width), BF16)],
        [VMEM_SPEC],
        [place] + parts,
        [SMEM_SPEC] + [VMEM_SPEC] * count,
        flops=2 * count * count * rows * rows * width,
        moved=4 * count * rows * width,
    )[0]


def attend_kernel(
    where,
    ref_count,
    narrow_rows,
    wide_rows,
    head_count,
    place_ref,
    near_ref,
    back_ref,
    far_ref,
    cos_ref,
    sin_ref,
    low_ref,
    *refs,
):
    parts, refs = refs[:ref_count], refs[ref_count:]
    (
        attn_in_ref,
        query_lin_ref,
        key_lin_ref,
        query_ref,
        keys_ref,
        probs_ref,
        attended_ref,
        gains_ref,
        small_gains_ref,
        attn_out_ref,
        middle_ref,
        ffn_in_ref,
    ) = refs[:12]
    weights, inside, sems = refs[12:]
    rows, width = near_ref.shape
    head_dim = key_lin_ref.shape[1]
    heads_width = head_count * head_dim
    rest = heads_width + 2 * head_dim + LANES
    groups = [(heads_width, rest - heads_width), (0, heads_width), (rest, heads_width)]
    first, second, third = [
        start_placing(
            where, parts, weights, sems, index * slots(where), place_ref[0], lane, lanes, True
        )
        for index, (lane, lanes) in enumerate(groups)
    ]
    score_scale = head_dim**-0.5
    blocks = [far_ref, back_ref, near_ref]
    scales = []
    for ref in blocks:
        scales.append(inverse_rms(ref[...].astype(F32)))
    wait_all(first)
    gain_start = heads_width + 2 * head_dim
    gain_cols = weights[:, gain_start : gain_start + LANES]
    pick = unit((8, LANES), iota((8, LANES), 0) == iota((8, LANES), 1))
    gains = dot_t(pick, gain_cols)
    spread = spread_matrix(head_dim, width, narrow_rows, wide_rows)
    small_gains = dot_t(gains.astype(BF16), spread)
    gains_ref[...] = gains
    small_gains_ref[...] = small_gains
    gain_an, gain_q, gain_k = gains[0:1], small_gains[4:5], small_gains[5:6]
    for index, ref in enumerate(blocks):
        normed = ref[...].astype(F32) * scales[index] * gain_an
        inside[index * rows : (index + 1) * rows, :] = normed.astype(BF16)
    attn_in_ref[...] = inside[2 * rows :, :]
    for index in range(3):
        span = slice(index * rows, (index + 1) * rows)
        part_in = inside[span, :]
        key_lin = dot(part_in, weights[:, heads_width : heads_width + head_dim])
        value = dot(part_in, weights[:, heads_width + head_dim : heads_width + 2 * head_dim])
        key = rotate(key_lin * inverse_rms(key_lin) * gain_k, cos_ref[span, :], sin_ref[span, :])
        keys_ref[span, :head_dim] = key.astype(BF16)
        keys_ref[span, head_dim:] = value.astype(BF16)
        if index == 2:
            key_lin_ref[...] = key_lin
    cosine, sine = cos_ref[2 * rows :, :], sin_ref[2 * rows :, :]
    column = iota((rows, 3 * rows), 1)
    seen = (column >= low_ref[:, :1]) & (column <= iota((rows, 3 * rows), 0) + 2 * rows)
    wait_all(second)
    for start, size in tiles_of(heads_width, 512):
        lanes = slice(start, start + size)
        query_lin_ref[:, lanes] = dot(inside[2 * rows :, :], weights[:, lanes])
    for head in range(head_count):
        lanes = slice(head * head_dim, (head + 1) * head_dim)
        query_lin = query_lin_ref[:, lanes]
        query = rotate(query_lin * inverse_rms(query_lin) * gain_q, cosine, sine).astype(BF16)
        query_ref[:, lanes] = query
        scores = jnp.where(seen, dot_t(query, keys_ref[:, :head_dim]) * score_scale, NEGATIVE)
        raised = jnp.exp(scores - jnp.max(scores, axis=-1, keepdims=True))
        probs = (raised * (1.0 / jnp.sum(raised, axis=-1, keepdims=True))).astype(BF16)
        probs_ref[head * rows : (head + 1) * rows, :] = probs
        attended_ref[:, lanes] = dot(probs, keys_ref[:, head_dim:]).astype(BF16)
    wait_all(third)
    for start, size in tiles_of(width, 384):
        attn_out_ref[:, start : start + size] = dot_t(
            attended_ref[...], weights[start : start + size, gain_start + LANES :]
        )
    attn_out = attn_out_ref[...]
    middle = near_ref[...].astype(F32) + attn_out * inverse_rms(attn_out) * gains[1:2]
    middle_ref[...] = middle
    ffn_in_ref[...] = (middle * inverse_rms(middle) * gains[2:3]).astype(BF16)


def attend(place, tokens3, cosine, sine, lowest, parts, head_count, head_dim, narrow_rows, wide_rows):
    rows, width = tokens3[0].shape
    heads_width = head_count * head_dim
    pack = parts.width
    outs = [
        shape_of((rows, width), BF16),
        shape_of((rows, heads_width), F32),
        shape_of((rows, head_dim), F32),
        shape_of((rows, heads_width), BF16),
        shape_of((3 * rows, 2 * head_dim), BF16),
        shape_of((head_count * rows, 3 * rows), BF16),
        shape_of((rows, heads_width), BF16),
        shape_of((8, width), F32),
        shape_of((8, head_dim), F32),
        shape_of((rows, width), F32),
        shape_of((rows, width), F32),
        shape_of((rows, width), BF16),
    ]
    return call(
        functools.partial(
            attend_kernel, parts.where, len(parts.arrays), narrow_rows, wide_rows, head_count
        ),
        outs,
        [VMEM_SPEC] * len(outs),
        [place] + list(tokens3) + [cosine, sine, lowest] + parts.arrays,
        [SMEM_SPEC] + [VMEM_SPEC] * 6 + [ANY_SPEC] * len(parts.arrays),
        [
            pltpu.VMEM((width, pack), BF16),
            pltpu.VMEM((3 * rows, width), BF16),
            pltpu.SemaphoreType.DMA((3 * slots(parts.where),)),
        ],
        flops=2 * rows * width * (heads_width + 6 * head_dim) + 12 * rows * rows * heads_width,
        moved=2 * width * pack + 16 * rows * width,
        exps=3 * head_count * rows * rows,
    )


def gelu_pair(gate):
    square = gate * gate
    tanh = jnp.tanh(gate * (0.7978845608028654 + 0.035677408136300125 * square))
    half = 0.5 + 0.5 * tanh
    value = gate * half
    slope = half + value * (1.0 - tanh) * (0.7978845608028654 + 0.10703222440890037 * square)
    return value, slope


def take_parts(wheres, counts, refs):
    parts = []
    for count in counts:
        parts.append(refs[:count])
        refs = refs[count:]
    bases = [sum(slots(where) for where in wheres[:index]) for index in range(len(wheres))]
    return parts, bases, refs


def parts_of(weights):
    wheres = tuple(parts.where for parts in weights)
    counts = tuple(len(parts.arrays) for parts in weights)
    arrays = [array for parts in weights for array in parts.arrays]
    return wheres, counts, arrays, sum(slots(where) for where in wheres)


def gate_up_body(rows_ref, gate_w, up_w, act_ref, gate_slope_ref, up_slope_ref):
    rows_in = rows_ref[...]
    for start, size in tiles_of(gate_w.shape[1], 256):
        lanes = slice(start, start + size)
        gate = dot(rows_in, gate_w[:, lanes])
        up = dot(rows_in, up_w[:, lanes])
        value, slope = gelu_pair(gate)
        act_ref[:, lanes] = (value * up).astype(BF16)
        gate_slope_ref[:, lanes] = (slope * up).astype(BF16)
        up_slope_ref[:, lanes] = value.astype(BF16)


def down_body(act_ref, down_w, out_ref):
    for start, size in tiles_of(down_w.shape[0], 384):
        lanes = slice(start, start + size)
        out_ref[:, lanes] = dot_t(act_ref[...], down_w[lanes, :]).astype(BF16)


def ffn_kernel(wheres, counts, place_ref, rows_ref, *refs):
    parts, bases, refs = take_parts(wheres, counts, refs)
    act_ref, gate_slope_ref, up_slope_ref, out_ref, gate_w, up_w, down_w, sems = refs
    seq = place_ref[0]
    copies = start_placing(wheres[0], parts[0], gate_w, sems, bases[0], seq)
    copies += start_placing(wheres[1], parts[1], up_w, sems, bases[1], seq)
    later = start_placing(wheres[2], parts[2], down_w, sems, bases[2], seq)
    wait_all(copies)
    gate_up_body(rows_ref, gate_w, up_w, act_ref, gate_slope_ref, up_slope_ref)
    wait_all(later)
    down_body(act_ref, down_w, out_ref)


def gate_up_kernel(wheres, counts, place_ref, rows_ref, *refs):
    parts, bases, refs = take_parts(wheres, counts, refs)
    act_ref, gate_slope_ref, up_slope_ref, gate_w, up_w, sems = refs
    seq = place_ref[0]
    copies = start_placing(wheres[0], parts[0], gate_w, sems, bases[0], seq)
    copies += start_placing(wheres[1], parts[1], up_w, sems, bases[1], seq)
    wait_all(copies)
    gate_up_body(rows_ref, gate_w, up_w, act_ref, gate_slope_ref, up_slope_ref)


def gate_up(place, rows_in, weights):
    rows, width = rows_in.shape
    hidden = weights[0].width
    wheres, counts, arrays, sem_count = parts_of(weights)
    return call(
        functools.partial(gate_up_kernel, wheres, counts),
        [shape_of((rows, hidden), BF16)] * 3,
        [VMEM_SPEC] * 3,
        [place, rows_in] + arrays,
        [SMEM_SPEC, VMEM_SPEC] + [ANY_SPEC] * len(arrays),
        [pltpu.VMEM((width, hidden), BF16)] * 2 + [pltpu.SemaphoreType.DMA((sem_count,))],
        flops=4 * rows * hidden * width,
        moved=4 * width * hidden + 6 * rows * hidden,
    )


def down_kernel(wheres, counts, place_ref, act_ref, *refs):
    parts, bases, refs = take_parts(wheres, counts, refs)
    out_ref, down_w, sems = refs
    wait_all(start_placing(wheres[0], parts[0], down_w, sems, bases[0], place_ref[0]))
    down_body(act_ref, down_w, out_ref)


def down(place, act, weights):
    rows, hidden = act.shape
    width = weights[0].rows
    wheres, counts, arrays, sem_count = parts_of(weights)
    return call(
        functools.partial(down_kernel, wheres, counts),
        [shape_of((rows, width), BF16)],
        [VMEM_SPEC],
        [place, act] + arrays,
        [SMEM_SPEC, VMEM_SPEC] + [ANY_SPEC] * len(arrays),
        [pltpu.VMEM((width, hidden), BF16), pltpu.SemaphoreType.DMA((sem_count,))],
        flops=2 * rows * hidden * width,
        moved=2 * width * hidden + 2 * rows * hidden,
    )[0]


def ffn(place, rows_in, weights):
    rows, width = rows_in.shape
    hidden = weights[0].width
    wheres, counts, arrays, sem_count = parts_of(weights)
    return call(
        functools.partial(ffn_kernel, wheres, counts),
        [shape_of((rows, hidden), BF16)] * 3 + [shape_of((rows, width), BF16)],
        [VMEM_SPEC] * 4,
        [place, rows_in] + arrays,
        [SMEM_SPEC, VMEM_SPEC] + [ANY_SPEC] * len(arrays),
        [pltpu.VMEM((width, hidden), BF16)] * 3 + [pltpu.SemaphoreType.DMA((sem_count,))],
        flops=6 * rows * hidden * width,
        moved=6 * width * hidden + 8 * rows * hidden,
    )


def turn_kernel(own_ref, came_ref, middle_ref, upstream_ref, gains_ref, *outs):
    output_ref, back_ref, gain_grad_ref = outs
    total = own_ref[...].astype(F32) + came_ref[...].astype(F32)
    scale = inverse_rms(total)
    normed = total * scale
    gain = gains_ref[3:4, :]
    output_ref[...] = (middle_ref[...] + normed * gain).astype(BF16)
    back, gain_grad = norm_back(normed, scale, gain, upstream_ref[...].astype(F32))
    back_ref[...] = back.astype(BF16)
    gain_grad_ref[...] = gain_grad


def turn(sums, middle, upstream, gains):
    rows, width = middle.shape
    return call(
        turn_kernel,
        [shape_of((rows, width), BF16), shape_of((rows, width), BF16), shape_of((1, width), F32)],
        [VMEM_SPEC] * 3,
        list(sums) + [middle, upstream, gains],
        [VMEM_SPEC] * 5,
        moved=20 * rows * width,
    )


def ffn_back_kernel(
    wheres, counts, place_ref, back_ref, gate_slope_ref, up_slope_ref, *refs
):
    parts, bases, refs = take_parts(wheres, counts, refs)
    d_gate_ref, d_up_ref, out_ref, gate_w, up_w, down_w, sems = refs
    seq = place_ref[0]
    copies = start_placing(wheres[2], parts[2], down_w, sems, bases[2], seq)
    later = start_placing(wheres[0], parts[0], gate_w, sems, bases[0], seq)
    later += start_placing(wheres[1], parts[1], up_w, sems, bases[1], seq)
    wait_all(copies)
    back = back_ref[...]
    for start, size in tiles_of(down_w.shape[1], 256):
        lanes = slice(start, start + size)
        d_act = dot(back, down_w[:, lanes])
        d_gate_ref[:, lanes] = (d_act * gate_slope_ref[:, lanes].astype(F32)).astype(BF16)
        d_up_ref[:, lanes] = (d_act * up_slope_ref[:, lanes].astype(F32)).astype(BF16)
    wait_all(later)
    for start, size in tiles_of(gate_w.shape[0], 384):
        lanes = slice(start, start + size)
        total = dot_t(d_gate_ref[...], gate_w[lanes, :])
        out_ref[:, lanes] = (total + dot_t(d_up_ref[...], up_w[lanes, :])).astype(BF16)


def ffn_back(place, back, slopes, weights):
    rows, width = back.shape
    hidden = weights[0].width
    wheres, counts, arrays, sem_count = parts_of(weights)
    return call(
        functools.partial(ffn_back_kernel, wheres, counts),
        [shape_of((rows, hidden), BF16)] * 2 + [shape_of((rows, width), BF16)],
        [VMEM_SPEC] * 3,
        [place, back] + list(slopes) + arrays,
        [SMEM_SPEC] + [VMEM_SPEC] * 3 + [ANY_SPEC] * len(arrays),
        [pltpu.VMEM((width, hidden), BF16)] * 3 + [pltpu.SemaphoreType.DMA((sem_count,))],
        flops=6 * rows * hidden * width,
        moved=6 * width * hidden + 12 * rows * hidden,
    )


def ffn_back_and_grad_kernel(in_counts, out_count, back_kernel, grad_kernel, place_ref, *refs):
    back_ins, refs = refs[: in_counts[0]], refs[in_counts[0] :]
    grad_ins, refs = refs[: in_counts[1]], refs[in_counts[1] :]
    back_outs, refs = refs[:3], refs[3:]
    grad_outs, refs = refs[:out_count], refs[out_count:]
    back_kernel(place_ref, *back_ins, *back_outs, *refs[:4])
    grad_kernel(place_ref, *grad_ins, *grad_outs, *refs[4:])


def ffn_back_and_grad(place, back, slopes, weights, lefts, rights):
    rows, width = back.shape
    hidden = weights[0].width
    wheres, counts, arrays, sem_count = parts_of(weights)
    count = lax.axis_size("seq")
    cuts = cut_shapes(width, hidden, count)
    all_rows = sum(piece.shape[0] for piece in lefts)
    grad_ins = list(lefts) + list(rights)
    back_ins = [back] + list(slopes) + arrays
    outs = call(
        functools.partial(
            ffn_back_and_grad_kernel,
            (len(back_ins), len(grad_ins)),
            len(cuts),
            functools.partial(ffn_back_kernel, wheres, counts),
            functools.partial(weight_grad_kernel, len(lefts), (len(rights),), len(cuts)),
        ),
        [shape_of((rows, hidden), BF16)] * 2 + [shape_of((rows, width), BF16)] + cuts,
        [VMEM_SPEC] * 3 + [ANY_SPEC] * len(cuts),
        [place] + back_ins + grad_ins,
        [SMEM_SPEC] + [VMEM_SPEC] * 3 + [ANY_SPEC] * (len(arrays) + len(grad_ins)),
        [pltpu.VMEM((width, hidden), BF16)] * 3
        + [pltpu.SemaphoreType.DMA((sem_count,))]
        + weight_grad_scratch(all_rows, width, hidden, len(lefts), [len(rights)], count),
        flops=2 * all_rows * width * hidden + 6 * rows * width * hidden,
        moved=8 * width * hidden,
    )
    return outs[0], outs[1], outs[2], outs[3:]


def weight_grad_scratch(rows, height, width, left_count, right_counts, count):
    sides, pieces = len(right_counts), sum(right_counts)
    tiles = len(tiles_of(width, 512))
    return [
        pltpu.VMEM((rows, height), BF16),
        pltpu.VMEM((sides, rows, width), BF16),
        pltpu.VMEM((sides, height, width), BF16),
        pltpu.SemaphoreType.DMA((left_count + tiles * pieces,)),
        pltpu.SemaphoreType.DMA((sides, count)),
    ]


def weight_grad_kernel(left_count, right_counts, out_count, place_ref, *refs):
    lefts, refs = refs[:left_count], refs[left_count:]
    rights = []
    for count in right_counts:
        rights.append(refs[:count])
        refs = refs[count:]
    outs, (left, right, whole, sems, out_sems) = refs[:-5], refs[-5:]
    number = 0

    def fetch(pieces, dest, *lanes):
        nonlocal number
        copies, start = [], 0
        for piece in pieces:
            rows = piece.shape[0]
            source = piece.at[:, lanes[0]] if lanes else piece
            target = dest.at[(pl.ds(start, rows),) + lanes]
            copies.append(pltpu.make_async_copy(source, target, sems.at[number]))
            number += 1
            start += rows
        for copy in copies:
            copy.start()
        return copies

    tiles = tiles_of(whole.shape[-1], 512)
    first = fetch(lefts, left)
    waits = [
        [fetch(pieces, right.at[index], pl.ds(lane, size)) for lane, size in tiles]
        for index, pieces in enumerate(rights)
    ]
    wait_all(first)
    cuts = []
    for index, pieces in enumerate(rights):
        for copies, (lane, size) in zip(waits[index], tiles):
            wait_all(copies)
            lanes = slice(lane, lane + size)
            whole[index, :, lanes] = dot_tn(left[...], right[index, :, lanes]).astype(BF16)
        cuts += start_cutting(
            whole.at[index],
            outs[index * out_count : (index + 1) * out_count],
            out_sems.at[index],
            0,
            place_ref[0],
        )
    wait_all(cuts)


def weight_grad(place, lefts, *rights):
    height, width = lefts[0].shape[1], rights[0][0].shape[1]
    rows = sum(piece.shape[0] for piece in lefts)
    count = lax.axis_size("seq")
    cuts = cut_shapes(height, width, count)
    pieces = [piece for side in rights for piece in side]
    sides = [len(side) for side in rights]
    outs = call(
        functools.partial(
            weight_grad_kernel, len(lefts), tuple(len(side) for side in rights), len(cuts)
        ),
        cuts * len(rights),
        [ANY_SPEC] * (len(cuts) * len(rights)),
        [place] + list(lefts) + pieces,
        [SMEM_SPEC] + [ANY_SPEC] * (len(lefts) + len(pieces)),
        weight_grad_scratch(rows, height, width, len(lefts), sides, count),
        flops=2 * rows * height * width * len(rights),
        moved=2 * (rows * (height + width) + height * width) * len(rights),
    )
    return [outs[start : start + len(cuts)] for start in range(0, len(outs), len(cuts))]


def attend_back_kernel(
    where,
    ref_count,
    head_count,
    place_ref,
    own_ref,
    came_ref,
    middle_ref,
    upstream_ref,
    attn_out_ref,
    gains_ref,
    query_ref,
    keys_ref,
    probs_ref,
    *refs,
):
    parts, refs = refs[:ref_count], refs[ref_count:]
    d_middle_ref, d_attn_ref, d_rotated_ref, far_halo_ref, back_halo_ref, near_ref, rows_ref = refs[:7]
    weights, d_keys, sems = refs[7:]
    rows, width = middle_ref.shape
    head_dim = keys_ref.shape[1] // 2
    heads_width = head_count * head_dim
    score_scale = head_dim**-0.5
    out_start = parts[0].shape[-1] - heads_width
    copies = start_placing(where, parts, weights, sems, 0, place_ref[0], out_start, heads_width)
    total = own_ref[...].astype(F32) + came_ref[...].astype(F32)
    middle = middle_ref[...]
    scale = inverse_rms(middle)
    back, grad_fn = norm_back(middle * scale, scale, gains_ref[2:3, :], total)
    d_middle = upstream_ref[...].astype(F32) + back
    d_middle_ref[...] = d_middle
    attn_out = attn_out_ref[...]
    scale = inverse_rms(attn_out)
    d_attn_out, grad_ap = norm_back(attn_out * scale, scale, gains_ref[1:2, :], d_middle)
    row = iota((8, width), 0)
    rows_ref[...] = jnp.where(row == 1, grad_ap, 0.0) + jnp.where(row == 2, grad_fn, 0.0)
    d_attn_low = d_attn_out.astype(BF16)
    d_attn_ref[...] = d_attn_low
    wait_all(copies)
    for head in range(head_count):
        lanes = slice(head * head_dim, (head + 1) * head_dim)
        d_attended = dot(d_attn_low, weights[:, lanes]).astype(BF16)
        probs_low = probs_ref[head * rows : (head + 1) * rows, :]
        probs = probs_low.astype(F32)
        d_probs = dot_t(d_attended, keys_ref[:, head_dim:])
        delta = jnp.sum(probs * d_probs, axis=-1, keepdims=True)
        d_scores = (probs * (d_probs - delta) * score_scale).astype(BF16)
        d_rotated_ref[:, lanes] = dot(d_scores, keys_ref[:, :head_dim])
        d_key = dot_tn(d_scores, query_ref[:, lanes])
        d_value = dot_tn(probs_low, d_attended)
        if head == 0:
            d_keys[:, :head_dim] = d_key
            d_keys[:, head_dim:] = d_value
        else:
            d_keys[:, :head_dim] += d_key
            d_keys[:, head_dim:] += d_value
    far_halo_ref[...] = d_keys[:rows, :].astype(BF16)
    back_halo_ref[...] = d_keys[rows : 2 * rows, :].astype(BF16)
    near_ref[...] = d_keys[2 * rows :, :]


def attend_back(place, sums, saved, parts, head_count):
    middle, upstream, attn_out, gains, query, keys, probs = saved
    rows, width = middle.shape
    head_dim = keys.shape[1] // 2
    heads_width = head_count * head_dim
    outs = [
        shape_of((rows, width), F32),
        shape_of((rows, width), BF16),
        shape_of((rows, heads_width), F32),
        shape_of((rows, 2 * head_dim), BF16),
        shape_of((rows, 2 * head_dim), BF16),
        shape_of((rows, 2 * head_dim), F32),
        shape_of((8, width), F32),
    ]
    ins = [place] + list(sums) + list(saved) + parts.arrays
    return call(
        functools.partial(attend_back_kernel, parts.where, len(parts.arrays), head_count),
        outs,
        [VMEM_SPEC] * 7,
        ins,
        [SMEM_SPEC] + [VMEM_SPEC] * 9 + [ANY_SPEC] * len(parts.arrays),
        [
            pltpu.VMEM((width, heads_width), BF16),
            pltpu.VMEM((3 * rows, 2 * head_dim), F32),
            pltpu.SemaphoreType.DMA((slots(parts.where),)),
        ],
        flops=2 * rows * width * heads_width + 30 * rows * rows * heads_width,
        moved=2 * width * heads_width + 24 * rows * width,
    )


def heads_kernel(
    where,
    ref_count,
    out_count,
    head_count,
    place_ref,
    d_attn_ref,
    attended_ref,
    attn_in_ref,
    d_rotated_ref,
    query_lin_ref,
    small_gains_ref,
    cos_ref,
    sin_ref,
    *refs,
):
    parts, refs = refs[:ref_count], refs[ref_count:]
    grads, refs = refs[:out_count], refs[out_count:]
    d_in_ref, query_gain_ref, weights, whole, d_query, sems, out_sems = refs
    rows, width = attn_in_ref.shape
    heads_width = attended_ref.shape[1]
    head_dim = heads_width // head_count
    seq = place_ref[0]
    copies = start_placing(where, parts, weights, sems, 0, seq, 0, heads_width)
    for start, size in tiles_of(heads_width, 512):
        lanes = slice(start, start + size)
        whole[0, :, lanes] = dot_tn(d_attn_ref[...], attended_ref[:, lanes]).astype(BF16)
    cuts = start_cutting(whole.at[0], grads, out_sems.at[0], 0, seq, 0)
    cosine, sine = cos_ref[2 * rows :, :], sin_ref[2 * rows :, :]
    gain_q = small_gains_ref[4:5, :]
    query_gain = jnp.zeros((1, head_dim), F32)
    for head in range(head_count):
        lanes = slice(head * head_dim, (head + 1) * head_dim)
        query_lin = query_lin_ref[:, lanes]
        scale = inverse_rms(query_lin)
        d_normed = rotate(d_rotated_ref[:, lanes], cosine, -sine)
        back, gain_grad = norm_back(query_lin * scale, scale, gain_q, d_normed)
        query_gain = query_gain + gain_grad
        d_query[:, lanes] = back.astype(BF16)
    query_gain_ref[...] = query_gain
    for start, size in tiles_of(heads_width, 512):
        lanes = slice(start, start + size)
        whole[1, :, lanes] = dot_tn(attn_in_ref[...], d_query[:, lanes]).astype(BF16)
    cuts += start_cutting(whole.at[1], grads, out_sems.at[1], 0, seq, 1)
    wait_all(copies)
    for start, size in tiles_of(width, 384):
        lanes = slice(start, start + size)
        d_in_ref[:, lanes] = dot_t(d_query[...], weights[lanes, :])
    wait_all(cuts)


def heads_back(place, ins, parts, head_count):
    attn_in, attended, small_gains = ins[2], ins[1], ins[5]
    rows, width = attn_in.shape
    heads_width, head_dim = attended.shape[1], small_gains.shape[1]
    count = lax.axis_size("seq")
    cuts = [
        shape_of((2,) + part.shape, BF16) for part in cut_shapes(width, heads_width, count)
    ]
    return call(
        functools.partial(
            heads_kernel, parts.where, len(parts.arrays), len(cuts), head_count
        ),
        cuts + [shape_of((rows, width), F32), shape_of((1, head_dim), F32)],
        [ANY_SPEC] * len(cuts) + [VMEM_SPEC] * 2,
        [place] + list(ins) + parts.arrays,
        [SMEM_SPEC] + [VMEM_SPEC] * 8 + [ANY_SPEC] * len(parts.arrays),
        [
            pltpu.VMEM((width, heads_width), BF16),
            pltpu.VMEM((2, width, heads_width), BF16),
            pltpu.VMEM((rows, heads_width), BF16),
            pltpu.SemaphoreType.DMA((slots(parts.where),)),
            pltpu.SemaphoreType.DMA((2, count)),
        ],
        flops=6 * rows * width * heads_width,
        moved=8 * width * heads_width,
    )


def finish_kernel(
    where,
    ref_count,
    out_count,
    narrow_rows,
    wide_rows,
    place_ref,
    near_ref,
    back_ref,
    far_ref,
    key_lin_ref,
    small_gains_ref,
    gains_ref,
    cos_ref,
    sin_ref,
    attn_in_ref,
    tokens_ref,
    d_middle_ref,
    d_in_ref,
    rows_ref,
    ffn_post_ref,
    query_gain_ref,
    *refs,
):
    parts, refs = refs[:ref_count], refs[ref_count:]
    grads, (input_grad_ref, first_w, whole, d_low, sems) = refs[:out_count], refs[out_count:]
    rows, width = tokens_ref.shape
    head_dim = key_lin_ref.shape[1]
    seq = place_ref[0]
    heads_width = (parts[0].shape[-1] - 2 * head_dim - LANES) // 2
    copies = start_placing(where, parts, first_w, sems, 0, seq, heads_width, 2 * head_dim)
    d_keys = near_ref[...] + back_ref[...].astype(F32) + far_ref[...].astype(F32)
    key_lin = key_lin_ref[...]
    scale = inverse_rms(key_lin)
    d_normed = rotate(d_keys[:, :head_dim], cos_ref[2 * rows :, :], -sin_ref[2 * rows :, :])
    back, key_gain = norm_back(key_lin * scale, scale, small_gains_ref[5:6, :], d_normed)
    d_low[:, :head_dim] = back.astype(BF16)
    d_low[:, head_dim:] = d_keys[:, head_dim:].astype(BF16)
    whole[:, : 2 * head_dim] = dot_tn(attn_in_ref[...], d_low[...]).astype(BF16)
    wait_all(copies)
    d_attn_in = d_in_ref[...] + dot_t(d_low[...], first_w[...])
    inputs = tokens_ref[...].astype(F32)
    scale = inverse_rms(inputs)
    back, grad_an = norm_back(inputs * scale, scale, gains_ref[0:1, :], d_attn_in)
    input_grad_ref[...] = d_middle_ref[...] + back
    row = iota((8, width), 0)
    gain_rows = rows_ref[...] + jnp.where(row == 0, grad_an, 0.0)
    gain_rows = gain_rows + jnp.where(row == 3, ffn_post_ref[...], 0.0)
    small_row = iota((8, head_dim), 0)
    small = jnp.where(small_row == 4, query_gain_ref[...], 0.0)
    small = small + jnp.where(small_row == 5, key_gain, 0.0)
    spread = spread_matrix(head_dim, width, narrow_rows, wide_rows)
    gain_rows = gain_rows + dot(small.astype(BF16), spread)
    pick = unit((8, LANES), iota((8, LANES), 0) == iota((8, LANES), 1))
    whole[:, 2 * head_dim :] = dot_tn(gain_rows.astype(BF16), pick).astype(BF16)
    wait_all(start_cutting(whole, grads, sems, slots(where), seq))


def finish(place, ins, parts, narrow_rows, wide_rows):
    tokens, key_lin = ins[9], ins[3]
    rows, width = tokens.shape
    head_dim = key_lin.shape[1]
    count = lax.axis_size("seq")
    pack = 2 * head_dim + LANES
    cuts = cut_shapes(width, pack, count)
    return call(
        functools.partial(
            finish_kernel, parts.where, len(parts.arrays), len(cuts), narrow_rows, wide_rows
        ),
        cuts + [shape_of((rows, width), F32)],
        [ANY_SPEC] * len(cuts) + [VMEM_SPEC],
        [place] + list(ins) + parts.arrays,
        [SMEM_SPEC] + [VMEM_SPEC] * len(ins) + [ANY_SPEC] * len(parts.arrays),
        [
            pltpu.VMEM((width, 2 * head_dim), BF16),
            pltpu.VMEM((width, pack), BF16),
            pltpu.VMEM((rows, 2 * head_dim), BF16),
            pltpu.SemaphoreType.DMA((slots(parts.where) + count,)),
        ],
        flops=8 * rows * width * head_dim,
        moved=4 * width * pack + 20 * rows * width,
    )


def layout(lengths, counts, first_slot, row_count):
    starts = jnp.cumsum(lengths) - lengths
    slot_index = first_slot + jnp.arange(row_count, dtype=jnp.int32)
    member = (slot_index[:, None] >= starts[None, :]).astype(jnp.int32)
    document = jnp.sum(member, axis=1) - 1
    onehot = (document[:, None] == jnp.arange(lengths.shape[0], dtype=jnp.int32)[None, :]).astype(
        jnp.int32
    )
    position = slot_index - jnp.sum(onehot * starts[None, :], axis=1)
    padded = jnp.sum(onehot * (lengths - counts)[None, :], axis=1)
    return (position, padded)


def on_device(
    tokens,
    cotangent,
    doc_lengths,
    true_counts,
    w_query,
    w_key,
    w_value,
    w_out,
    w_gate,
    w_up,
    w_down,
    attn_norm_gain,
    query_gain,
    key_gain,
    attn_post_gain,
    ffn_norm_gain,
    ffn_post_gain,
):
    row_count = tokens.shape[1]
    head_dim = w_key.shape[1]
    heads_width = w_query.shape[1]
    head_count = heads_width // head_dim
    seq_index, plane_index = lax.axis_index("seq"), lax.axis_index("fsdp")
    place = jnp.stack([seq_index, plane_index]).astype(jnp.int32)
    inputs, upstream = tokens[0], cotangent[0]
    wide_rows, narrow_rows = attn_norm_gain.shape[0], query_gain.shape[0]

    planes_count = lax.axis_size("fsdp")
    far_masks = [mask for mask in seq_masks() if mask > 2]

    def swap_far(parts):
        parts = dict(parts)
        for mask in far_masks:
            parts.update({rel ^ mask: swap(part, "seq", mask) for rel, part in parts.items()})
        return parts

    def swap_both(parts, rel):
        if rel not in far_masks:
            return swap(parts[rel], "seq", 2)
        split = (parts[rel].shape[-2] // 2 + 15) // 16 * 16
        top = swap(parts[rel][..., :split, :], "seq", 2)
        bottom = swap(parts[2][..., split:, :], "seq", rel)
        return jnp.concatenate([top, bottom], axis=-2)

    pack = pack_attn(
        w_query,
        w_key,
        w_value,
        w_out,
        [attn_norm_gain, attn_post_gain, ffn_norm_gain, ffn_post_gain],
        [query_gain, key_gain],
    )
    gate_up_own = jnp.stack([w_gate, w_up])
    pack, gate_up_own, inputs, w_down = sync((pack, gate_up_own, inputs, w_down))

    planes = [pack] + [shift(pack, "fsdp", steps) for steps in range(1, planes_count)]
    gate_up_far = swap_far({0: gate_up_own})
    gate_up_half = gate_up_far | {2: swap(gate_up_own, "seq", 2)}
    first_slot = seq_index * row_count
    position, padded = layout(
        doc_lengths[0], true_counts[0], first_slot - WINDOW, row_count + WINDOW
    )
    frequency = ROPE_BASE ** (-2.0 * jnp.arange(head_dim // 2, dtype=F32) / head_dim)
    angles = position.astype(F32)[:, None] * frequency
    cosine, sine = jnp.cos(angles), jnp.sin(angles)
    reach = jnp.clip(position[WINDOW:] - padded[WINDOW:], 0, WINDOW - 1)
    lowest = (WINDOW + jnp.arange(row_count, dtype=jnp.int32) - reach)[:, None]
    lowest = jnp.broadcast_to(lowest, (row_count, LANES))
    state = (planes, cosine, sine, lowest, inputs, w_down)
    planes, cosine, sine, lowest, inputs, w_down = sync(state)
    pack_rows, gate_up_half, inputs, w_down = sync(
        (place_planes(planes, place), gate_up_half, inputs, w_down)
    )

    rows_far = swap_far({0: pack_rows})
    rows_half = rows_far | {2: swap(pack_rows, "seq", 2)}
    behind = from_behind(inputs, 1)
    gate_up_rels, gate_up_core = core_stack(gate_up_half)
    state = (rows_half, behind, gate_up_half, gate_up_core, w_down)
    rows_half, behind, gate_up_half, gate_up_core, w_down = sync(state)
    rows_rest = {rel ^ 2: swap_both(rows_half, rel) for rel in rows_far if rel}
    half_rels, half_core = core_stack(rows_half)
    tokens3 = [inputs, behind, from_behind(behind, 1)]
    state = (rows_half, rows_rest, half_core, tokens3, gate_up_half, w_down)
    rows_half, rows_rest, half_core, tokens3, gate_up_half, w_down = sync(state)
    rest_rels, rest_core = core_stack(rows_rest)
    rest_core, gate_up_half, w_down = sync((rest_core, gate_up_half, w_down))
    cores = [(half_rels, half_core), (rest_rels, rest_core)]
    parts = all_parts(with_cores(plain(rows_half | rows_rest), cores))

    gate_rest = {rel ^ 2: swap(gate_up_half[rel][0], "seq", 2) for rel in gate_up_far if rel}
    up_rest = swap_far({2: gate_up_half[2][1]})
    up_rest = {rel: up_rest[rel] for rel in gate_rest}
    (
        attn_in,
        query_lin,
        key_lin,
        query,
        keys,
        probs,
        attended,
        gains,
        small_gains,
        attn_out,
        middle,
        ffn_in,
    ) = attend(
        place,
        tokens3,
        cosine,
        sine,
        lowest,
        parts,
        head_count,
        head_dim,
        narrow_rows,
        wide_rows,
    )
    ffn_in, gate_rest, up_rest, w_down = sync((ffn_in, gate_rest, up_rest, w_down))

    rest_rels, rest_core = core_stack(
        {rel: jnp.stack([gate_rest[rel], up_rest[rel]]) for rel in gate_rest}
    )
    down_far = swap_far({0: w_down})
    down_half = down_far | {2: swap(w_down, "seq", 2)}
    state = (shift(ffn_in, "fsdp", 1), rest_core, down_half)
    block, rest_core, down_half = sync(state)
    weights = []
    for index, rest in enumerate((gate_rest, up_rest)):
        entries = {rel: (part, (index,)) for rel, part in gate_up_half.items()} | plain(rest)
        for rels, stack in ((gate_up_rels, gate_up_core), (rest_rels, rest_core)):
            entries |= {rel ^ 1: (stack, (place_in, index)) for place_in, rel in enumerate(rels)}
        weights.append(all_parts(entries))
    blocks = [ffn_in, block]
    down_rest = {rel ^ 2: swap_both(down_half, rel) for rel in down_far if rel}
    half_rels, half_core = core_stack(down_half)
    act, gate_slope, up_slope = gate_up(place, blocks[1], weights)
    state = (shift(blocks[1], "fsdp", 1), act, down_rest, half_core)
    block, act, down_rest, half_core = sync(state)
    blocks.append(block)
    rest_rels, rest_core = core_stack(down_rest)
    act, rest_core = sync((act, rest_core))
    cores = [(half_rels, half_core), (rest_rels, rest_core)]
    weights.append(all_parts(with_cores(plain(down_half | down_rest), cores)))
    acts, slopes = {1: act}, {1: (gate_slope, up_slope)}
    partials = {1: sync(down(place, act, weights[2:]))}
    carried = None
    for step in range(2, planes_count + 1):
        state = {}
        if step < planes_count - 1:
            state["block"] = shift(blocks[step], "fsdp", 1)
        leaving = partials[step - 1]
        if carried is not None:
            leaving = add_rounded(leaving, carried)
        index = step % planes_count
        acts[index], gate_slope, up_slope, partials[index] = ffn(place, blocks[index], weights)
        slopes[index] = (gate_slope, up_slope)
        state["carried"] = shift(leaving, "fsdp", 1)
        state, partials = sync((state, partials))
        carried = state["carried"]
        if "block" in state:
            blocks.append(state["block"])
    output, d_ffn_low, grad_fp = turn([partials[0], carried], middle, upstream, gains)

    backs, partials, d_gates, d_ups = [sync(d_ffn_low)], {}, [], []
    carried, down_pair, down_sent = None, None, None
    all_acts = [acts[index] for index in range(planes_count)]
    for step in range(planes_count):
        state = {}
        if step < planes_count - 2:
            state["block"] = shift(backs[step], "fsdp", 1)
        if step == planes_count - 3:
            state["last"] = shift(backs[0], "fsdp", -1)
        if step >= 2:
            leaving = partials[step - 1]
            if carried is not None:
                leaving = add_rounded(leaving, carried)
            state["carried"] = shift(leaving, "fsdp", 1)
        if step == planes_count - 2:
            d_gate, d_up, partials[step], down_pair = ffn_back_and_grad(
                place, backs[step], slopes[step], weights, backs, all_acts
            )
        else:
            d_gate, d_up, partials[step] = ffn_back(place, backs[step], slopes[step], weights)
        if step == planes_count - 1:
            state["down"] = cores_send(down_pair)
        d_gates.append(d_gate)
        d_ups.append(d_up)
        state, partials, d_gates, d_ups, down_pair = sync(
            (state, partials, d_gates, d_ups, down_pair)
        )
        carried = state.get("carried", carried)
        backs += [state[name] for name in ("block", "last") if name in state]
        down_sent = state.get("down")
    carried = shift(add_rounded(partials[planes_count - 1], carried), "fsdp", 1)
    down_part = add_rounded(*down_sent)
    down_terms = [down_part[0]] + straight(down_part, 1, 2)
    gate_pair, up_pair = weight_grad(place, blocks, d_gates, d_ups)
    carried, gate_pair, up_pair, down_terms, down_part = sync(
        (carried, gate_pair, up_pair, down_terms, down_part)
    )

    gate_sent, up_sent = cores_send(gate_pair), cores_send(up_pair)
    down_terms += straight(down_part, *range(3, down_part.shape[0]))
    saved = (middle, upstream, attn_out, gains, query, keys, probs)
    d_middle, d_attn, d_rotated, far_halo, back_halo, near, gain_rows = attend_back(
        place, [partials[0], carried], saved, parts, head_count
    )
    state = (far_halo, back_halo, d_attn, d_rotated, gate_sent, up_sent)
    far_halo, back_halo, d_attn, d_rotated, gate_sent, up_sent = sync(state)
    halos = [from_behind(back_halo, -1), from_behind(far_halo, -2)]
    ins = [d_attn, attended, attn_in, d_rotated, query_lin, small_gains, cosine, sine]
    *head_grads, d_in, query_gain_grad = heads_back(place, ins, parts, head_count)
    gate_cut, up_cut = far_cut(add_rounded(*gate_sent)), across_cut(add_rounded(*up_sent))
    state = (halos, head_grads, gate_cut, up_cut, down_terms)
    halos, head_grads, gate_cut, up_cut, down_terms = sync(state)
    head_sent = cores_send(head_grads)
    gate_sides = (gate_cut[0], swap(gate_cut[1], "seq", far_masks[0]))
    up_sides = (up_cut[0], swap(up_cut[1], "seq", 2))
    ins = [
        near,
        *halos,
        key_lin,
        small_gains,
        gains,
        cosine,
        sine,
        attn_in,
        inputs,
        d_middle,
        d_in,
        gain_rows,
        grad_fp,
        query_gain_grad,
    ]
    *last_grads, input_grad = finish(place, ins, parts, narrow_rows, wide_rows)
    head_part = add_rounded(*head_sent)
    out_cut, query_cut = far_cut(head_part[0]), across_cut(head_part[1])
    last_grads, out_cut, query_cut = sync((last_grads, out_cut, query_cut))
    last_sent = cores_send(last_grads)
    out_sides = (out_cut[0], swap(out_cut[1], "seq", far_masks[0]))
    query_sides = (query_cut[0], swap(query_cut[1], "seq", 2))
    state = (last_sent, out_sides, query_sides, gate_sides, up_sides)
    last_sent, out_sides, query_sides, gate_sides, up_sides = sync(state)
    out_part = add_rounded(*out_sides)
    out_came = swap(out_part[1], "seq", 2)
    query_sides = far_step(add_rounded(*query_sides))
    last_part = add_rounded(*last_sent)
    last_terms = [last_part[0]] + straight(last_part, *range(1, last_part.shape[0]))
    gate_part, up_part = add_rounded(*gate_sides), add_rounded(*up_sides)
    state = (out_part, out_came, query_sides, last_terms, gate_part, up_part)
    out_part, out_came, query_sides, last_terms, gate_part, up_part = sync(state)
    reduced = jnp.concatenate(
        [
            add_rounded(out_part[0], out_came),
            add_rounded(*query_sides)[0],
            add_up(last_terms).astype(BF16),
        ],
        axis=1,
    )
    terms = planes_send(reduced)
    gate_came = swap(gate_part[1], "seq", 2)
    up_sides = far_step(up_part)
    grad_gate = add_up([gate_part[0], gate_came])
    grad_up = add_up(up_sides)[0]
    terms, grad_gate, grad_up = sync((terms, grad_gate, grad_up))
    rows = add_up(terms)
    last_start = 2 * heads_width
    gain_cols = rows[:, last_start + 2 * head_dim :]
    return (
        output[None],
        input_grad[None],
        rows[:, heads_width:last_start],
        rows[:, last_start : last_start + head_dim],
        rows[:, last_start + head_dim : last_start + 2 * head_dim],
        rows[:, :heads_width],
        grad_gate,
        grad_up,
        add_up(down_terms),
        gain_cols[:, 0],
        gain_cols[:narrow_rows, 4],
        gain_cols[:narrow_rows, 5],
        gain_cols[:, 1],
        gain_cols[:, 2],
        gain_cols[:, 3],
    )


def solution(mesh):
    rows = P("fsdp", "seq", None)
    shard, tile, vector = P(("seq", "fsdp"), None), P("seq", "fsdp"), P(("seq", "fsdp"))
    groups = P("fsdp", None)
    return jax.shard_map(
        on_device,
        mesh=mesh,
        in_specs=(rows, rows, groups, groups) + (shard,) * 4 + (tile,) * 3 + (vector,) * 6,
        out_specs=(rows, rows) + (shard,) * 4 + (tile,) * 3 + (vector,) * 6,
        check_vma=False,
    )
```
